32 devices in a mesh: gx: 4 (over y, x), gy: 4 (over z), dst: 2 (over core).
Axes of the slice: x: 2, y: 2, z: 4, core: 2. Of those that a mesh axis runs over, the one named last changes fastest.
Arguments:
- features: bfloat16 [32, 8, 16384], P(None, None, ('gx', 'gy')), may hold values from 0.09 to 3.1
- cost_weights: float32 [32], replicated, may hold values from 0.1 to 1
- successors: int32 [8, 16384], P(None, ('gx', 'gy')), may hold values from 0 to 1535, as said below
- turn_valid: int32 [8, 16384], P(None, ('gx', 'gy')), may hold values from 0 to 1, as said below
- border_lists: int32 [4, 2048], P(None, ('gx', 'gy')), may hold values from 0 to 1023, as said below
- destinations: int32 [32], P('dst'), may hold values from 0 to 16383
- anchors: float32 [32, 16384], P('dst', ('gx', 'gy')), may hold values from 0.25 to 4
- demo_counts: int32 [8, 16384], P(None, ('gx', 'gy')), may hold values from 0 to 3
Outputs:
- count_gap: float32 [8, 16384], P(None, ('gx', 'gy'))
- gradient: float32 [32], replicated
The draws below stay inside these ranges and needn't reach their ends.
Inputs may be any that keep to these rules, and one draw needn't show every extreme that they name: `successors`: values below 1024 are segments of the same block and turn 0 is always one of them; 1024 + k * 128 + j is entry j of the border list of the neighbour on side k (0: one gx position lower, 1: higher, 2: one gy position lower, 3: higher) that faces this block. `turn_valid`: turn 0 is always 1; a turn into a side where the grid has no neighbouring block is 0. `border_lists`: within one block and side the 128 entries are distinct local segment numbers.
All inputs are finite; a program needn't handle non-finite values.
Results may differ from the reference program's by a relative error of at most 0.0003.
Values sent between devices are 32-bit elements; how exact they have to be, the bound alone decides.
No kernel may reach another device: no remote copies, remote signals or barrier semaphores. Data moves between devices by JAX's collectives and lax.ppermute only.
A program may use at most 64 MiB of HBM per device.

```python
import math
import jax
import jax.numpy as jnp
from jax import lax

F = 32
K = 8
HORIZON = 8
S_DEV = 1024
BORDER = 128
NSEG = 16384
DEST = 32
N_GX = 4
N_GY = 4


def graph_turns(key):
    total_count = S_DEV * N_GX * N_GY
    kind_key, side_key, slot_key, local_key, keep_key = jax.random.split(key, 5)
    turn_shape = (K, total_count)
    crossing_draw = jax.random.randint(kind_key, turn_shape, 0, 4)
    side_draw = jax.random.randint(side_key, turn_shape, 0, 4)
    slot_draw = jax.random.randint(slot_key, turn_shape, 0, BORDER)
    local_draw = jax.random.randint(local_key, turn_shape, 0, S_DEV)
    keep_draw = jax.random.randint(keep_key, turn_shape, 0, 4)
    turn_number = jnp.arange(K, dtype=jnp.int32)[:, None]
    crossing = (crossing_draw < 3) & (turn_number > 0)
    successor = jnp.where(crossing, S_DEV + side_draw * BORDER + slot_draw, local_draw)
    block_index = jnp.arange(total_count, dtype=jnp.int32)[None, :] // S_DEV
    grid_row = block_index // N_GY
    grid_col = block_index % N_GY
    has_side = jnp.where(side_draw == 0, grid_row > 0, jnp.where(side_draw == 1, grid_row < N_GX - 1, jnp.where(side_draw == 2, grid_col > 0, grid_col < N_GY - 1)))
    usable = ((keep_draw > 0) | (turn_number == 0)) & (~crossing | has_side)
    return (successor.astype(jnp.int32), usable.astype(jnp.int32))


def draw_successors(key, part):
    return graph_turns(key)[0]


def draw_turn_valid(key, part):
    return graph_turns(key)[1]


def pick_rows(row_key):
    return jax.random.permutation(row_key, S_DEV)[:BORDER]


def draw_border_lists(key, part):
    key = jax.random.fold_in(key, 7)
    block_total = N_GX * N_GY
    row_keys = jax.random.split(key, block_total * 4)
    lists_drawn = jax.vmap(pick_rows)(row_keys)
    lists_drawn = lists_drawn.reshape(block_total, 4, BORDER).transpose(1, 0, 2)
    return lists_drawn.reshape(4, block_total * BORDER).astype(jnp.int32)


def draw_features(key, part):
    key = jax.random.fold_in(key, 11)
    total_count = S_DEV * N_GX * N_GY
    block_index = jnp.arange(total_count, dtype=jnp.int32) // S_DEV
    rising = 1.0 + 2.0 * block_index.astype(jnp.float32) / max(N_GX * N_GY - 1, 1)
    base_draw = jnp.exp(jax.random.uniform(key, (F, K, total_count), jnp.float32, math.log(0.1), 0.0))
    return (base_draw * rising[None, None, :]).astype(jnp.bfloat16)


def plant(values, own_key, low, top_value):
    place = [jax.random.randint(jax.random.fold_in(own_key, axis), (), 0, length) for axis, length in enumerate(values.shape)]
    widest = values.shape.index(max(values.shape))
    next_to = place[:widest] + [(place[widest] + 1) % values.shape[widest]] + place[widest + 1:]
    return values.at[tuple(place)].set(low).at[tuple(next_to)].set(top_value)


def shard_levels(key, extent, cuts, smallest, top_value):
    def one(axis_at, blocks):
        steps = jax.random.uniform(jax.random.fold_in(jax.random.fold_in(key, 6), axis_at), (blocks,), jnp.float32, smallest / len(cuts), top_value / len(cuts))
        return jnp.repeat(jnp.exp(steps), extent[axis_at] // blocks).reshape((-1,) + (1,) * (len(extent) - axis_at - 1))

    loudness = one(*cuts[0])
    for cut in cuts[1:]:
        loudness = loudness * one(*cut)
    return loudness


def setup_inputs(seed: int = 0) -> dict:
    streams_of = jax.random.split(jax.random.key(seed), 9)
    features = draw_features(jax.random.fold_in(streams_of[8], 71), 0)
    cost_weights = jnp.clip(jnp.exp(jax.random.uniform(streams_of[1], (F,), jnp.float32, math.log(0.1), math.log(1.0))), 0.1, 1.0)
    successors = draw_successors(jax.random.fold_in(streams_of[8], 71), 0)
    turn_valid = draw_turn_valid(jax.random.fold_in(streams_of[8], 71), 0)
    border_lists = draw_border_lists(jax.random.fold_in(streams_of[8], 71), 0)
    destinations = plant(jax.random.randint(streams_of[5], (DEST,), 0, NSEG), jax.random.fold_in(streams_of[5], 1), 0, NSEG - 1).astype(jnp.int32)
    anchors = jnp.clip(jnp.exp(math.log(4.0) - 2.7725887 * jax.random.uniform(streams_of[6], (DEST, NSEG), jnp.float32) ** shard_levels(streams_of[6], (DEST, NSEG), ((0, 2), (1, 16)), -0.2, 0.2)), 0.25, 4.0)
    demo_counts = plant(jax.random.randint(streams_of[7], (K, NSEG), 0, 4), jax.random.fold_in(streams_of[7], 1), 0, 3).astype(jnp.int32)
    return {"features": features, "cost_weights": cost_weights, "successors": successors, "turn_valid": turn_valid, "border_lists": border_lists, "destinations": destinations, "anchors": anchors, "demo_counts": demo_counts}


NEG = -1.0e30
START_COST = 100.0


def global_turns(successors, turn_valid, border_lists):
    segment = jnp.arange(NSEG, dtype=jnp.int32)
    block_index = segment // S_DEV
    grid_row = block_index // N_GY
    grid_col = block_index % N_GY
    is_local = successors < S_DEV
    halo_slot = jnp.clip(successors - S_DEV, 0, 4 * BORDER - 1)
    side_index = halo_slot // BORDER
    slot_place = halo_slot % BORDER
    step_row = jnp.where(side_index == 0, -1, jnp.where(side_index == 1, 1, 0))
    step_col = jnp.where(side_index == 2, -1, jnp.where(side_index == 3, 1, 0))
    next_row = grid_row[None, :] + step_row
    next_col = grid_col[None, :] + step_col
    inside = (next_row >= 0) & (next_row < N_GX) & (next_col >= 0) & (next_col < N_GY)
    neighbour = jnp.clip(next_row, 0, N_GX - 1) * N_GY + jnp.clip(next_col, 0, N_GY - 1)
    opposite = side_index + 1 - 2 * (side_index % 2)
    list_entry = border_lists[opposite, neighbour * BORDER + slot_place]
    far_index = neighbour * S_DEV + list_entry
    near_index = block_index[None, :] * S_DEV + successors
    target = jnp.where(is_local, near_index, far_index).astype(jnp.int32)
    usable = (turn_valid == 1) & (is_local | inside)
    return target, usable


def reference(features, cost_weights, successors, turn_valid, border_lists, destinations, anchors, demo_counts):
    target, usable = global_turns(successors, turn_valid, border_lists)
    feats = features.astype(jnp.float32)
    reward = -jnp.sum(feats * cost_weights[:, None, None], axis=0)
    segment = jnp.arange(NSEG, dtype=jnp.int32)
    group_rows = math.gcd(DEST, 8)
    group_count = DEST // group_rows

    def turn_scores(values):
        scores = reward[None] + values[:, target]
        return jnp.where(usable[None], scores, NEG)

    def one_group(group_pair):
        dest_rows, anchor_rows = group_pair
        is_target = segment[None, :] == dest_rows[:, None]
        values = jnp.where(is_target, 0.0, -START_COST).astype(jnp.float32)
        for round_index in range(HORIZON):
            scores = turn_scores(values)
            row_max = jnp.max(scores, axis=1)
            summed = jnp.sum(jnp.exp(scores - row_max[:, None]), axis=1)
            values = jnp.where(is_target, 0.0, row_max + jnp.log(summed))
        scores = turn_scores(values)
        row_max = jnp.max(scores, axis=1)
        raised = jnp.exp(scores - row_max[:, None])
        policy = raised / jnp.sum(raised, axis=1, keepdims=True)
        mass_now = jnp.where(is_target, 0.0, anchor_rows)
        counts = jnp.zeros((K, NSEG), jnp.float32)
        for round_index in range(HORIZON):
            turn_flow = mass_now[:, None, :] * policy
            counts = counts + jnp.sum(turn_flow, axis=0)
            if round_index + 1 < HORIZON:
                arrived = jnp.zeros_like(mass_now).at[:, target].add(turn_flow)
                mass_now = jnp.where(is_target, 0.0, arrived)
        return counts

    grouped = lax.map(one_group, (destinations.reshape(group_count, group_rows),
                                  anchors.reshape(group_count, group_rows, NSEG)))
    visits = jnp.sum(grouped, axis=0) / (DEST * HORIZON)
    demo_term = jnp.where(usable, demo_counts, 0).astype(jnp.float32) / 3.0
    count_gap = demo_term - visits
    gradient = jnp.sum(count_gap[None] * feats, axis=(1, 2)) / NSEG
    return count_gap, gradient
```

```python
import functools

import jax
import jax.numpy as jnp
from jax import lax
from jax.experimental import pallas as pl
from jax.experimental.pallas import tpu as pltpu
from jax.sharding import PartitionSpec as P

HORIZON = 8
NEG = -1e30
START_COST = 100.0
LANES = 128
ROWS = 60
RANKS = -(-ROWS // 16) * 16
STEP = 19
DEPTH = -(-ROWS // STEP) * STEP
BLOCK_AXES = ("gx", "gy")

LANE_PICK = lax.GatherDimensionNumbers(
    offset_dims=(),
    collapsed_slice_dims=(1,),
    start_index_map=(1,),
    operand_batching_dims=(0,),
    start_indices_batching_dims=(0,),
)


def lane_gather(table, index):
    return lax.gather(
        table,
        index[..., None],
        LANE_PICK,
        (1, 1),
        mode=lax.GatherScatterMode.PROMISE_IN_BOUNDS,
    )


def tree_select(picked, bits):
    level = list(picked)
    for bit in bits:
        if len(level) == 1:
            break
        nxt = []
        for n in range(0, len(level), 2):
            if n + 1 < len(level):
                nxt.append(jnp.where(bit, level[n + 1], level[n]))
            else:
                nxt.append(level[n])
        level = nxt
    return level[0]


def row_bits(index, count):
    return [(index & (LANES << i)) != 0 for i in range(count)]


def table_gather(table_rows, index):
    lane = index & (LANES - 1)
    bits = row_bits(index, max(len(table_rows) - 1, 1).bit_length())
    return tree_select([lane_gather(row, lane) for row in table_rows], bits)


def run_copies(copies):
    for copy in copies:
        copy.start()
    for copy in copies:
        copy.wait()


def of_blocks(ref, half, row, per_block):
    return ref[pl.ds(half * 8 * per_block + row, 8, stride=per_block), :]


def whole_copies(pairs, sem):
    return [pltpu.make_async_copy(src, dst, sem.at[n]) for n, (src, dst) in enumerate(pairs)]


def by_core(what, mine, other):
    first = lax.axis_index("dst") == 0
    pl.when(first)(lambda: what(mine, other))
    pl.when(jnp.logical_not(first))(lambda: what(other, mine))


def own_block(grid_y):
    return lax.axis_index("gx") * grid_y + lax.axis_index("gy")


def target_mask(dest, half, chunk, per_block):
    sub = lax.broadcasted_iota(jnp.int32, (8, LANES), 0)
    lane = lax.broadcasted_iota(jnp.int32, (8, LANES), 1)
    return (half * 8 + sub) * per_block + chunk * LANES + lane == dest


def arrange_kernel(
    succ_any, valid_any, border_any, reward_ref, out_any,
    succ_ref, valid_ref, border_ref, out_ref, count_ref, first_ref, order_ref, inverse_ref, placed_ref,
    pair_ref, lane_ref, code_ref, column_ref, acc_ref, sem
):
    run_copies(
        whole_copies([(succ_any, succ_ref), (valid_any, valid_ref), (border_any, border_ref)], sem)
    )
    turns, width = succ_ref.shape
    chunks = width // LANES
    slots = chunks + 4
    step = 2 * LANES
    tops = 16
    square = (LANES, LANES)
    down = lax.broadcasted_iota(jnp.int32, square, 0)
    along = lax.broadcasted_iota(jnp.int32, square, 1)
    down_f, along_f = down.astype(jnp.float32), along.astype(jnp.float32)
    before = down < along
    unit = jnp.where(down == along, 1.0, 0.0)
    lane_row = lax.broadcasted_iota(jnp.int32, (LANES, step), 0)
    top_row = lax.broadcasted_iota(jnp.int32, (tops, step), 0)
    rank_row = lax.broadcasted_iota(jnp.int32, (RANKS, step), 0).astype(jnp.float32)
    last_dims = (((1,), (1,)), ((), ()))

    def product(left, right):
        return lax.dot_general(left, right, last_dims, preferred_element_type=jnp.float32)

    def columns(rows):
        return lax.dot_general(
            unit, rows, last_dims, precision=lax.Precision.HIGHEST, preferred_element_type=jnp.float32
        )

    def summed_down(array):
        return jnp.sum(array, axis=0, keepdims=True)

    def place_of(row, col):
        return summed_down(jnp.where((col > row) | ((col == row) & before), 1.0, 0.0))

    def count(a, total):
        for c in range(width // step):
            cols = slice(c * step, (c + 1) * step)
            u = succ_ref[pl.ds(a, 1), cols]
            low = jnp.where(valid_ref[pl.ds(a, 1), cols] == 1, u & (LANES - 1), -1)
            hot_low = jnp.where(low == lane_row, 1.0, 0.0).astype(jnp.bfloat16)
            hot_top = jnp.where((u >> 7) == top_row, 1.0, 0.0).astype(jnp.bfloat16)
            total = total + product(hot_top, hot_low)
        return total

    counts = lax.fori_loop(0, turns, count, jnp.zeros((tops, LANES), jnp.float32), unroll=2)
    count_columns = columns(counts)
    out_ref[...] = jnp.zeros_like(out_ref)
    for ref in (count_ref, first_ref, order_ref, inverse_ref, placed_ref, pair_ref):
        ref[...] = jnp.zeros_like(ref)
    for n in range(slots):
        i = n if n < chunks else n - chunks
        place = place_of(counts[n : n + 1, :], count_columns[:, n : n + 1])
        place = place if i % 2 == 0 else (LANES - 1.0) - place
        if (i // 2) % 2:
            place = jnp.where(place >= LANES // 2, place - LANES // 2, place + LANES // 2)
        first_ref[n : n + 1, :] = place
    first_columns = columns(first_ref[...])
    for n in range(slots):
        hit = first_columns[:, n : n + 1] == along_f
        inverse_ref[n : n + 1, :] = summed_down(jnp.where(hit, down_f, 0.0))
        placed_ref[n : n + 1, :] = summed_down(jnp.where(hit, count_columns[:, n : n + 1], 0.0))
    local = summed_down(placed_ref[0:chunks, :])
    room = -summed_down(placed_ref[chunks:tops, :])
    pair_ref[0:1, :] = local
    pair_ref[1:2, :] = room
    pair = columns(pair_ref[...])
    local_place, room_place = place_of(local, pair[:, 0:1]), place_of(room, pair[:, 1:2])
    pair_ref[0:1, :] = local_place
    pair_ref[1:2, :] = room_place
    pair = columns(pair_ref[...])
    goes = summed_down(jnp.where(pair[:, 1:2] == local_place, down_f, 0.0))
    comes = summed_down(jnp.where(pair[:, 0:1] == room_place, down_f, 0.0))
    full = (chunks, LANES)
    comes = jnp.broadcast_to(comes, full).astype(jnp.int32)
    goes = jnp.broadcast_to(goes, full)
    order_ref[0:chunks, :] = lane_gather(goes, first_ref[0:chunks, :].astype(jnp.int32))
    order_ref[chunks:tops, :] = first_ref[chunks:tops, :]
    inverse_ref[0:chunks, :] = lane_gather(inverse_ref[0:chunks, :], comes)
    placed_ref[0:chunks, :] = lane_gather(placed_ref[0:chunks, :], comes)
    running = jnp.zeros((1, LANES), jnp.float32)
    for n in range(slots):
        count_ref[n : n + 1, :] = running
        running = running + placed_ref[n : n + 1, :]
        out_ref[ROWS + n : ROWS + n + 1, :] = running
        out_ref[ROWS + slots + n : ROWS + slots + n + 1, :] = order_ref[n : n + 1, :]
        out_ref[ROWS + 2 * slots + n : ROWS + 2 * slots + n + 1, :] = inverse_ref[n : n + 1, :]
    for k in range(chunks):
        cols = slice(k * LANES, (k + 1) * LANES)
        u = succ_ref[:, cols]
        rows = [jnp.broadcast_to(order_ref[n : n + 1, :], (turns, LANES)) for n in range(slots)]
        lane = jnp.where(valid_ref[:, cols] == 1, table_gather(rows, u), -1.0)
        code = jnp.where(lane >= 0.0, lane + ((u >> 7) * LANES).astype(jnp.float32), -1.0)
        lane_ref[:, cols] = lane
        code_ref[:, cols] = code
        column_ref[cols, :] = columns(code)
    acc_ref[...] = jnp.zeros_like(acc_ref)
    earlier = jnp.where(
        lax.broadcasted_iota(jnp.int32, (step, step), 0) < lax.broadcasted_iota(jnp.int32, (step, step), 1),
        1.0,
        0.0,
    )
    lane_row_f = lane_row.astype(jnp.float32)

    def one_chunk(c, base):
        start = pl.multiple_of(c * step, step)
        cols = pl.ds(start, step)
        s = start + lax.broadcasted_iota(jnp.int32, (1, step), 1)
        source = [
            (s & ~7).astype(jnp.float32).astype(jnp.bfloat16),
            (s & 7).astype(jnp.float32).astype(jnp.bfloat16),
        ]
        for a in range(turns):
            row = slice(a, a + 1)
            hot = jnp.where(lane_ref[row, cols] == lane_row_f, 1.0, 0.0).astype(jnp.bfloat16)
            hot_top = jnp.where((succ_ref[row, cols] >> 7) == top_row, 1.0, 0.0)
            same = column_ref[cols, row] == code_ref[row, cols]
            within = summed_down(jnp.where(same, earlier, 0.0))
            coarse = (base.astype(jnp.int32) & ~127).astype(jnp.float32)
            both = jnp.concatenate([coarse, base - coarse], axis=0).astype(jnp.bfloat16)
            starts = jnp.dot(both, hot, preferred_element_type=jnp.float32)
            begin = summed_down((starts[:tops] + starts[tops:]) * hot_top)
            base = base + product(hot_top.astype(jnp.bfloat16), hot)
            match = jnp.where(begin + within == rank_row, 1.0, 0.0).astype(jnp.bfloat16)
            r = reward_ref[row, cols]
            r1 = r.astype(jnp.bfloat16)
            rest = r - r1.astype(jnp.float32)
            r2 = rest.astype(jnp.bfloat16)
            r3 = (rest - r2.astype(jnp.float32)).astype(jnp.bfloat16)
            left = jnp.concatenate([match * piece for piece in (*source, r1, r2, r3)], axis=0)
            acc_ref[...] += product(left, hot)
        return base

    lax.fori_loop(0, width // step, one_chunk, count_ref[...])
    part = [acc_ref[i * RANKS : i * RANKS + ROWS, :] for i in range(5)]
    share = out_ref.shape[0] // 2
    out_ref[0:ROWS, :] = part[0] + part[1]
    out_ref[share : share + ROWS, :] = (part[2] + part[3]) + part[4]
    listed = columns(border_ref[...].astype(jnp.float32)).astype(jnp.int32)
    for side in range(4):
        for q in range(chunks):
            found = jnp.where(listed[:, side : side + 1] == along + q * LANES, down_f + 1.0, 0.0)
            row = share + ROWS + side * chunks + q
            out_ref[row : row + 1, :] = summed_down(found)
    half = out_ref.at[pl.ds(pl.multiple_of(lax.axis_index("dst") * share, 8), share)]
    blocks = out_any.shape[0] // share
    run_copies(whole_copies([(half, out_any.at[pl.ds(b * share, share)]) for b in range(blocks)], sem))


def graph_kernel(
    weight_ref, feature_any, succ_any, valid_any, border_any, anchor_any, out_ref, reward_ref,
    feature_ref, succ_ref, valid_ref, border_ref, anchor_ref, part_ref, split_ref, sem
):
    run_copies(
        whole_copies(
            [
                (feature_any, feature_ref),
                (succ_any, succ_ref),
                (valid_any, valid_ref),
                (border_any, border_ref),
                (anchor_any, anchor_ref),
            ],
            sem,
        )
    )
    turns, width = succ_ref.shape
    chunks = width // LANES
    edges = turns * chunks
    part_ref[edges : edges + 8, :] = jnp.zeros((8, LANES), jnp.float32)
    part_ref[edges : edges + 4, :] = border_ref[...].astype(jnp.float32)
    first_core = lax.axis_index("dst") == 0
    for q in range(chunks):
        cols = slice(q * LANES, (q + 1) * LANES)
        cost = weight_ref[0] * feature_ref[0, :, cols].astype(jnp.float32)
        for f in range(1, feature_ref.shape[0]):
            cost = cost + weight_ref[f] * feature_ref[f, :, cols].astype(jnp.float32)
        reward_ref[:, cols] = -cost
        masked = jnp.where(valid_ref[:, cols] == 1, -cost, NEG)
        turn_to = succ_ref[:, cols].astype(jnp.float32)
        part_ref[pl.ds(q, turns, chunks), :] = jnp.where(first_core, masked, turn_to)
        split_ref[pl.ds(q, anchor_ref.shape[0], chunks), :] = anchor_ref[:, cols]
    blocks = anchor_ref.shape[0]
    size, common = out_ref.shape[0] // blocks, part_ref.shape[0]
    for b in range(blocks):
        out_ref[b * size : b * size + common, :] = part_ref[...]
        out_ref[b * size + common : (b + 1) * size, :] = split_ref[b * chunks : (b + 1) * chunks, :]


def value_kernel(
    grid_y, dest_ref, mine_ref, other_ref, ext_ref, raised_ref, max_ref, inv_ref,
    reward, index, border, side_pad, spare_ref
):
    halves = ext_ref.shape[0]
    size = mine_ref.shape[0] // (8 * halves)
    chunks = ext_ref.shape[1] - 4
    turns = raised_ref.shape[1] // chunks
    edges = turns * chunks
    per_block = chunks * LANES
    dest = dest_ref[own_block(grid_y)]
    side_pad[...] = jnp.zeros_like(side_pad)
    sub = lax.broadcasted_iota(jnp.int32, (8, LANES), 0)
    lane = lax.broadcasted_iota(jnp.int32, (8, LANES), 1)
    dest_block, dest_place = lax.div(dest, per_block), lax.rem(dest, per_block)

    def unpack(first, second):
        for h in range(halves):

            def rows(i, carry, h=h):
                reward[h, i] = of_blocks(first, h, i, size)
                index[h, i] = of_blocks(second, h, i, size).astype(jnp.int32)
                return carry

            lax.fori_loop(0, edges, rows, 0, unroll=8)
            for side in range(4):
                border[h, side] = of_blocks(first, h, edges + side, size).astype(jnp.int32)

    by_core(unpack, mine_ref, other_ref)
    for h in range(halves):
        for side in range(4):
            found = (border[h, side] == dest_place) & (h * 8 + sub == dest_block)
            entry = jnp.max(jnp.where(found, lane + 1, 0).astype(jnp.float32), axis=1, keepdims=True)
            side_pad[side, 8 + 8 * h : 16 + 8 * h, :] = jnp.broadcast_to(entry, (8, LANES))
    shifts = ((1, -grid_y), (0, grid_y), (3, -1), (2, 1))

    def shown(h, side):
        facing, by = shifts[side]
        start = 8 + 8 * h + by
        return side_pad[facing, start : start + 8, :]

    def dest_index(h):
        where = jnp.where(h * 8 + sub == dest_block, dest_place, -1)
        for side in range(4):
            entry = shown(h, side).astype(jnp.int32)
            where = jnp.where(entry > 0, per_block + side * LANES + entry - 1, where)
        return where

    def bring_halo(values):
        for h in range(halves):
            table = [values[h, q] for q in range(chunks)]
            for side in range(4):
                side_pad[side, 8 + 8 * h : 16 + 8 * h, :] = table_gather(table, border[h, side])
        for h in range(halves):
            for side in range(4):
                values[h, chunks + side] = shown(h, side)

    def summed(out):
        top = functools.reduce(jnp.maximum, out)
        raised = [jnp.exp(score - top) for score in out]
        return top, raised, functools.reduce(jnp.add, raised)

    def scores_of(values, h, q):
        tables = [values[h, r] for r in range(chunks + 4)]
        out = []
        for a in range(turns):
            rows = tables if a else tables[:chunks]
            out.append(reward[h, a * chunks + q] + table_gather(rows, index[h, a * chunks + q]))
        return summed(out)

    def store_value(h, q, top, total, into):
        value = top + jnp.log(total)
        into[h, q] = jnp.where(target_mask(dest, h, q, per_block), 0.0, value)

    wanted = [dest_index(h) for h in range(halves)]

    def first_chunk(q, inner):
        for h in range(halves):
            out = []
            for a in range(turns):
                before = jnp.where(index[h, a * chunks + q] == wanted[h], 0.0, -START_COST)
                out.append(reward[h, a * chunks + q] + before)
            top, _, total = summed(out)
            store_value(h, q, top, total, spare_ref)
        return inner

    lax.fori_loop(0, chunks, first_chunk, 0, unroll=2)

    def backup(values, into):
        bring_halo(values)

        def one_chunk(q, inner):
            for h in range(halves):
                top, _, total = scores_of(values, h, q)
                store_value(h, q, top, total, into)
            return inner

        lax.fori_loop(0, chunks, one_chunk, 0, unroll=chunks)

    def two_backups(step, carry):
        backup(spare_ref, ext_ref)
        backup(ext_ref, spare_ref)
        return carry

    lax.fori_loop(0, (HORIZON - 2) // 2, two_backups, 0)
    backup(spare_ref, ext_ref)
    bring_halo(ext_ref)

    def last_chunk(q, inner):
        for h in range(halves):
            top, raised, total = scores_of(ext_ref, h, q)
            max_ref[h, q] = top
            inv_ref[h, q] = 1.0 / total
            for a in range(turns):
                raised_ref[h, a * chunks + q] = raised[a]
        return inner

    lax.fori_loop(0, chunks, last_chunk, 0, unroll=chunks)


def push_kernel(
    grid_y, scale, dest_ref, mine_ref, other_ref, graph_mine, graph_other, ext_ref, raised_ref, max_ref,
    inv_ref, keep_ref, send_ref, ends, order, values, source, slot, policy, back, scaled, total, arrived, side_pad, raw
):
    halves = ext_ref.shape[0]
    blocks = 8 * halves
    size, share = graph_mine.shape[0] // blocks, mine_ref.shape[0] // blocks
    chunks = max_ref.shape[1]
    edges = raised_ref.shape[1]
    turns = edges // chunks
    per_block = chunks * LANES
    slots = chunks + 4
    dest = dest_ref[own_block(grid_y)]
    core = lax.axis_index("dst")
    side_pad[...] = jnp.zeros_like(side_pad)

    def unpack(first, second):
        for h in range(halves):
            for n in range(slots):
                ends[h, n] = of_blocks(first, h, ROWS + n, share)
                order[h, n] = of_blocks(first, h, ROWS + slots + n, share).astype(jnp.int32)
                inverse = of_blocks(first, h, ROWS + 2 * slots + n, share).astype(jnp.int32)
                values[h, n] = lane_gather(ext_ref[h, n], inverse)

            def rows(r, carry, h=h):
                source[h, r] = of_blocks(first, h, r, share).astype(jnp.int32)
                policy[h, r] = of_blocks(second, h, r, share)
                return carry

            lax.fori_loop(0, ROWS, rows, 0, unroll=6)
            for r in range(ROWS, DEPTH):
                source[h, r] = jnp.zeros((8, LANES), jnp.int32)
                policy[h, r] = jnp.zeros((8, LANES), jnp.float32)
            for n in range(4 * chunks):
                back[h, n] = of_blocks(second, h, ROWS + n, share).astype(jnp.int32) - 1

    by_core(unpack, mine_ref, other_ref)
    deepest = jnp.max(functools.reduce(jnp.maximum, [ends[h, slots - 1] for h in range(halves)]))
    deepest = deepest.astype(jnp.int32)
    fits = deepest <= ROWS
    steps = lax.div(jnp.minimum(deepest, ROWS) + (STEP - 1), STEP)
    shifts = ((1, -grid_y), (0, grid_y), (3, -1), (2, 1))

    def shown(h, side):
        facing, by = shifts[side]
        start = 8 + 8 * h + by
        return side_pad[facing, start : start + 8, :]

    @pl.when(jnp.logical_not(fits))
    def _():
        for h in range(halves):
            for n in range(slots):
                order[h, n] = lax.broadcasted_iota(jnp.int32, (8, LANES), 1)

    for h in range(halves):
        for side in range(4):
            side_pad[side, 8 + 8 * h : 16 + 8 * h, :] = order[h, chunks + side].astype(jnp.float32)
    for h in range(halves):
        for side in range(4):
            lanes = shown(h, side).astype(jnp.int32)
            for q in range(chunks):
                entry = back[h, side * chunks + q]
                back[h, side * chunks + q] = jnp.where(
                    entry >= 0, lane_gather(lanes, jnp.maximum(entry, 0)), -1
                )

    def prepare(t, carry):
        for i in range(STEP):
            for h in range(halves):
                r = t * STEP + i
                src = source[h, r]
                place = r.astype(jnp.float32)
                row = functools.reduce(
                    jnp.add, [jnp.where(ends[h, n] <= place, 1, 0) for n in range(slots)]
                )
                slot[h, r] = row
                bits = [(row & (1 << n)) != 0 for n in range(4)]
                picked = tree_select([values[h, n] for n in range(slots)], bits)
                top = table_gather([max_ref[h, q] for q in range(chunks)], src)
                policy[h, r] = jnp.exp(policy[h, r] + picked - top)
        return carry

    lax.fori_loop(0, steps, prepare, 0)
    for h in range(halves):
        for q in range(chunks):
            own = of_blocks(graph_mine, h, size - chunks + q, size)
            first = jnp.where(target_mask(dest, h, q, per_block), 0.0, own)
            total[h, q] = first
            scaled[h, q] = first * inv_ref[h, q]

    @pl.when(jnp.logical_not(fits))
    def _():
        def keep_turns(first, second):
            for h in range(halves):

                def rows(e, carry, h=h):
                    raw[h, e] = of_blocks(second, h, e, size).astype(jnp.int32)
                    return carry

                lax.fori_loop(0, edges, rows, 0)

        by_core(keep_turns, graph_mine, graph_other)

    zero = jnp.zeros((8, LANES), jnp.float32)

    def keep(h):
        for side in range(4):
            side_pad[side, 8 + 8 * h : 16 + 8 * h, :] = arrived[h, chunks + side]

    def add_flow(acc, row, flow):
        return [acc[n] + jnp.where(row == n, flow, 0.0) for n in range(slots)]

    def sum_arranged():
        for h in range(halves):
            for n in range(slots):
                arrived[h, n] = zero

        def one_step(t, carry):
            for h in range(halves):
                table = [scaled[h, q] for q in range(chunks)]
                acc = [arrived[h, n] for n in range(slots)]
                for i in range(STEP):
                    r = t * STEP + i
                    flow = table_gather(table, source[h, r]) * policy[h, r]
                    acc = add_flow(acc, slot[h, r], flow)
                for n in range(slots):
                    arrived[h, n] = acc[n]
            return carry

        lax.fori_loop(0, steps, one_step, 0)
        for h in range(halves):
            keep(h)

    def sum_turned():
        lane = lax.broadcasted_iota(jnp.int32, (8, LANES), 1)
        for h in range(halves):

            def one_edge_row(e, acc, h=h):
                flow = scaled[h, lax.rem(e, chunks)] * raised_ref[h, e]
                where = raw[h, e]

                def one_turn(k, state):
                    flow, where, acc = state[0], state[1], list(state[2:])
                    here = jnp.where((where & (LANES - 1)) == lane, where >> 7, -1)
                    acc = add_flow(acc, here, flow)
                    return (pltpu.roll(flow, 1, 1), pltpu.roll(where, 1, 1), *acc)

                return tuple(lax.fori_loop(0, LANES, one_turn, (flow, where, *acc))[2:])

            for n, value in enumerate(lax.fori_loop(0, edges, one_edge_row, (zero,) * slots)):
                arrived[h, n] = value
            keep(h)

    def push(round_index, carry):
        pl.when(fits)(sum_arranged)
        pl.when(jnp.logical_not(fits))(sum_turned)
        for h in range(halves):
            landed = [shown(h, side) for side in range(4)]
            for q in range(chunks):
                value = lane_gather(arrived[h, q], order[h, q])
                for side in range(4):
                    entry = back[h, side * chunks + q]
                    got = lane_gather(landed[side], jnp.maximum(entry, 0))
                    value = value + jnp.where(entry >= 0, got, 0.0)
                value = jnp.where(target_mask(dest, h, q, per_block), 0.0, value)
                total[h, q] = total[h, q] + value
                scaled[h, q] = value * inv_ref[h, q]
        return carry

    lax.fori_loop(0, HORIZON - 1, push, 0)
    for h in range(halves):
        for q in range(chunks):
            weight = total[h, q] * inv_ref[h, q] * scale
            for part, out_ref in ((core, keep_ref), (1 - core, send_ref)):
                for a in range(turns // 2):
                    value = weight * raised_ref[h, (part * (turns // 2) + a) * chunks + q]
                    start = h * 4 * edges + a * chunks + q
                    out_ref[pl.ds(start, 8, stride=edges // 2), :] = value


VMEM_SPEC = pl.BlockSpec(memory_space=pltpu.VMEM)
SMEM_SPEC = pl.BlockSpec(memory_space=pltpu.SMEM)
HBM_SPEC = pl.BlockSpec(memory_space=pltpu.HBM)
PARAMS = pltpu.CompilerParams(vmem_limit_bytes=48 * 1024 * 1024)


def f32(*shape):
    return jax.ShapeDtypeStruct(shape, jnp.float32)


def call_graph(cost_weights, features, successors, turn_valid, border_lists, anchors):
    turns, width = successors.shape
    blocks = anchors.shape[0]
    chunks = width // LANES
    rows = turns * chunks + 8
    return pl.pallas_call(
        graph_kernel,
        out_shape=(f32(blocks * (rows + chunks), LANES), f32(turns, width)),
        in_specs=[SMEM_SPEC] + [HBM_SPEC] * 5,
        out_specs=(VMEM_SPEC, VMEM_SPEC),
        scratch_shapes=[
            pltpu.VMEM(features.shape, features.dtype),
            pltpu.VMEM(successors.shape, jnp.int32),
            pltpu.VMEM(turn_valid.shape, jnp.int32),
            pltpu.VMEM(border_lists.shape, jnp.int32),
            pltpu.VMEM(anchors.shape, jnp.float32),
            pltpu.VMEM((rows, LANES), jnp.float32),
            pltpu.VMEM((blocks * chunks, LANES), jnp.float32),
            pltpu.SemaphoreType.DMA((5,)),
        ],
        compiler_params=pltpu.CompilerParams(vmem_limit_bytes=63 * 1024 * 1024),
        name="own_graph",
    )(cost_weights, features, successors, turn_valid, border_lists, anchors)


def arranged_rows(chunks):
    most = ROWS + max(3 * (chunks + 4), 4 * chunks)
    return -(-most // 8) * 8


def call_arrange(successors, turn_valid, border_lists, reward, blocks):
    chunks = successors.shape[1] // LANES
    share = arranged_rows(chunks)
    return pl.pallas_call(
        arrange_kernel,
        out_shape=f32(blocks * share, LANES),
        in_specs=[HBM_SPEC] * 3 + [VMEM_SPEC],
        out_specs=HBM_SPEC,
        scratch_shapes=[
            pltpu.VMEM(successors.shape, jnp.int32),
            pltpu.VMEM(turn_valid.shape, jnp.int32),
            pltpu.VMEM(border_lists.shape, jnp.int32),
            pltpu.VMEM((2 * share, LANES), jnp.float32),
            *[pltpu.VMEM((16, LANES), jnp.float32)] * 5,
            pltpu.VMEM((8, LANES), jnp.float32),
            pltpu.VMEM(successors.shape, jnp.float32),
            pltpu.VMEM(successors.shape, jnp.float32),
            pltpu.VMEM(successors.shape[::-1], jnp.float32),
            pltpu.VMEM((5 * RANKS, LANES), jnp.float32),
            pltpu.SemaphoreType.DMA((blocks,)),
        ],
        compiler_params=PARAMS,
        cost_estimate=pl.CostEstimate(flops=4_000_000_000, bytes_accessed=400_000, transcendentals=0),
        name="arrange_turns",
    )(successors, turn_valid, border_lists, reward)


def call_values(destinations, mine, other, blocks, grid_y, turns, chunks):
    halves = blocks // 8
    edges = turns * chunks
    return pl.pallas_call(
        functools.partial(value_kernel, grid_y),
        out_shape=(
            f32(halves, chunks + 4, 8, LANES),
            f32(halves, edges, 8, LANES),
            f32(halves, chunks, 8, LANES),
            f32(halves, chunks, 8, LANES),
        ),
        in_specs=[SMEM_SPEC, VMEM_SPEC, VMEM_SPEC],
        out_specs=(VMEM_SPEC,) * 4,
        scratch_shapes=[
            pltpu.VMEM((halves, edges, 8, LANES), jnp.float32),
            pltpu.VMEM((halves, edges, 8, LANES), jnp.int32),
            pltpu.VMEM((halves, 4, 8, LANES), jnp.int32),
            pltpu.VMEM((4, blocks + 16, LANES), jnp.float32),
            pltpu.VMEM((halves, chunks + 4, 8, LANES), jnp.float32),
        ],
        compiler_params=PARAMS,
        cost_estimate=pl.CostEstimate(flops=40_000_000, bytes_accessed=40_000_000, transcendentals=2_000_000),
        name="soft_values",
    )(destinations, mine, other)


def call_push(destinations, mine, other, graph_mine, graph_other, ext, raised, top, inv, grid_y, scale):
    halves, edges = raised.shape[:2]
    blocks = 8 * halves
    chunks = top.shape[1]

    def vmem(rows, dtype=jnp.float32):
        return pltpu.VMEM((halves, rows, 8, LANES), dtype)

    return pl.pallas_call(
        functools.partial(push_kernel, grid_y, scale),
        out_shape=(f32(blocks * edges // 2, LANES),) * 2,
        in_specs=[SMEM_SPEC] + [VMEM_SPEC] * 8,
        out_specs=(VMEM_SPEC,) * 2,
        scratch_shapes=[
            vmem(chunks + 4),
            vmem(chunks + 4, jnp.int32),
            vmem(chunks + 4),
            vmem(DEPTH, jnp.int32),
            vmem(DEPTH, jnp.int32),
            vmem(DEPTH),
            vmem(4 * chunks, jnp.int32),
            vmem(chunks),
            vmem(chunks),
            vmem(chunks + 4),
            pltpu.VMEM((4, blocks + 16, LANES), jnp.float32),
            vmem(edges, jnp.int32),
        ],
        compiler_params=PARAMS,
        name="push_mass",
    )(destinations, mine, other, graph_mine, graph_other, ext, raised, top, inv)


def to_blocks(array):
    return lax.all_to_all(array, BLOCK_AXES, 0, 0, tiled=True)


def other_core(array):
    return lax.ppermute(array, "dst", [(0, 1), (1, 0)])


def per_destination(
    features, cost_weights, successors, turn_valid, border_lists, destinations, anchors, demo_counts
):
    turns, own_count = successors.shape
    chunks = own_count // LANES
    edges = turns * chunks
    grid_y = lax.axis_size("gy")
    blocks = lax.axis_size("gx") * grid_y
    groups = lax.axis_size("dst")
    pieces, reward = call_graph(cost_weights, features, successors, turn_valid, border_lists, anchors)
    graph = to_blocks(pieces)
    arranged = call_arrange(successors, turn_valid, border_lists, reward, blocks)
    core = lax.axis_index("dst")
    demo_term = jnp.where(turn_valid == 1, demo_counts, 0).astype(jnp.float32) / 3.0
    own_feats = lax.dynamic_slice_in_dim(features, core * (turns // 2), turns // 2, axis=1)
    graph = lax.optimization_barrier((graph, arranged))[0]
    arranged = to_blocks(arranged)
    graph = (graph, other_core(graph))
    values = call_values(destinations, *graph, blocks, grid_y, turns, chunks)
    arranged, own_feats, demo_term, *values = lax.optimization_barrier(
        (arranged, own_feats, demo_term, *values)
    )
    arranged = (arranged, other_core(arranged))
    scale = 1.0 / (anchors.shape[0] * groups * HORIZON)
    kept, sent = call_push(destinations, *arranged, *graph, *values, grid_y, scale)
    halved = (kept + other_core(sent)).reshape(blocks, edges // 2, LANES)
    half = jnp.sum(to_blocks(halved), axis=0)
    other = other_core(half)
    part = (turns // 2, own_count)
    own_gap = lax.dynamic_slice_in_dim(demo_term, core * part[0], part[0]) - half.reshape(part)
    own_feats = own_feats.astype(jnp.float32)
    block_term = jnp.sum(own_gap[None] * own_feats, axis=(1, 2)) / (own_count * blocks)
    terms = jnp.broadcast_to(block_term, (groups * blocks, 1, block_term.shape[0]))
    terms = lax.all_to_all(terms, (*BLOCK_AXES, "dst"), 0, 0, tiled=True)
    visits = jnp.concatenate([jnp.where(core == 0, half, other), jnp.where(core == 0, other, half)])
    return demo_term - visits.reshape(turns, own_count), jnp.sum(terms, axis=(0, 1))


def passed_along(array, axis, by):
    length = lax.axis_size(axis)
    pairs = [(i, i + by) for i in range(length) if 0 <= i + by < length]
    return lax.ppermute(array, axis, pairs)


def bring_values(values, border_lists):
    outgoing = values[:, border_lists]
    north_part = passed_along(outgoing[:, 1], "gx", 1)
    south_part = passed_along(outgoing[:, 0], "gx", -1)
    west_part = passed_along(outgoing[:, 3], "gy", 1)
    east_part = passed_along(outgoing[:, 2], "gy", -1)
    return jnp.concatenate([north_part, south_part, west_part, east_part], axis=1)


def return_flow(arrived, border_lists, own_count, border_width):
    local_part = arrived[:, :own_count]
    halo_part = arrived[:, own_count:].reshape(arrived.shape[0], 4, border_width)
    from_south = passed_along(halo_part[:, 0], "gx", -1)
    from_north = passed_along(halo_part[:, 1], "gx", 1)
    from_east = passed_along(halo_part[:, 2], "gy", -1)
    from_west = passed_along(halo_part[:, 3], "gy", 1)
    returned = jnp.stack([from_north, from_south, from_west, from_east], axis=1)
    return local_part.at[:, border_lists].add(returned)


def select_cells(cells, flat_index, turn_shape):
    picked = jnp.take(cells, flat_index, axis=1)
    return picked.reshape(cells.shape[0], turn_shape[0], turn_shape[1])


def turn_scores(values, halo_cells, reward, flat_turns, usable):
    extended = jnp.concatenate([values, halo_cells], axis=1)
    scores = reward[None] + select_cells(extended, flat_turns, usable.shape)
    return jnp.where(usable[None], scores, NEG)


def per_block(
    features, cost_weights, successors, turn_valid, border_lists, destinations, anchors, demo_counts
):
    own_count = successors.shape[1]
    border_width = border_lists.shape[1]
    dest_count = anchors.shape[0]
    slot_total = own_count + 4 * border_width
    block_index = lax.axis_index("gx") * lax.axis_size("gy") + lax.axis_index("gy")
    positions = jnp.arange(own_count, dtype=jnp.int32)
    is_target = positions[None, :] == (destinations - block_index * own_count)[:, None]
    usable = turn_valid == 1
    feats = features.astype(jnp.float32)
    reward = -jnp.sum(feats * cost_weights[:, None, None], axis=0)
    flat_turns = successors.reshape(-1)
    values = jnp.where(is_target, 0.0, -START_COST).astype(jnp.float32)
    for round_index in range(HORIZON):
        halo_cells = bring_values(values, border_lists)
        scores = turn_scores(values, halo_cells, reward, flat_turns, usable)
        row_max = jnp.max(scores, axis=1)
        new_values = row_max + jnp.log(jnp.sum(jnp.exp(scores - row_max[:, None]), axis=1))
        values = jnp.where(is_target, 0.0, new_values)
    halo_cells = bring_values(values, border_lists)
    scores = turn_scores(values, halo_cells, reward, flat_turns, usable)
    row_max = jnp.max(scores, axis=1)
    raised = jnp.exp(scores - row_max[:, None])
    policy = raised / jnp.sum(raised, axis=1, keepdims=True)
    mass_now = jnp.where(is_target, 0.0, anchors)
    turn_counts = jnp.zeros(successors.shape, jnp.float32)
    for round_index in range(HORIZON):
        turn_flow = mass_now[:, None, :] * policy
        turn_counts = turn_counts + jnp.sum(turn_flow, axis=0)
        if round_index + 1 < HORIZON:
            arrived = (
                jnp.zeros((dest_count, slot_total), jnp.float32)
                .at[:, flat_turns]
                .add(turn_flow.reshape(dest_count, -1))
            )
            landed = return_flow(arrived, border_lists, own_count, border_width)
            mass_now = jnp.where(is_target, 0.0, landed)
    local_visits = turn_counts / (dest_count * lax.axis_size("dst") * HORIZON)
    visits = lax.psum(local_visits, "dst")
    demo_term = jnp.where(usable, demo_counts, 0).astype(jnp.float32) / 3.0
    count_gap = demo_term - visits
    total_segments = own_count * lax.axis_size("gx") * lax.axis_size("gy")
    own_gap = demo_term / lax.axis_size("dst") - local_visits
    block_term = jnp.sum(own_gap[None] * feats, axis=(1, 2)) / total_segments
    gradient = lax.psum(block_term, ("gx", "gy", "dst"))
    return (count_gap, gradient)


def local(features, cost_weights, successors, turn_valid, border_lists, destinations, anchors, demo_counts):
    args = (
        features, cost_weights, successors, turn_valid, border_lists, destinations, anchors, demo_counts
    )
    blocks = lax.axis_size("gx") * lax.axis_size("gy")
    fits = (
        anchors.shape[0] == blocks
        and blocks % 8 == 0
        and lax.axis_size("dst") == 2
        and lax.axis_size("gx") in (2, 4, 8)
        and lax.axis_size("gy") in (2, 4, 8)
        and successors.shape[1] == 8 * LANES
        and border_lists.shape[1] == LANES
    )
    return per_destination(*args) if fits else per_block(*args)


def solution(mesh):
    in_specs = (
        P(None, None, ("gx", "gy")),
        P(),
        P(None, ("gx", "gy")),
        P(None, ("gx", "gy")),
        P(None, ("gx", "gy")),
        P("dst"),
        P("dst", ("gx", "gy")),
        P(None, ("gx", "gy")),
    )
    out_specs = (P(None, ("gx", "gy")), P())
    return jax.shard_map(local, mesh=mesh, in_specs=in_specs, out_specs=out_specs, check_vma=False)
```

```python
import functools

import jax
import jax.numpy as jnp
from jax import lax
from jax.experimental import pallas as pl
from jax.experimental.pallas import tpu as pltpu
from jax.sharding import PartitionSpec as P

HORIZON = 8
NEG = -1e30
START_COST = 100.0
LANES = 128
ROWS = 60
RANKS = -(-ROWS // 16) * 16
STEP = 14
DEPTH = -(-ROWS // STEP) * STEP
BLOCK_AXES = ("gy", "gx")

LANE_PICK = lax.GatherDimensionNumbers(
    offset_dims=(),
    collapsed_slice_dims=(1,),
    start_index_map=(1,),
    operand_batching_dims=(0,),
    start_indices_batching_dims=(0,),
)


def lane_gather(table, index):
    return lax.gather(
        table,
        index[..., None],
        LANE_PICK,
        (1, 1),
        mode=lax.GatherScatterMode.PROMISE_IN_BOUNDS,
    )


def tree_select(picked, bits):
    level = list(picked)
    for bit in bits:
        if len(level) == 1:
            break
        nxt = []
        for n in range(0, len(level), 2):
            if n + 1 < len(level):
                nxt.append(jnp.where(bit, level[n + 1], level[n]))
            else:
                nxt.append(level[n])
        level = nxt
    return level[0]


def row_bits(index, count):
    return [(index & (LANES << i)) != 0 for i in range(count)]


def table_gather(table_rows, index):
    lane = index & (LANES - 1)
    bits = row_bits(index, max(len(table_rows) - 1, 1).bit_length())
    return tree_select([lane_gather(row, lane) for row in table_rows], bits)


def run_copies(copies):
    for copy in copies:
        copy.start()
    for copy in copies:
        copy.wait()


def of_blocks(ref, half, row, per_block):
    return ref[pl.ds(half * 8 * per_block + row, 8, stride=per_block), :]


def whole_copies(pairs, sem):
    return [pltpu.make_async_copy(src, dst, sem.at[n]) for n, (src, dst) in enumerate(pairs)]


def by_core(what, mine, other):
    first = lax.axis_index("dst") == 0
    pl.when(first)(lambda: what(mine, other))
    pl.when(jnp.logical_not(first))(lambda: what(other, mine))


def own_block(grid_x):
    return lax.axis_index("gy") * grid_x + lax.axis_index("gx")


def renumbered(segment, per_block, blocks, grid_x):
    grid_y = blocks // grid_x
    block, place = lax.div(segment, per_block), lax.rem(segment, per_block)
    return (lax.rem(block, grid_y) * grid_x + lax.div(block, grid_y)) * per_block + place


def padded_rows(rows):
    tiles = -(-rows // 8)
    return (tiles + 1 - tiles % 2) * 8


def target_mask(dest, half, chunk, per_block):
    sub = lax.broadcasted_iota(jnp.int32, (8, LANES), 0)
    lane = lax.broadcasted_iota(jnp.int32, (8, LANES), 1)
    return (half * 8 + sub) * per_block + chunk * LANES + lane == dest


def arrange_kernel(
    succ_any, valid_any, border_any, anchor_any, reward_ref, out_any,
    succ_ref, valid_ref, border_ref, anchor_ref, split_ref, out_ref, count_ref, first_ref, order_ref, inverse_ref, placed_ref,
    pair_ref, lane_ref, code_ref, column_ref, acc_ref, sem
):
    run_copies(
        whole_copies(
            [
                (succ_any, succ_ref),
                (valid_any, valid_ref),
                (border_any, border_ref),
                (anchor_any, anchor_ref),
            ],
            sem,
        )
    )
    turns, width = succ_ref.shape
    chunks = width // LANES
    slots = chunks + 4
    step = 2 * LANES
    tops = 16
    square = (LANES, LANES)
    down = lax.broadcasted_iota(jnp.int32, square, 0)
    along = lax.broadcasted_iota(jnp.int32, square, 1)
    down_f, along_f = down.astype(jnp.float32), along.astype(jnp.float32)
    before = down < along
    unit = jnp.where(down == along, 1.0, 0.0)
    lane_row = lax.broadcasted_iota(jnp.int32, (LANES, step), 0)
    top_row = lax.broadcasted_iota(jnp.int32, (tops, step), 0)
    rank_row = lax.broadcasted_iota(jnp.int32, (RANKS, step), 0).astype(jnp.float32)
    last_dims = (((1,), (1,)), ((), ()))

    def product(left, right):
        return lax.dot_general(left, right, last_dims, preferred_element_type=jnp.float32)

    def columns(rows):
        return lax.dot_general(
            unit, rows, last_dims, precision=lax.Precision.HIGHEST, preferred_element_type=jnp.float32
        )

    def summed_down(array):
        return jnp.sum(array, axis=0, keepdims=True)

    def place_of(row, col):
        return summed_down(jnp.where((col > row) | ((col == row) & before), 1.0, 0.0))

    def count(a, total):
        for c in range(width // step):
            cols = slice(c * step, (c + 1) * step)
            u = succ_ref[pl.ds(a, 1), cols]
            low = jnp.where(valid_ref[pl.ds(a, 1), cols] == 1, u & (LANES - 1), -1)
            hot_low = jnp.where(low == lane_row, 1.0, 0.0).astype(jnp.bfloat16)
            hot_top = jnp.where((u >> 7) == top_row, 1.0, 0.0).astype(jnp.bfloat16)
            total = total + product(hot_top, hot_low)
        return total

    counts = lax.fori_loop(0, turns, count, jnp.zeros((tops, LANES), jnp.float32), unroll=2)
    count_columns = columns(counts)
    out_ref[...] = jnp.zeros_like(out_ref)
    for ref in (count_ref, first_ref, order_ref, inverse_ref, placed_ref, pair_ref):
        ref[...] = jnp.zeros_like(ref)
    for n in range(slots):
        i = n if n < chunks else n - chunks
        place = place_of(counts[n : n + 1, :], count_columns[:, n : n + 1])
        place = place if i % 2 == 0 else (LANES - 1.0) - place
        if (i // 2) % 2:
            place = jnp.where(place >= LANES // 2, place - LANES // 2, place + LANES // 2)
        first_ref[n : n + 1, :] = place
    first_columns = columns(first_ref[...])
    for n in range(slots):
        hit = first_columns[:, n : n + 1] == along_f
        inverse_ref[n : n + 1, :] = summed_down(jnp.where(hit, down_f, 0.0))
        placed_ref[n : n + 1, :] = summed_down(jnp.where(hit, count_columns[:, n : n + 1], 0.0))
    local = summed_down(placed_ref[0:chunks, :])
    room = -summed_down(placed_ref[chunks:tops, :])
    pair_ref[0:1, :] = local
    pair_ref[1:2, :] = room
    pair = columns(pair_ref[...])
    local_place, room_place = place_of(local, pair[:, 0:1]), place_of(room, pair[:, 1:2])
    pair_ref[0:1, :] = local_place
    pair_ref[1:2, :] = room_place
    pair = columns(pair_ref[...])
    goes = summed_down(jnp.where(pair[:, 1:2] == local_place, down_f, 0.0))
    comes = summed_down(jnp.where(pair[:, 0:1] == room_place, down_f, 0.0))
    full = (chunks, LANES)
    comes = jnp.broadcast_to(comes, full).astype(jnp.int32)
    goes = jnp.broadcast_to(goes, full)
    order_ref[0:chunks, :] = lane_gather(goes, first_ref[0:chunks, :].astype(jnp.int32))
    order_ref[chunks:tops, :] = first_ref[chunks:tops, :]
    inverse_ref[0:chunks, :] = lane_gather(inverse_ref[0:chunks, :], comes)
    placed_ref[0:chunks, :] = lane_gather(placed_ref[0:chunks, :], comes)
    running = jnp.zeros((1, LANES), jnp.float32)
    for n in range(slots):
        count_ref[n : n + 1, :] = running
        running = running + placed_ref[n : n + 1, :]
        out_ref[ROWS + n : ROWS + n + 1, :] = running
        out_ref[ROWS + slots + n : ROWS + slots + n + 1, :] = order_ref[n : n + 1, :]
        out_ref[ROWS + 2 * slots + n : ROWS + 2 * slots + n + 1, :] = inverse_ref[n : n + 1, :]
    for k in range(chunks):
        cols = slice(k * LANES, (k + 1) * LANES)
        u = succ_ref[:, cols]
        rows = [jnp.broadcast_to(order_ref[n : n + 1, :], (turns, LANES)) for n in range(slots)]
        lane = jnp.where(valid_ref[:, cols] == 1, table_gather(rows, u), -1.0)
        code = jnp.where(lane >= 0.0, lane + ((u >> 7) * LANES).astype(jnp.float32), -1.0)
        lane_ref[:, cols] = lane
        code_ref[:, cols] = code
        column_ref[cols, :] = columns(code)
    acc_ref[...] = jnp.zeros_like(acc_ref)
    earlier = jnp.where(
        lax.broadcasted_iota(jnp.int32, (step, step), 0) < lax.broadcasted_iota(jnp.int32, (step, step), 1),
        1.0,
        0.0,
    )
    lane_row_f = lane_row.astype(jnp.float32)

    def one_chunk(c, base):
        start = pl.multiple_of(c * step, step)
        cols = pl.ds(start, step)
        s = start + lax.broadcasted_iota(jnp.int32, (1, step), 1)
        source = [
            (s & ~7).astype(jnp.float32).astype(jnp.bfloat16),
            (s & 7).astype(jnp.float32).astype(jnp.bfloat16),
        ]
        for a in range(turns):
            row = slice(a, a + 1)
            hot = jnp.where(lane_ref[row, cols] == lane_row_f, 1.0, 0.0).astype(jnp.bfloat16)
            hot_top = jnp.where((succ_ref[row, cols] >> 7) == top_row, 1.0, 0.0)
            same = column_ref[cols, row] == code_ref[row, cols]
            within = summed_down(jnp.where(same, earlier, 0.0))
            coarse = (base.astype(jnp.int32) & ~127).astype(jnp.float32)
            both = jnp.concatenate([coarse, base - coarse], axis=0).astype(jnp.bfloat16)
            starts = jnp.dot(both, hot, preferred_element_type=jnp.float32)
            begin = summed_down((starts[:tops] + starts[tops:]) * hot_top)
            base = base + product(hot_top.astype(jnp.bfloat16), hot)
            match = jnp.where(begin + within == rank_row, 1.0, 0.0).astype(jnp.bfloat16)
            r = reward_ref[row, cols]
            r1 = r.astype(jnp.bfloat16)
            rest = r - r1.astype(jnp.float32)
            r2 = rest.astype(jnp.bfloat16)
            r3 = (rest - r2.astype(jnp.float32)).astype(jnp.bfloat16)
            left = jnp.concatenate([match * piece for piece in (*source, r1, r2, r3)], axis=0)
            acc_ref[...] += product(left, hot)
        return base

    lax.fori_loop(0, width // step, one_chunk, count_ref[...])
    part = [acc_ref[i * RANKS : i * RANKS + ROWS, :] for i in range(5)]
    share = out_ref.shape[0] // 2
    out_ref[0:ROWS, :] = part[0] + part[1]
    out_ref[share : share + ROWS, :] = (part[2] + part[3]) + part[4]
    listed = columns(border_ref[...].astype(jnp.float32)).astype(jnp.int32)
    for side in range(4):
        for q in range(chunks):
            found = jnp.where(listed[:, side : side + 1] == along + q * LANES, down_f + 1.0, 0.0)
            row = share + ROWS + side * chunks + q
            out_ref[row : row + 1, :] = summed_down(found)
    blocks = anchor_ref.shape[0]
    for q in range(chunks):
        split_ref[pl.ds(q, blocks, chunks), :] = anchor_ref[:, q * LANES : (q + 1) * LANES]
    half = out_ref.at[pl.ds(pl.multiple_of(lax.axis_index("dst") * share, 8), share)]
    size = share + chunks
    pairs = []
    for b in range(blocks):
        pairs.append((half, out_any.at[pl.ds(b * size, share)]))
        pairs.append((split_ref.at[pl.ds(b * chunks, chunks)], out_any.at[pl.ds(b * size + share, chunks)]))
    run_copies(whole_copies(pairs, sem))


def graph_kernel(
    weight_ref, feature_any, succ_any, valid_any, border_any, out_ref, reward_ref,
    feature_ref, succ_ref, valid_ref, border_ref, part_ref, sem
):
    run_copies(
        whole_copies(
            [
                (feature_any, feature_ref),
                (succ_any, succ_ref),
                (valid_any, valid_ref),
                (border_any, border_ref),
            ],
            sem,
        )
    )
    turns, width = succ_ref.shape
    chunks = width // LANES
    edges = turns * chunks
    part_ref[edges : edges + 8, :] = jnp.zeros((8, LANES), jnp.float32)
    part_ref[edges : edges + 4, :] = border_ref[...].astype(jnp.float32)
    first_core = lax.axis_index("dst") == 0
    for q in range(chunks):
        cols = slice(q * LANES, (q + 1) * LANES)
        cost = weight_ref[0] * feature_ref[0, :, cols].astype(jnp.float32)
        for f in range(1, feature_ref.shape[0]):
            cost = cost + weight_ref[f] * feature_ref[f, :, cols].astype(jnp.float32)
        reward_ref[:, cols] = -cost
        masked = jnp.where(valid_ref[:, cols] == 1, -cost, NEG)
        turn_to = succ_ref[:, cols].astype(jnp.float32)
        part_ref[pl.ds(q, turns, chunks), :] = jnp.where(first_core, masked, turn_to)
    common = part_ref.shape[0]
    for b in range(out_ref.shape[0] // common):
        out_ref[b * common : (b + 1) * common, :] = part_ref[...]


def value_kernel(
    grid_x, dest_ref, mine_ref, other_ref, ext_ref, raised_ref, max_ref, inv_ref,
    reward, index, border, side_pad, spare_ref
):
    halves = ext_ref.shape[0]
    blocks = 8 * halves
    size = mine_ref.shape[0] // blocks
    chunks = ext_ref.shape[1] - 4
    turns = raised_ref.shape[1] // chunks
    edges = turns * chunks
    per_block = chunks * LANES
    dest = renumbered(dest_ref[own_block(grid_x)], per_block, blocks, grid_x)
    side_pad[...] = jnp.zeros_like(side_pad)
    sub = lax.broadcasted_iota(jnp.int32, (8, LANES), 0)
    lane = lax.broadcasted_iota(jnp.int32, (8, LANES), 1)
    dest_block, dest_place = lax.div(dest, per_block), lax.rem(dest, per_block)

    def unpack(first, second):
        for h in range(halves):

            def rows(i, carry, h=h):
                reward[h, i] = of_blocks(first, h, i, size)
                index[h, i] = of_blocks(second, h, i, size).astype(jnp.int32)
                return carry

            lax.fori_loop(0, edges, rows, 0, unroll=8)
            for side in range(4):
                border[h, side] = of_blocks(first, h, edges + side, size).astype(jnp.int32)

    by_core(unpack, mine_ref, other_ref)
    for h in range(halves):
        for side in range(4):
            found = (border[h, side] == dest_place) & (h * 8 + sub == dest_block)
            entry = jnp.max(jnp.where(found, lane + 1, 0).astype(jnp.float32), axis=1, keepdims=True)
            side_pad[side, 8 + 8 * h : 16 + 8 * h, :] = jnp.broadcast_to(entry, (8, LANES))
    shifts = ((1, -1), (0, 1), (3, -grid_x), (2, grid_x))

    def shown(h, side):
        facing, by = shifts[side]
        start = 8 + 8 * h + by
        return side_pad[facing, start : start + 8, :]

    def dest_index(h):
        where = jnp.where(h * 8 + sub == dest_block, dest_place, -1)
        for side in range(4):
            entry = shown(h, side).astype(jnp.int32)
            where = jnp.where(entry > 0, per_block + side * LANES + entry - 1, where)
        return where

    def bring_halo(values):
        for h in range(halves):
            table = [values[h, q] for q in range(chunks)]
            for side in range(4):
                side_pad[side, 8 + 8 * h : 16 + 8 * h, :] = table_gather(table, border[h, side])
        for h in range(halves):
            for side in range(4):
                values[h, chunks + side] = shown(h, side)

    def summed(out):
        top = functools.reduce(jnp.maximum, out)
        raised = [jnp.exp(score - top) for score in out]
        return top, raised, functools.reduce(jnp.add, raised)

    def scores_of(values, h, q):
        tables = [values[h, r] for r in range(chunks + 4)]
        out = []
        for a in range(turns):
            rows = tables if a else tables[:chunks]
            out.append(reward[h, a * chunks + q] + table_gather(rows, index[h, a * chunks + q]))
        return summed(out)

    def store_value(h, q, top, total, into):
        value = top + jnp.log(total)
        into[h, q] = jnp.where(target_mask(dest, h, q, per_block), 0.0, value)

    wanted = [dest_index(h) for h in range(halves)]

    def first_chunk(q, inner):
        for h in range(halves):
            out = []
            for a in range(turns):
                before = jnp.where(index[h, a * chunks + q] == wanted[h], 0.0, -START_COST)
                out.append(reward[h, a * chunks + q] + before)
            top, _, total = summed(out)
            store_value(h, q, top, total, spare_ref)
        return inner

    lax.fori_loop(0, chunks, first_chunk, 0, unroll=2)

    def backup(values, into):
        bring_halo(values)

        def one_chunk(q, inner):
            for h in range(halves):
                top, _, total = scores_of(values, h, q)
                store_value(h, q, top, total, into)
            return inner

        lax.fori_loop(0, chunks, one_chunk, 0, unroll=chunks // 2)

    def two_backups(step, carry):
        backup(spare_ref, ext_ref)
        backup(ext_ref, spare_ref)
        return carry

    lax.fori_loop(0, (HORIZON - 2) // 2, two_backups, 0)
    backup(spare_ref, ext_ref)
    bring_halo(ext_ref)

    def last_chunk(q, inner):
        for h in range(halves):
            top, raised, total = scores_of(ext_ref, h, q)
            max_ref[h, q] = top
            inv_ref[h, q] = 1.0 / total
            for a in range(turns):
                raised_ref[h, a * chunks + q] = raised[a]
        return inner

    lax.fori_loop(0, chunks, last_chunk, 0, unroll=chunks)


def push_kernel(
    grid_x, scale, dest_ref, mine_ref, other_ref, graph_mine, graph_other, ext_ref, raised_ref, max_ref,
    inv_ref, keep_ref, send_ref, counts, ends, order, values, source, slot, going, policy, back, scaled, total, arrived, side_pad, raw
):
    halves = ext_ref.shape[0]
    blocks = 8 * halves
    size, share = graph_mine.shape[0] // blocks, mine_ref.shape[0] // blocks
    chunks = max_ref.shape[1]
    edges = raised_ref.shape[1]
    turns = edges // chunks
    per_block = chunks * LANES
    slots = chunks + 4
    dest = renumbered(dest_ref[own_block(grid_x)], per_block, blocks, grid_x)
    core = lax.axis_index("dst")
    side_pad[...] = jnp.zeros_like(side_pad)

    def unpack(first, second):
        for h in range(halves):
            for n in range(slots):
                ends[h, n] = of_blocks(first, h, ROWS + n, share)
                order[h, n] = of_blocks(first, h, ROWS + slots + n, share).astype(jnp.int32)
                inverse = of_blocks(first, h, ROWS + 2 * slots + n, share).astype(jnp.int32)
                values[h, n] = lane_gather(ext_ref[h, n], inverse)

            def rows(r, carry, h=h):
                source[h, r] = of_blocks(first, h, r, share).astype(jnp.int32)
                policy[h, r] = of_blocks(second, h, r, share)
                return carry

            lax.fori_loop(0, ROWS, rows, 0, unroll=6)
            for r in range(ROWS, DEPTH):
                source[h, r] = jnp.zeros((8, LANES), jnp.int32)
                policy[h, r] = jnp.zeros((8, LANES), jnp.float32)
            for n in range(4 * chunks):
                back[h, n] = of_blocks(second, h, ROWS + n, share).astype(jnp.int32) - 1

    by_core(unpack, mine_ref, other_ref)
    deepest = jnp.max(functools.reduce(jnp.maximum, [ends[h, slots - 1] for h in range(halves)]))
    deepest = deepest.astype(jnp.int32)
    fits = deepest <= ROWS
    steps = lax.div(jnp.minimum(deepest, ROWS) + (STEP - 1), STEP)
    shifts = ((1, -1), (0, 1), (3, -grid_x), (2, grid_x))

    def shown(h, side):
        facing, by = shifts[side]
        start = 8 + 8 * h + by
        return side_pad[facing, start : start + 8, :]

    @pl.when(jnp.logical_not(fits))
    def _():
        for h in range(halves):
            for n in range(slots):
                order[h, n] = lax.broadcasted_iota(jnp.int32, (8, LANES), 1)

    for h in range(halves):
        for side in range(4):
            side_pad[side, 8 + 8 * h : 16 + 8 * h, :] = order[h, chunks + side].astype(jnp.float32)
    for h in range(halves):
        for side in range(4):
            lanes = shown(h, side).astype(jnp.int32)
            for q in range(chunks):
                entry = back[h, side * chunks + q]
                back[h, side * chunks + q] = jnp.where(
                    entry >= 0, lane_gather(lanes, jnp.maximum(entry, 0)), -1
                )

    def prepare(t, carry):
        row_before = [None] * halves
        for i in range(STEP):
            for h in range(halves):
                r = t * STEP + i
                src = source[h, r]
                place = r.astype(jnp.float32)
                row = functools.reduce(
                    jnp.add, [jnp.where(ends[h, n] <= place, 1, 0) for n in range(slots)]
                )
                slot[h, r] = row
                if i:
                    going[h, r] = jnp.where(row == row_before[h], 1.0, 0.0)
                row_before[h] = row
                bits = [(row & (1 << n)) != 0 for n in range(4)]
                picked = tree_select([values[h, n] for n in range(slots)], bits)
                top = table_gather([max_ref[h, q] for q in range(chunks)], src)
                policy[h, r] = jnp.exp(policy[h, r] + picked - top)
        return carry

    lax.fori_loop(0, steps, prepare, 0)
    for h in range(halves):
        for q in range(chunks):
            own = of_blocks(mine_ref, h, share - chunks + q, share)
            first = jnp.where(target_mask(dest, h, q, per_block), 0.0, own)
            total[h, q] = first
            scaled[h, q] = first * inv_ref[h, q]

    @pl.when(jnp.logical_not(fits))
    def _():
        def keep_turns(first, second):
            for h in range(halves):

                def rows(e, carry, h=h):
                    raw[h, e] = of_blocks(second, h, e, size).astype(jnp.int32)
                    return carry

                lax.fori_loop(0, edges, rows, 0)

        by_core(keep_turns, graph_mine, graph_other)

    zero = jnp.zeros((8, LANES), jnp.float32)

    def keep(h):
        for side in range(4):
            side_pad[side, 8 + 8 * h : 16 + 8 * h, :] = arrived[h, chunks + side]

    def add_flow(acc, row, flow):
        return [acc[n] + jnp.where(row == n, flow, 0.0) for n in range(slots)]

    def sum_arranged():
        for h in range(halves):
            for n in range(slots):
                arrived[h, n] = zero

        def one_step(t, carry):
            for h in range(halves):
                table = [scaled[h, q] for q in range(chunks)]
                step_sums = [zero] * slots
                for i in range(STEP):
                    r = t * STEP + i
                    flow = table_gather(table, source[h, r]) * policy[h, r]
                    if i:
                        flow = flow + going[h, r] * so_far
                    so_far = flow
                    row = slot[h, r]
                    step_sums = [jnp.where(row == n, so_far, step_sums[n]) for n in range(slots)]
                for n in range(slots):
                    arrived[h, n] = arrived[h, n] + step_sums[n]
            return carry

        lax.fori_loop(0, steps, one_step, 0)
        for h in range(halves):
            keep(h)

    def sum_turned():
        lane = lax.broadcasted_iota(jnp.int32, (8, LANES), 1)
        for h in range(halves):

            def one_edge_row(e, acc, h=h):
                flow = scaled[h, lax.rem(e, chunks)] * raised_ref[h, e]
                where = raw[h, e]

                def one_turn(k, state):
                    flow, where, acc = state[0], state[1], list(state[2:])
                    here = jnp.where((where & (LANES - 1)) == lane, where >> 7, -1)
                    acc = add_flow(acc, here, flow)
                    return (pltpu.roll(flow, 1, 1), pltpu.roll(where, 1, 1), *acc)

                return tuple(lax.fori_loop(0, LANES, one_turn, (flow, where, *acc))[2:])

            for n, value in enumerate(lax.fori_loop(0, edges, one_edge_row, (zero,) * slots)):
                arrived[h, n] = value
            keep(h)

    def push(round_index, carry):
        pl.when(fits)(sum_arranged)
        pl.when(jnp.logical_not(fits))(sum_turned)
        for h in range(halves):
            landed = [shown(h, side) for side in range(4)]
            for q in range(chunks):
                value = lane_gather(arrived[h, q], order[h, q])
                for side in range(4):
                    entry = back[h, side * chunks + q]
                    got = lane_gather(landed[side], jnp.maximum(entry, 0))
                    value = value + jnp.where(entry >= 0, got, 0.0)
                value = jnp.where(target_mask(dest, h, q, per_block), 0.0, value)
                total[h, q] = total[h, q] + value
                scaled[h, q] = value * inv_ref[h, q]
        return carry

    lax.fori_loop(0, HORIZON - 1, push, 0)
    rows_out = edges // 2
    apart = counts.shape[1] // blocks
    for h in range(halves):
        for q in range(chunks):
            weight = total[h, q] * inv_ref[h, q] * scale
            for part, piece in ((core, 0), (1 - core, 1)):
                for a in range(turns // 2):
                    value = weight * raised_ref[h, (part * (turns // 2) + a) * chunks + q]
                    start = h * 8 * apart + a * chunks + q
                    counts[piece, pl.ds(start, 8, stride=apart), :] = value
    for piece, out_ref in ((0, keep_ref), (1, send_ref)):
        for b in range(blocks):
            out_ref[b * rows_out : (b + 1) * rows_out, :] = counts[
                piece, b * apart : b * apart + rows_out, :
            ]


VMEM_SPEC = pl.BlockSpec(memory_space=pltpu.VMEM)
SMEM_SPEC = pl.BlockSpec(memory_space=pltpu.SMEM)
HBM_SPEC = pl.BlockSpec(memory_space=pltpu.HBM)
PARAMS = pltpu.CompilerParams(vmem_limit_bytes=48 * 1024 * 1024)


def f32(*shape):
    return jax.ShapeDtypeStruct(shape, jnp.float32)


def call_graph(cost_weights, features, successors, turn_valid, border_lists, blocks):
    turns, width = successors.shape
    chunks = width // LANES
    rows = turns * chunks + 8
    return pl.pallas_call(
        graph_kernel,
        out_shape=(f32(blocks * rows, LANES), f32(turns, width)),
        in_specs=[SMEM_SPEC] + [HBM_SPEC] * 4,
        out_specs=(VMEM_SPEC, VMEM_SPEC),
        scratch_shapes=[
            pltpu.VMEM(features.shape, features.dtype),
            pltpu.VMEM(successors.shape, jnp.int32),
            pltpu.VMEM(turn_valid.shape, jnp.int32),
            pltpu.VMEM(border_lists.shape, jnp.int32),
            pltpu.VMEM((rows, LANES), jnp.float32),
            pltpu.SemaphoreType.DMA((4,)),
        ],
        compiler_params=pltpu.CompilerParams(vmem_limit_bytes=63 * 1024 * 1024),
        name="own_graph",
    )(cost_weights, features, successors, turn_valid, border_lists)


def arranged_rows(chunks):
    most = ROWS + max(3 * (chunks + 4), 4 * chunks)
    return -(-most // 8) * 8


def call_arrange(successors, turn_valid, border_lists, anchors, reward):
    chunks = successors.shape[1] // LANES
    share = arranged_rows(chunks)
    blocks = anchors.shape[0]
    return pl.pallas_call(
        arrange_kernel,
        out_shape=f32(blocks * (share + chunks), LANES),
        in_specs=[HBM_SPEC] * 4 + [VMEM_SPEC],
        out_specs=HBM_SPEC,
        scratch_shapes=[
            pltpu.VMEM(successors.shape, jnp.int32),
            pltpu.VMEM(turn_valid.shape, jnp.int32),
            pltpu.VMEM(border_lists.shape, jnp.int32),
            pltpu.VMEM(anchors.shape, jnp.float32),
            pltpu.VMEM((blocks * chunks, LANES), jnp.float32),
            pltpu.VMEM((2 * share, LANES), jnp.float32),
            *[pltpu.VMEM((16, LANES), jnp.float32)] * 5,
            pltpu.VMEM((8, LANES), jnp.float32),
            pltpu.VMEM(successors.shape, jnp.float32),
            pltpu.VMEM(successors.shape, jnp.float32),
            pltpu.VMEM(successors.shape[::-1], jnp.float32),
            pltpu.VMEM((5 * RANKS, LANES), jnp.float32),
            pltpu.SemaphoreType.DMA((2 * blocks,)),
        ],
        compiler_params=PARAMS,
        cost_estimate=pl.CostEstimate(flops=4_000_000_000, bytes_accessed=400_000, transcendentals=0),
        name="arrange_turns",
    )(successors, turn_valid, border_lists, anchors, reward)


def call_values(destinations, mine, other, blocks, grid_x, turns, chunks):
    halves = blocks // 8
    edges = turns * chunks
    return pl.pallas_call(
        functools.partial(value_kernel, grid_x),
        out_shape=(
            f32(halves, chunks + 4, 8, LANES),
            f32(halves, edges, 8, LANES),
            f32(halves, chunks, 8, LANES),
            f32(halves, chunks, 8, LANES),
        ),
        in_specs=[SMEM_SPEC, VMEM_SPEC, VMEM_SPEC],
        out_specs=(VMEM_SPEC,) * 4,
        scratch_shapes=[
            pltpu.VMEM((halves, edges, 8, LANES), jnp.float32),
            pltpu.VMEM((halves, edges, 8, LANES), jnp.int32),
            pltpu.VMEM((halves, 4, 8, LANES), jnp.int32),
            pltpu.VMEM((4, blocks + 16, LANES), jnp.float32),
            pltpu.VMEM((halves, chunks + 4, 8, LANES), jnp.float32),
        ],
        compiler_params=PARAMS,
        cost_estimate=pl.CostEstimate(flops=40_000_000, bytes_accessed=40_000_000, transcendentals=2_000_000),
        name="soft_values",
    )(destinations, mine, other)


def call_push(destinations, mine, other, graph_mine, graph_other, ext, raised, top, inv, grid_x, scale):
    halves, edges = raised.shape[:2]
    blocks = 8 * halves
    chunks = top.shape[1]

    def vmem(rows, dtype=jnp.float32):
        return pltpu.VMEM((halves, rows, 8, LANES), dtype)

    return pl.pallas_call(
        functools.partial(push_kernel, grid_x, scale),
        out_shape=(f32(blocks * edges // 2, LANES),) * 2,
        in_specs=[SMEM_SPEC] + [VMEM_SPEC] * 8,
        out_specs=(VMEM_SPEC,) * 2,
        scratch_shapes=[
            pltpu.VMEM((2, blocks * padded_rows(edges // 2), LANES), jnp.float32),
            vmem(chunks + 4),
            vmem(chunks + 4, jnp.int32),
            vmem(chunks + 4),
            vmem(DEPTH, jnp.int32),
            vmem(DEPTH, jnp.int32),
            vmem(DEPTH),
            vmem(DEPTH),
            vmem(4 * chunks, jnp.int32),
            vmem(chunks),
            vmem(chunks),
            vmem(chunks + 4),
            pltpu.VMEM((4, blocks + 16, LANES), jnp.float32),
            vmem(edges, jnp.int32),
        ],
        compiler_params=PARAMS,
        name="push_mass",
    )(destinations, mine, other, graph_mine, graph_other, ext, raised, top, inv)


def to_blocks(array):
    return lax.all_to_all(array, BLOCK_AXES, 0, 0, tiled=True)


def other_core(array):
    return lax.ppermute(array, "dst", [(0, 1), (1, 0)])


def per_destination(
    features, cost_weights, successors, turn_valid, border_lists, destinations, anchors, demo_counts
):
    turns, own_count = successors.shape
    chunks = own_count // LANES
    edges = turns * chunks
    grid_x = lax.axis_size("gx")
    blocks = lax.axis_size("gy") * grid_x
    groups = lax.axis_size("dst")
    pieces, reward = call_graph(cost_weights, features, successors, turn_valid, border_lists, blocks)
    graph = to_blocks(pieces)
    arranged = call_arrange(successors, turn_valid, border_lists, anchors, reward)
    core = lax.axis_index("dst")
    demo_term = jnp.where(turn_valid == 1, demo_counts, 0).astype(jnp.float32) / 3.0
    own_feats = lax.dynamic_slice_in_dim(features, core * (turns // 2), turns // 2, axis=1)
    graph = lax.optimization_barrier((graph, arranged))[0]
    arranged = to_blocks(arranged)
    graph = (graph, other_core(graph))
    values = call_values(destinations, *graph, blocks, grid_x, turns, chunks)
    arranged, own_feats, demo_term, *values = lax.optimization_barrier(
        (arranged, own_feats, demo_term, *values)
    )
    arranged = (arranged, other_core(arranged))
    scale = 1.0 / (anchors.shape[0] * groups * HORIZON)
    kept, sent = call_push(destinations, *arranged, *graph, *values, grid_x, scale)
    halved = (kept + other_core(sent)).reshape(blocks, edges // 2, LANES)
    half = jnp.sum(to_blocks(halved), axis=0)
    other = other_core(half)
    part = (turns // 2, own_count)
    own_gap = lax.dynamic_slice_in_dim(demo_term, core * part[0], part[0]) - half.reshape(part)
    own_feats = own_feats.astype(jnp.float32)
    block_term = jnp.sum(own_gap[None] * own_feats, axis=(1, 2)) / (own_count * blocks)
    terms = jnp.broadcast_to(block_term, (groups * blocks, 1, block_term.shape[0]))
    terms = lax.all_to_all(terms, (*BLOCK_AXES, "dst"), 0, 0, tiled=True)
    visits = jnp.concatenate([jnp.where(core == 0, half, other), jnp.where(core == 0, other, half)])
    return demo_term - visits.reshape(turns, own_count), jnp.sum(terms, axis=(0, 1))


def passed_along(array, axis, by):
    length = lax.axis_size(axis)
    pairs = [(i, i + by) for i in range(length) if 0 <= i + by < length]
    return lax.ppermute(array, axis, pairs)


def bring_values(values, border_lists):
    outgoing = values[:, border_lists]
    north_part = passed_along(outgoing[:, 1], "gx", 1)
    south_part = passed_along(outgoing[:, 0], "gx", -1)
    west_part = passed_along(outgoing[:, 3], "gy", 1)
    east_part = passed_along(outgoing[:, 2], "gy", -1)
    return jnp.concatenate([north_part, south_part, west_part, east_part], axis=1)


def return_flow(arrived, border_lists, own_count, border_width):
    local_part = arrived[:, :own_count]
    halo_part = arrived[:, own_count:].reshape(arrived.shape[0], 4, border_width)
    from_south = passed_along(halo_part[:, 0], "gx", -1)
    from_north = passed_along(halo_part[:, 1], "gx", 1)
    from_east = passed_along(halo_part[:, 2], "gy", -1)
    from_west = passed_along(halo_part[:, 3], "gy", 1)
    returned = jnp.stack([from_north, from_south, from_west, from_east], axis=1)
    return local_part.at[:, border_lists].add(returned)


def select_cells(cells, flat_index, turn_shape):
    picked = jnp.take(cells, flat_index, axis=1)
    return picked.reshape(cells.shape[0], turn_shape[0], turn_shape[1])


def turn_scores(values, halo_cells, reward, flat_turns, usable):
    extended = jnp.concatenate([values, halo_cells], axis=1)
    scores = reward[None] + select_cells(extended, flat_turns, usable.shape)
    return jnp.where(usable[None], scores, NEG)


def per_block(
    features, cost_weights, successors, turn_valid, border_lists, destinations, anchors, demo_counts
):
    own_count = successors.shape[1]
    border_width = border_lists.shape[1]
    dest_count = anchors.shape[0]
    slot_total = own_count + 4 * border_width
    block_index = lax.axis_index("gx") * lax.axis_size("gy") + lax.axis_index("gy")
    positions = jnp.arange(own_count, dtype=jnp.int32)
    is_target = positions[None, :] == (destinations - block_index * own_count)[:, None]
    usable = turn_valid == 1
    feats = features.astype(jnp.float32)
    reward = -jnp.sum(feats * cost_weights[:, None, None], axis=0)
    flat_turns = successors.reshape(-1)
    values = jnp.where(is_target, 0.0, -START_COST).astype(jnp.float32)
    for round_index in range(HORIZON):
        halo_cells = bring_values(values, border_lists)
        scores = turn_scores(values, halo_cells, reward, flat_turns, usable)
        row_max = jnp.max(scores, axis=1)
        new_values = row_max + jnp.log(jnp.sum(jnp.exp(scores - row_max[:, None]), axis=1))
        values = jnp.where(is_target, 0.0, new_values)
    halo_cells = bring_values(values, border_lists)
    scores = turn_scores(values, halo_cells, reward, flat_turns, usable)
    row_max = jnp.max(scores, axis=1)
    raised = jnp.exp(scores - row_max[:, None])
    policy = raised / jnp.sum(raised, axis=1, keepdims=True)
    mass_now = jnp.where(is_target, 0.0, anchors)
    turn_counts = jnp.zeros(successors.shape, jnp.float32)
    for round_index in range(HORIZON):
        turn_flow = mass_now[:, None, :] * policy
        turn_counts = turn_counts + jnp.sum(turn_flow, axis=0)
        if round_index + 1 < HORIZON:
            arrived = (
                jnp.zeros((dest_count, slot_total), jnp.float32)
                .at[:, flat_turns]
                .add(turn_flow.reshape(dest_count, -1))
            )
            landed = return_flow(arrived, border_lists, own_count, border_width)
            mass_now = jnp.where(is_target, 0.0, landed)
    local_visits = turn_counts / (dest_count * lax.axis_size("dst") * HORIZON)
    visits = lax.psum(local_visits, "dst")
    demo_term = jnp.where(usable, demo_counts, 0).astype(jnp.float32) / 3.0
    count_gap = demo_term - visits
    total_segments = own_count * lax.axis_size("gx") * lax.axis_size("gy")
    own_gap = demo_term / lax.axis_size("dst") - local_visits
    block_term = jnp.sum(own_gap[None] * feats, axis=(1, 2)) / total_segments
    gradient = lax.psum(block_term, ("gx", "gy", "dst"))
    return (count_gap, gradient)


def local(features, cost_weights, successors, turn_valid, border_lists, destinations, anchors, demo_counts):
    args = (
        features, cost_weights, successors, turn_valid, border_lists, destinations, anchors, demo_counts
    )
    blocks = lax.axis_size("gx") * lax.axis_size("gy")
    fits = (
        anchors.shape[0] == blocks
        and blocks % 8 == 0
        and lax.axis_size("dst") == 2
        and lax.axis_size("gx") in (2, 4, 8)
        and lax.axis_size("gy") in (2, 4, 8)
        and successors.shape[1] == 8 * LANES
        and border_lists.shape[1] == LANES
    )
    return per_destination(*args) if fits else per_block(*args)


def solution(mesh):
    in_specs = (
        P(None, None, ("gx", "gy")),
        P(),
        P(None, ("gx", "gy")),
        P(None, ("gx", "gy")),
        P(None, ("gx", "gy")),
        P("dst"),
        P("dst", ("gx", "gy")),
        P(None, ("gx", "gy")),
    )
    out_specs = (P(None, ("gx", "gy")), P())
    return jax.shard_map(local, mesh=mesh, in_specs=in_specs, out_specs=out_specs, check_vma=False)
```

```python
import functools

import jax
import jax.numpy as jnp
from jax import lax
from jax.experimental import pallas as pl
from jax.experimental.pallas import tpu as pltpu
from jax.sharding import PartitionSpec as P

HORIZON = 8
NEG = -1e30
START_COST = 100.0
LANES = 128
ROWS = 60
RANKS = -(-ROWS // 16) * 16
STEP = 14
DEPTH = -(-ROWS // STEP) * STEP
BLOCK_AXES = ("gy", "gx")

LANE_PICK = lax.GatherDimensionNumbers(
    offset_dims=(),
    collapsed_slice_dims=(1,),
    start_index_map=(1,),
    operand_batching_dims=(0,),
    start_indices_batching_dims=(0,),
)


def lane_gather(table, index):
    return lax.gather(
        table,
        index[..., None],
        LANE_PICK,
        (1, 1),
        mode=lax.GatherScatterMode.PROMISE_IN_BOUNDS,
    )


def tree_select(picked, bits):
    level = list(picked)
    for bit in bits:
        if len(level) == 1:
            break
        nxt = []
        for n in range(0, len(level), 2):
            if n + 1 < len(level):
                nxt.append(jnp.where(bit, level[n + 1], level[n]))
            else:
                nxt.append(level[n])
        level = nxt
    return level[0]


def row_bits(index, count):
    return [(index & (LANES << i)) != 0 for i in range(count)]


def table_gather(table_rows, index):
    lane = index & (LANES - 1)
    bits = row_bits(index, max(len(table_rows) - 1, 1).bit_length())
    return tree_select([lane_gather(row, lane) for row in table_rows], bits)


def run_copies(copies):
    for copy in copies:
        copy.start()
    for copy in copies:
        copy.wait()


def of_blocks(ref, half, row, per_block):
    return ref[pl.ds(half * 8 * per_block + row, 8, stride=per_block), :]


def whole_copies(pairs, sem):
    return [pltpu.make_async_copy(src, dst, sem.at[n]) for n, (src, dst) in enumerate(pairs)]


def by_core(what, mine, other):
    first = lax.axis_index("dst") == 0
    pl.when(first)(lambda: what(mine, other))
    pl.when(jnp.logical_not(first))(lambda: what(other, mine))


def own_block(grid_x):
    return lax.axis_index("gy") * grid_x + lax.axis_index("gx")


def renumbered(segment, per_block, blocks, grid_x):
    grid_y = blocks // grid_x
    block, place = lax.div(segment, per_block), lax.rem(segment, per_block)
    return (lax.rem(block, grid_y) * grid_x + lax.div(block, grid_y)) * per_block + place


def padded_rows(rows):
    tiles = -(-rows // 8)
    return (tiles + 1 - tiles % 2) * 8


def target_mask(dest, half, chunk, per_block):
    sub = lax.broadcasted_iota(jnp.int32, (8, LANES), 0)
    lane = lax.broadcasted_iota(jnp.int32, (8, LANES), 1)
    return (half * 8 + sub) * per_block + chunk * LANES + lane == dest


def arrange_kernel(
    succ_any, valid_any, border_any, anchor_any, reward_ref, out_any,
    succ_ref, valid_ref, border_ref, anchor_ref, split_ref, out_ref, count_ref, first_ref, order_ref, inverse_ref, placed_ref,
    pair_ref, lane_ref, code_ref, column_ref, acc_ref, sem
):
    run_copies(
        whole_copies(
            [
                (succ_any, succ_ref),
                (valid_any, valid_ref),
                (border_any, border_ref),
                (anchor_any, anchor_ref),
            ],
            sem,
        )
    )
    turns, width = succ_ref.shape
    chunks = width // LANES
    slots = chunks + 4
    step = 2 * LANES
    tops = 16
    square = (LANES, LANES)
    down = lax.broadcasted_iota(jnp.int32, square, 0)
    along = lax.broadcasted_iota(jnp.int32, square, 1)
    down_f, along_f = down.astype(jnp.float32), along.astype(jnp.float32)
    before = down < along
    unit = jnp.where(down == along, 1.0, 0.0)
    lane_row = lax.broadcasted_iota(jnp.int32, (LANES, step), 0)
    top_row = lax.broadcasted_iota(jnp.int32, (tops, step), 0)
    rank_row = lax.broadcasted_iota(jnp.int32, (RANKS, step), 0).astype(jnp.float32)
    last_dims = (((1,), (1,)), ((), ()))

    def product(left, right):
        return lax.dot_general(left, right, last_dims, preferred_element_type=jnp.float32)

    def columns(rows):
        return lax.dot_general(
            unit, rows, last_dims, precision=lax.Precision.HIGHEST, preferred_element_type=jnp.float32
        )

    def summed_down(array):
        return jnp.sum(array, axis=0, keepdims=True)

    def place_of(row, col):
        return summed_down(jnp.where((col > row) | ((col == row) & before), 1.0, 0.0))

    def count(a, total):
        for c in range(width // step):
            cols = slice(c * step, (c + 1) * step)
            u = succ_ref[pl.ds(a, 1), cols]
            low = jnp.where(valid_ref[pl.ds(a, 1), cols] == 1, u & (LANES - 1), -1)
            hot_low = jnp.where(low == lane_row, 1.0, 0.0).astype(jnp.bfloat16)
            hot_top = jnp.where((u >> 7) == top_row, 1.0, 0.0).astype(jnp.bfloat16)
            total = total + product(hot_top, hot_low)
        return total

    counts = lax.fori_loop(0, turns, count, jnp.zeros((tops, LANES), jnp.float32), unroll=2)
    count_columns = columns(counts)
    out_ref[...] = jnp.zeros_like(out_ref)
    for ref in (count_ref, first_ref, order_ref, inverse_ref, placed_ref, pair_ref):
        ref[...] = jnp.zeros_like(ref)
    for n in range(slots):
        i = n if n < chunks else n - chunks
        place = place_of(counts[n : n + 1, :], count_columns[:, n : n + 1])
        place = place if i % 2 == 0 else (LANES - 1.0) - place
        if (i // 2) % 2:
            place = jnp.where(place >= LANES // 2, place - LANES // 2, place + LANES // 2)
        first_ref[n : n + 1, :] = place
    first_columns = columns(first_ref[...])
    for n in range(slots):
        hit = first_columns[:, n : n + 1] == along_f
        inverse_ref[n : n + 1, :] = summed_down(jnp.where(hit, down_f, 0.0))
        placed_ref[n : n + 1, :] = summed_down(jnp.where(hit, count_columns[:, n : n + 1], 0.0))
    local = summed_down(placed_ref[0:chunks, :])
    room = -summed_down(placed_ref[chunks:tops, :])
    pair_ref[0:1, :] = local
    pair_ref[1:2, :] = room
    pair = columns(pair_ref[...])
    local_place, room_place = place_of(local, pair[:, 0:1]), place_of(room, pair[:, 1:2])
    pair_ref[0:1, :] = local_place
    pair_ref[1:2, :] = room_place
    pair = columns(pair_ref[...])
    goes = summed_down(jnp.where(pair[:, 1:2] == local_place, down_f, 0.0))
    comes = summed_down(jnp.where(pair[:, 0:1] == room_place, down_f, 0.0))
    full = (chunks, LANES)
    comes = jnp.broadcast_to(comes, full).astype(jnp.int32)
    goes = jnp.broadcast_to(goes, full)
    order_ref[0:chunks, :] = lane_gather(goes, first_ref[0:chunks, :].astype(jnp.int32))
    order_ref[chunks:tops, :] = first_ref[chunks:tops, :]
    inverse_ref[0:chunks, :] = lane_gather(inverse_ref[0:chunks, :], comes)
    placed_ref[0:chunks, :] = lane_gather(placed_ref[0:chunks, :], comes)
    running = jnp.zeros((1, LANES), jnp.float32)
    for n in range(slots):
        count_ref[n : n + 1, :] = running
        running = running + placed_ref[n : n + 1, :]
        out_ref[ROWS + n : ROWS + n + 1, :] = running
        out_ref[ROWS + slots + n : ROWS + slots + n + 1, :] = order_ref[n : n + 1, :]
        out_ref[ROWS + 2 * slots + n : ROWS + 2 * slots + n + 1, :] = inverse_ref[n : n + 1, :]
    for k in range(chunks):
        cols = slice(k * LANES, (k + 1) * LANES)
        u = succ_ref[:, cols]
        rows = [jnp.broadcast_to(order_ref[n : n + 1, :], (turns, LANES)) for n in range(slots)]
        lane = jnp.where(valid_ref[:, cols] == 1, table_gather(rows, u), -1.0)
        code = jnp.where(lane >= 0.0, lane + ((u >> 7) * LANES).astype(jnp.float32), -1.0)
        lane_ref[:, cols] = lane
        code_ref[:, cols] = code
        column_ref[cols, :] = columns(code)
    acc_ref[...] = jnp.zeros_like(acc_ref)
    earlier = jnp.where(
        lax.broadcasted_iota(jnp.int32, (step, step), 0) < lax.broadcasted_iota(jnp.int32, (step, step), 1),
        1.0,
        0.0,
    )
    lane_row_f = lane_row.astype(jnp.float32)

    def one_chunk(c, base):
        start = pl.multiple_of(c * step, step)
        cols = pl.ds(start, step)
        s = start + lax.broadcasted_iota(jnp.int32, (1, step), 1)
        source = [
            (s & ~7).astype(jnp.float32).astype(jnp.bfloat16),
            (s & 7).astype(jnp.float32).astype(jnp.bfloat16),
        ]
        for a in range(turns):
            row = slice(a, a + 1)
            hot = jnp.where(lane_ref[row, cols] == lane_row_f, 1.0, 0.0).astype(jnp.bfloat16)
            hot_top = jnp.where((succ_ref[row, cols] >> 7) == top_row, 1.0, 0.0)
            same = column_ref[cols, row] == code_ref[row, cols]
            within = summed_down(jnp.where(same, earlier, 0.0))
            coarse = (base.astype(jnp.int32) & ~127).astype(jnp.float32)
            both = jnp.concatenate([coarse, base - coarse], axis=0).astype(jnp.bfloat16)
            starts = jnp.dot(both, hot, preferred_element_type=jnp.float32)
            begin = summed_down((starts[:tops] + starts[tops:]) * hot_top)
            base = base + product(hot_top.astype(jnp.bfloat16), hot)
            match = jnp.where(begin + within == rank_row, 1.0, 0.0).astype(jnp.bfloat16)
            r = reward_ref[row, cols]
            r1 = r.astype(jnp.bfloat16)
            rest = r - r1.astype(jnp.float32)
            r2 = rest.astype(jnp.bfloat16)
            r3 = (rest - r2.astype(jnp.float32)).astype(jnp.bfloat16)
            left = jnp.concatenate([match * piece for piece in (*source, r1, r2, r3)], axis=0)
            acc_ref[...] += product(left, hot)
        return base

    lax.fori_loop(0, width // step, one_chunk, count_ref[...])
    part = [acc_ref[i * RANKS : i * RANKS + ROWS, :] for i in range(5)]
    share = out_ref.shape[0] // 2
    out_ref[0:ROWS, :] = part[0] + part[1]
    out_ref[share : share + ROWS, :] = (part[2] + part[3]) + part[4]
    listed = columns(border_ref[...].astype(jnp.float32)).astype(jnp.int32)
    for side in range(4):
        for q in range(chunks):
            found = jnp.where(listed[:, side : side + 1] == along + q * LANES, down_f + 1.0, 0.0)
            row = share + ROWS + side * chunks + q
            out_ref[row : row + 1, :] = summed_down(found)
    blocks = anchor_ref.shape[0]
    for q in range(chunks):
        split_ref[pl.ds(q, blocks, chunks), :] = anchor_ref[:, q * LANES : (q + 1) * LANES]
    half = out_ref.at[pl.ds(pl.multiple_of(lax.axis_index("dst") * share, 8), share)]
    size = share + chunks
    pairs = []
    for b in range(blocks):
        pairs.append((half, out_any.at[pl.ds(b * size, share)]))
        pairs.append((split_ref.at[pl.ds(b * chunks, chunks)], out_any.at[pl.ds(b * size + share, chunks)]))
    run_copies(whole_copies(pairs, sem))


def graph_kernel(
    weight_ref, feature_any, succ_any, valid_any, border_any, out_ref, reward_ref,
    feature_ref, succ_ref, valid_ref, border_ref, part_ref, sem
):
    run_copies(
        whole_copies(
            [
                (feature_any, feature_ref),
                (succ_any, succ_ref),
                (valid_any, valid_ref),
                (border_any, border_ref),
            ],
            sem,
        )
    )
    turns, width = succ_ref.shape
    chunks = width // LANES
    edges = turns * chunks
    part_ref[edges : edges + 8, :] = jnp.zeros((8, LANES), jnp.float32)
    part_ref[edges : edges + 4, :] = border_ref[...].astype(jnp.float32)
    first_core = lax.axis_index("dst") == 0
    for q in range(chunks):
        cols = slice(q * LANES, (q + 1) * LANES)
        cost = weight_ref[0] * feature_ref[0, :, cols].astype(jnp.float32)
        for f in range(1, feature_ref.shape[0]):
            cost = cost + weight_ref[f] * feature_ref[f, :, cols].astype(jnp.float32)
        reward_ref[:, cols] = -cost
        masked = jnp.where(valid_ref[:, cols] == 1, -cost, NEG)
        turn_to = succ_ref[:, cols].astype(jnp.float32)
        part_ref[pl.ds(q, turns, chunks), :] = jnp.where(first_core, masked, turn_to)
    common = part_ref.shape[0]
    for b in range(out_ref.shape[0] // common):
        out_ref[b * common : (b + 1) * common, :] = part_ref[...]


def regroup_kernel(pieces_ref, out_ref):
    halves, rows = out_ref.shape[:2]
    size = pieces_ref.shape[0] // (8 * halves)
    for h in range(halves):

        def one_row(i, carry, h=h):
            out_ref[h, i] = of_blocks(pieces_ref, h, i, size)
            return carry

        lax.fori_loop(0, rows, one_row, 0, unroll=8)


def value_kernel(
    grid_x, dest_ref, mine_ref, other_ref, ext_ref, raised_ref, max_ref, inv_ref,
    reward, index, border, side_pad, spare_ref
):
    halves = ext_ref.shape[0]
    blocks = 8 * halves
    chunks = ext_ref.shape[1] - 4
    turns = raised_ref.shape[1] // chunks
    edges = turns * chunks
    per_block = chunks * LANES
    dest = renumbered(dest_ref[own_block(grid_x)], per_block, blocks, grid_x)
    side_pad[...] = jnp.zeros_like(side_pad)
    sub = lax.broadcasted_iota(jnp.int32, (8, LANES), 0)
    lane = lax.broadcasted_iota(jnp.int32, (8, LANES), 1)
    dest_block, dest_place = lax.div(dest, per_block), lax.rem(dest, per_block)

    def unpack(first, second):
        for h in range(halves):

            def rows(i, carry, h=h):
                reward[h, i] = first[h, i]
                index[h, i] = second[h, i].astype(jnp.int32)
                return carry

            lax.fori_loop(0, edges, rows, 0, unroll=8)
            for side in range(4):
                border[h, side] = first[h, edges + side].astype(jnp.int32)

    by_core(unpack, mine_ref, other_ref)
    for h in range(halves):
        for side in range(4):
            found = (border[h, side] == dest_place) & (h * 8 + sub == dest_block)
            entry = jnp.max(jnp.where(found, lane + 1, 0).astype(jnp.float32), axis=1, keepdims=True)
            side_pad[side, 8 + 8 * h : 16 + 8 * h, :] = jnp.broadcast_to(entry, (8, LANES))
    shifts = ((1, -1), (0, 1), (3, -grid_x), (2, grid_x))

    def shown(h, side):
        facing, by = shifts[side]
        start = 8 + 8 * h + by
        return side_pad[facing, start : start + 8, :]

    def dest_index(h):
        where = jnp.where(h * 8 + sub == dest_block, dest_place, -1)
        for side in range(4):
            entry = shown(h, side).astype(jnp.int32)
            where = jnp.where(entry > 0, per_block + side * LANES + entry - 1, where)
        return where

    def bring_halo(values):
        for h in range(halves):
            table = [values[h, q] for q in range(chunks)]
            for side in range(4):
                side_pad[side, 8 + 8 * h : 16 + 8 * h, :] = table_gather(table, border[h, side])
        for h in range(halves):
            for side in range(4):
                values[h, chunks + side] = shown(h, side)

    def summed(out):
        top = functools.reduce(jnp.maximum, out)
        raised = [jnp.exp(score - top) for score in out]
        return top, raised, functools.reduce(jnp.add, raised)

    def scores_of(values, h, q):
        tables = [values[h, r] for r in range(chunks + 4)]
        out = []
        for a in range(turns):
            rows = tables if a else tables[:chunks]
            out.append(reward[h, a * chunks + q] + table_gather(rows, index[h, a * chunks + q]))
        return summed(out)

    def store_value(h, q, top, total, into):
        value = top + jnp.log(total)
        into[h, q] = jnp.where(target_mask(dest, h, q, per_block), 0.0, value)

    wanted = [dest_index(h) for h in range(halves)]

    def first_chunk(q, inner):
        for h in range(halves):
            out = []
            for a in range(turns):
                before = jnp.where(index[h, a * chunks + q] == wanted[h], 0.0, -START_COST)
                out.append(reward[h, a * chunks + q] + before)
            top, _, total = summed(out)
            store_value(h, q, top, total, spare_ref)
        return inner

    lax.fori_loop(0, chunks, first_chunk, 0, unroll=2)

    def backup(values, into):
        bring_halo(values)

        def one_chunk(q, inner):
            for h in range(halves):
                top, _, total = scores_of(values, h, q)
                store_value(h, q, top, total, into)
            return inner

        lax.fori_loop(0, chunks, one_chunk, 0, unroll=chunks)

    def two_backups(step, carry):
        backup(spare_ref, ext_ref)
        backup(ext_ref, spare_ref)
        return carry

    lax.fori_loop(0, (HORIZON - 2) // 2, two_backups, 0)
    backup(spare_ref, ext_ref)
    bring_halo(ext_ref)

    def last_chunk(q, inner):
        for h in range(halves):
            top, raised, total = scores_of(ext_ref, h, q)
            max_ref[h, q] = top
            inv_ref[h, q] = 1.0 / total
            for a in range(turns):
                raised_ref[h, a * chunks + q] = raised[a]
        return inner

    lax.fori_loop(0, chunks, last_chunk, 0, unroll=chunks)


def push_kernel(
    grid_x, scale, dest_ref, mine_ref, other_ref, graph_mine, graph_other, ext_ref, raised_ref, max_ref,
    inv_ref, keep_ref, send_ref, counts, ends, order, values, source, slot, going, policy, back, scaled, total, arrived, side_pad, raw
):
    halves = ext_ref.shape[0]
    blocks = 8 * halves
    share = mine_ref.shape[1]
    chunks = max_ref.shape[1]
    edges = raised_ref.shape[1]
    turns = edges // chunks
    per_block = chunks * LANES
    slots = chunks + 4
    dest = renumbered(dest_ref[own_block(grid_x)], per_block, blocks, grid_x)
    core = lax.axis_index("dst")
    side_pad[...] = jnp.zeros_like(side_pad)

    def unpack(first, second):
        for h in range(halves):
            for n in range(slots):
                ends[h, n] = first[h, ROWS + n]
                order[h, n] = first[h, ROWS + slots + n].astype(jnp.int32)
                inverse = first[h, ROWS + 2 * slots + n].astype(jnp.int32)
                values[h, n] = lane_gather(ext_ref[h, n], inverse)

            def rows(r, carry, h=h):
                source[h, r] = first[h, r].astype(jnp.int32)
                policy[h, r] = second[h, r]
                return carry

            lax.fori_loop(0, ROWS, rows, 0, unroll=6)
            for r in range(ROWS, DEPTH):
                source[h, r] = jnp.zeros((8, LANES), jnp.int32)
                policy[h, r] = jnp.zeros((8, LANES), jnp.float32)
            for n in range(4 * chunks):
                back[h, n] = second[h, ROWS + n].astype(jnp.int32) - 1

    by_core(unpack, mine_ref, other_ref)
    deepest = jnp.max(functools.reduce(jnp.maximum, [ends[h, slots - 1] for h in range(halves)]))
    deepest = deepest.astype(jnp.int32)
    fits = deepest <= ROWS
    steps = lax.div(jnp.minimum(deepest, ROWS) + (STEP - 1), STEP)
    shifts = ((1, -1), (0, 1), (3, -grid_x), (2, grid_x))

    def shown(h, side):
        facing, by = shifts[side]
        start = 8 + 8 * h + by
        return side_pad[facing, start : start + 8, :]

    @pl.when(jnp.logical_not(fits))
    def _():
        for h in range(halves):
            for n in range(slots):
                order[h, n] = lax.broadcasted_iota(jnp.int32, (8, LANES), 1)

    for h in range(halves):
        for side in range(4):
            side_pad[side, 8 + 8 * h : 16 + 8 * h, :] = order[h, chunks + side].astype(jnp.float32)
    for h in range(halves):
        for side in range(4):
            lanes = shown(h, side).astype(jnp.int32)
            for q in range(chunks):
                entry = back[h, side * chunks + q]
                back[h, side * chunks + q] = jnp.where(
                    entry >= 0, lane_gather(lanes, jnp.maximum(entry, 0)), -1
                )

    def prepare(t, carry):
        row_before = [None] * halves
        for i in range(STEP):
            for h in range(halves):
                r = t * STEP + i
                src = source[h, r]
                place = r.astype(jnp.float32)
                row = functools.reduce(
                    jnp.add, [jnp.where(ends[h, n] <= place, 1, 0) for n in range(slots)]
                )
                slot[h, r] = row
                if i:
                    going[h, r] = jnp.where(row == row_before[h], 1.0, 0.0)
                row_before[h] = row
                bits = [(row & (1 << n)) != 0 for n in range(4)]
                picked = tree_select([values[h, n] for n in range(slots)], bits)
                top = table_gather([max_ref[h, q] for q in range(chunks)], src)
                policy[h, r] = jnp.exp(policy[h, r] + picked - top)
        return carry

    lax.fori_loop(0, steps, prepare, 0)
    for h in range(halves):
        for q in range(chunks):
            own = mine_ref[h, share - chunks + q]
            first = jnp.where(target_mask(dest, h, q, per_block), 0.0, own)
            total[h, q] = first
            scaled[h, q] = first * inv_ref[h, q]

    @pl.when(jnp.logical_not(fits))
    def _():
        def keep_turns(first, second):
            for h in range(halves):

                def rows(e, carry, h=h):
                    raw[h, e] = second[h, e].astype(jnp.int32)
                    return carry

                lax.fori_loop(0, edges, rows, 0)

        by_core(keep_turns, graph_mine, graph_other)

    zero = jnp.zeros((8, LANES), jnp.float32)

    def keep(h):
        for side in range(4):
            side_pad[side, 8 + 8 * h : 16 + 8 * h, :] = arrived[h, chunks + side]

    def add_flow(acc, row, flow):
        return [acc[n] + jnp.where(row == n, flow, 0.0) for n in range(slots)]

    def sum_arranged():
        for h in range(halves):
            for n in range(slots):
                arrived[h, n] = zero

        def one_step(t, carry):
            for h in range(halves):
                table = [scaled[h, q] for q in range(chunks)]
                step_sums = [zero] * slots
                for i in range(STEP):
                    r = t * STEP + i
                    flow = table_gather(table, source[h, r]) * policy[h, r]
                    if i:
                        flow = flow + going[h, r] * so_far
                    so_far = flow
                    row = slot[h, r]
                    step_sums = [jnp.where(row == n, so_far, step_sums[n]) for n in range(slots)]
                for n in range(slots):
                    arrived[h, n] = arrived[h, n] + step_sums[n]
            return carry

        lax.fori_loop(0, steps, one_step, 0)
        for h in range(halves):
            keep(h)

    def sum_turned():
        lane = lax.broadcasted_iota(jnp.int32, (8, LANES), 1)
        for h in range(halves):

            def one_edge_row(e, acc, h=h):
                flow = scaled[h, lax.rem(e, chunks)] * raised_ref[h, e]
                where = raw[h, e]

                def one_turn(k, state):
                    flow, where, acc = state[0], state[1], list(state[2:])
                    here = jnp.where((where & (LANES - 1)) == lane, where >> 7, -1)
                    acc = add_flow(acc, here, flow)
                    return (pltpu.roll(flow, 1, 1), pltpu.roll(where, 1, 1), *acc)

                return tuple(lax.fori_loop(0, LANES, one_turn, (flow, where, *acc))[2:])

            for n, value in enumerate(lax.fori_loop(0, edges, one_edge_row, (zero,) * slots)):
                arrived[h, n] = value
            keep(h)

    def push(round_index, carry):
        pl.when(fits)(sum_arranged)
        pl.when(jnp.logical_not(fits))(sum_turned)
        for h in range(halves):
            landed = [shown(h, side) for side in range(4)]
            for q in range(chunks):
                value = lane_gather(arrived[h, q], order[h, q])
                for side in range(4):
                    entry = back[h, side * chunks + q]
                    got = lane_gather(landed[side], jnp.maximum(entry, 0))
                    value = value + jnp.where(entry >= 0, got, 0.0)
                value = jnp.where(target_mask(dest, h, q, per_block), 0.0, value)
                total[h, q] = total[h, q] + value
                scaled[h, q] = value * inv_ref[h, q]
        return carry

    lax.fori_loop(0, HORIZON - 1, push, 0)
    rows_out = edges // 2
    apart = counts.shape[1] // blocks
    for h in range(halves):
        for q in range(chunks):
            weight = total[h, q] * inv_ref[h, q] * scale
            for part, piece in ((core, 0), (1 - core, 1)):
                for a in range(turns // 2):
                    value = weight * raised_ref[h, (part * (turns // 2) + a) * chunks + q]
                    start = h * 8 * apart + a * chunks + q
                    counts[piece, pl.ds(start, 8, stride=apart), :] = value
    for piece, out_ref in ((0, keep_ref), (1, send_ref)):
        for b in range(blocks):
            out_ref[b * rows_out : (b + 1) * rows_out, :] = counts[
                piece, b * apart : b * apart + rows_out, :
            ]


VMEM_SPEC = pl.BlockSpec(memory_space=pltpu.VMEM)
SMEM_SPEC = pl.BlockSpec(memory_space=pltpu.SMEM)
HBM_SPEC = pl.BlockSpec(memory_space=pltpu.HBM)
PARAMS = pltpu.CompilerParams(vmem_limit_bytes=48 * 1024 * 1024)


def f32(*shape):
    return jax.ShapeDtypeStruct(shape, jnp.float32)


def call_graph(cost_weights, features, successors, turn_valid, border_lists, blocks):
    turns, width = successors.shape
    chunks = width // LANES
    rows = turns * chunks + 8
    return pl.pallas_call(
        graph_kernel,
        out_shape=(f32(blocks * rows, LANES), f32(turns, width)),
        in_specs=[SMEM_SPEC] + [HBM_SPEC] * 4,
        out_specs=(VMEM_SPEC, VMEM_SPEC),
        scratch_shapes=[
            pltpu.VMEM(features.shape, features.dtype),
            pltpu.VMEM(successors.shape, jnp.int32),
            pltpu.VMEM(turn_valid.shape, jnp.int32),
            pltpu.VMEM(border_lists.shape, jnp.int32),
            pltpu.VMEM((rows, LANES), jnp.float32),
            pltpu.SemaphoreType.DMA((4,)),
        ],
        compiler_params=pltpu.CompilerParams(vmem_limit_bytes=63 * 1024 * 1024),
        name="own_graph",
    )(cost_weights, features, successors, turn_valid, border_lists)


def arranged_rows(chunks):
    most = ROWS + max(3 * (chunks + 4), 4 * chunks)
    return -(-most // 8) * 8


def call_arrange(successors, turn_valid, border_lists, anchors, reward):
    chunks = successors.shape[1] // LANES
    share = arranged_rows(chunks)
    blocks = anchors.shape[0]
    return pl.pallas_call(
        arrange_kernel,
        out_shape=f32(blocks * (share + chunks), LANES),
        in_specs=[HBM_SPEC] * 4 + [VMEM_SPEC],
        out_specs=HBM_SPEC,
        scratch_shapes=[
            pltpu.VMEM(successors.shape, jnp.int32),
            pltpu.VMEM(turn_valid.shape, jnp.int32),
            pltpu.VMEM(border_lists.shape, jnp.int32),
            pltpu.VMEM(anchors.shape, jnp.float32),
            pltpu.VMEM((blocks * chunks, LANES), jnp.float32),
            pltpu.VMEM((2 * share, LANES), jnp.float32),
            *[pltpu.VMEM((16, LANES), jnp.float32)] * 5,
            pltpu.VMEM((8, LANES), jnp.float32),
            pltpu.VMEM(successors.shape, jnp.float32),
            pltpu.VMEM(successors.shape, jnp.float32),
            pltpu.VMEM(successors.shape[::-1], jnp.float32),
            pltpu.VMEM((5 * RANKS, LANES), jnp.float32),
            pltpu.SemaphoreType.DMA((2 * blocks,)),
        ],
        compiler_params=PARAMS,
        cost_estimate=pl.CostEstimate(flops=4_000_000_000, bytes_accessed=400_000, transcendentals=0),
        name="arrange_turns",
    )(successors, turn_valid, border_lists, anchors, reward)


def call_regroup(pieces, blocks):
    return pl.pallas_call(
        regroup_kernel,
        out_shape=f32(blocks // 8, pieces.shape[0] // blocks, 8, LANES),
        in_specs=[VMEM_SPEC],
        out_specs=VMEM_SPEC,
        compiler_params=PARAMS,
        name="regroup",
    )(pieces)


def call_values(destinations, mine, other, blocks, grid_x, turns, chunks):
    halves = blocks // 8
    edges = turns * chunks
    return pl.pallas_call(
        functools.partial(value_kernel, grid_x),
        out_shape=(
            f32(halves, chunks + 4, 8, LANES),
            f32(halves, edges, 8, LANES),
            f32(halves, chunks, 8, LANES),
            f32(halves, chunks, 8, LANES),
        ),
        in_specs=[SMEM_SPEC, VMEM_SPEC, VMEM_SPEC],
        out_specs=(VMEM_SPEC,) * 4,
        scratch_shapes=[
            pltpu.VMEM((halves, edges, 8, LANES), jnp.float32),
            pltpu.VMEM((halves, edges, 8, LANES), jnp.int32),
            pltpu.VMEM((halves, 4, 8, LANES), jnp.int32),
            pltpu.VMEM((4, blocks + 16, LANES), jnp.float32),
            pltpu.VMEM((halves, chunks + 4, 8, LANES), jnp.float32),
        ],
        compiler_params=PARAMS,
        cost_estimate=pl.CostEstimate(flops=40_000_000, bytes_accessed=40_000_000, transcendentals=2_000_000),
        name="soft_values",
    )(destinations, mine, other)


def call_push(destinations, mine, other, graph_mine, graph_other, ext, raised, top, inv, grid_x, scale):
    halves, edges = raised.shape[:2]
    blocks = 8 * halves
    chunks = top.shape[1]

    def vmem(rows, dtype=jnp.float32):
        return pltpu.VMEM((halves, rows, 8, LANES), dtype)

    return pl.pallas_call(
        functools.partial(push_kernel, grid_x, scale),
        out_shape=(f32(blocks * edges // 2, LANES),) * 2,
        in_specs=[SMEM_SPEC] + [VMEM_SPEC] * 8,
        out_specs=(VMEM_SPEC,) * 2,
        scratch_shapes=[
            pltpu.VMEM((2, blocks * padded_rows(edges // 2), LANES), jnp.float32),
            vmem(chunks + 4),
            vmem(chunks + 4, jnp.int32),
            vmem(chunks + 4),
            vmem(DEPTH, jnp.int32),
            vmem(DEPTH, jnp.int32),
            vmem(DEPTH),
            vmem(DEPTH),
            vmem(4 * chunks, jnp.int32),
            vmem(chunks),
            vmem(chunks),
            vmem(chunks + 4),
            pltpu.VMEM((4, blocks + 16, LANES), jnp.float32),
            vmem(edges, jnp.int32),
        ],
        compiler_params=PARAMS,
        name="push_mass",
    )(destinations, mine, other, graph_mine, graph_other, ext, raised, top, inv)


def to_blocks(array):
    return lax.all_to_all(array, BLOCK_AXES, 0, 0, tiled=True)


def other_core(array):
    return lax.ppermute(array, "dst", [(0, 1), (1, 0)])


def per_destination(
    features, cost_weights, successors, turn_valid, border_lists, destinations, anchors, demo_counts
):
    turns, own_count = successors.shape
    chunks = own_count // LANES
    edges = turns * chunks
    grid_x = lax.axis_size("gx")
    blocks = lax.axis_size("gy") * grid_x
    groups = lax.axis_size("dst")
    pieces, reward = call_graph(cost_weights, features, successors, turn_valid, border_lists, blocks)
    graph = to_blocks(pieces)
    arranged = call_arrange(successors, turn_valid, border_lists, anchors, reward)
    core = lax.axis_index("dst")
    demo_term = jnp.where(turn_valid == 1, demo_counts, 0).astype(jnp.float32) / 3.0
    own_feats = lax.dynamic_slice_in_dim(features, core * (turns // 2), turns // 2, axis=1)
    graph = lax.optimization_barrier((graph, arranged))[0]
    arranged = to_blocks(arranged)
    graph = call_regroup(graph, blocks)
    graph = (graph, other_core(graph))
    values = call_values(destinations, *graph, blocks, grid_x, turns, chunks)
    arranged, own_feats, demo_term, *values = lax.optimization_barrier(
        (arranged, own_feats, demo_term, *values)
    )
    arranged = call_regroup(arranged, blocks)
    arranged = (arranged, other_core(arranged))
    scale = 1.0 / (anchors.shape[0] * groups * HORIZON)
    kept, sent = call_push(destinations, *arranged, *graph, *values, grid_x, scale)
    halved = (kept + other_core(sent)).reshape(blocks, edges // 2, LANES)
    half = jnp.sum(to_blocks(halved), axis=0)
    other = other_core(half)
    part = (turns // 2, own_count)
    own_gap = lax.dynamic_slice_in_dim(demo_term, core * part[0], part[0]) - half.reshape(part)
    own_feats = own_feats.astype(jnp.float32)
    block_term = jnp.sum(own_gap[None] * own_feats, axis=(1, 2)) / (own_count * blocks)
    terms = jnp.broadcast_to(block_term, (groups * blocks, 1, block_term.shape[0]))
    terms = lax.all_to_all(terms, (*BLOCK_AXES, "dst"), 0, 0, tiled=True)
    visits = jnp.concatenate([jnp.where(core == 0, half, other), jnp.where(core == 0, other, half)])
    return demo_term - visits.reshape(turns, own_count), jnp.sum(terms, axis=(0, 1))


def passed_along(array, axis, by):
    length = lax.axis_size(axis)
    pairs = [(i, i + by) for i in range(length) if 0 <= i + by < length]
    return lax.ppermute(array, axis, pairs)


def bring_values(values, border_lists):
    outgoing = values[:, border_lists]
    north_part = passed_along(outgoing[:, 1], "gx", 1)
    south_part = passed_along(outgoing[:, 0], "gx", -1)
    west_part = passed_along(outgoing[:, 3], "gy", 1)
    east_part = passed_along(outgoing[:, 2], "gy", -1)
    return jnp.concatenate([north_part, south_part, west_part, east_part], axis=1)


def return_flow(arrived, border_lists, own_count, border_width):
    local_part = arrived[:, :own_count]
    halo_part = arrived[:, own_count:].reshape(arrived.shape[0], 4, border_width)
    from_south = passed_along(halo_part[:, 0], "gx", -1)
    from_north = passed_along(halo_part[:, 1], "gx", 1)
    from_east = passed_along(halo_part[:, 2], "gy", -1)
    from_west = passed_along(halo_part[:, 3], "gy", 1)
    returned = jnp.stack([from_north, from_south, from_west, from_east], axis=1)
    return local_part.at[:, border_lists].add(returned)


def select_cells(cells, flat_index, turn_shape):
    picked = jnp.take(cells, flat_index, axis=1)
    return picked.reshape(cells.shape[0], turn_shape[0], turn_shape[1])


def turn_scores(values, halo_cells, reward, flat_turns, usable):
    extended = jnp.concatenate([values, halo_cells], axis=1)
    scores = reward[None] + select_cells(extended, flat_turns, usable.shape)
    return jnp.where(usable[None], scores, NEG)


def per_block(
    features, cost_weights, successors, turn_valid, border_lists, destinations, anchors, demo_counts
):
    own_count = successors.shape[1]
    border_width = border_lists.shape[1]
    dest_count = anchors.shape[0]
    slot_total = own_count + 4 * border_width
    block_index = lax.axis_index("gx") * lax.axis_size("gy") + lax.axis_index("gy")
    positions = jnp.arange(own_count, dtype=jnp.int32)
    is_target = positions[None, :] == (destinations - block_index * own_count)[:, None]
    usable = turn_valid == 1
    feats = features.astype(jnp.float32)
    reward = -jnp.sum(feats * cost_weights[:, None, None], axis=0)
    flat_turns = successors.reshape(-1)
    values = jnp.where(is_target, 0.0, -START_COST).astype(jnp.float32)
    for round_index in range(HORIZON):
        halo_cells = bring_values(values, border_lists)
        scores = turn_scores(values, halo_cells, reward, flat_turns, usable)
        row_max = jnp.max(scores, axis=1)
        new_values = row_max + jnp.log(jnp.sum(jnp.exp(scores - row_max[:, None]), axis=1))
        values = jnp.where(is_target, 0.0, new_values)
    halo_cells = bring_values(values, border_lists)
    scores = turn_scores(values, halo_cells, reward, flat_turns, usable)
    row_max = jnp.max(scores, axis=1)
    raised = jnp.exp(scores - row_max[:, None])
    policy = raised / jnp.sum(raised, axis=1, keepdims=True)
    mass_now = jnp.where(is_target, 0.0, anchors)
    turn_counts = jnp.zeros(successors.shape, jnp.float32)
    for round_index in range(HORIZON):
        turn_flow = mass_now[:, None, :] * policy
        turn_counts = turn_counts + jnp.sum(turn_flow, axis=0)
        if round_index + 1 < HORIZON:
            arrived = (
                jnp.zeros((dest_count, slot_total), jnp.float32)
                .at[:, flat_turns]
                .add(turn_flow.reshape(dest_count, -1))
            )
            landed = return_flow(arrived, border_lists, own_count, border_width)
            mass_now = jnp.where(is_target, 0.0, landed)
    local_visits = turn_counts / (dest_count * lax.axis_size("dst") * HORIZON)
    visits = lax.psum(local_visits, "dst")
    demo_term = jnp.where(usable, demo_counts, 0).astype(jnp.float32) / 3.0
    count_gap = demo_term - visits
    total_segments = own_count * lax.axis_size("gx") * lax.axis_size("gy")
    own_gap = demo_term / lax.axis_size("dst") - local_visits
    block_term = jnp.sum(own_gap[None] * feats, axis=(1, 2)) / total_segments
    gradient = lax.psum(block_term, ("gx", "gy", "dst"))
    return (count_gap, gradient)


def local(features, cost_weights, successors, turn_valid, border_lists, destinations, anchors, demo_counts):
    args = (
        features, cost_weights, successors, turn_valid, border_lists, destinations, anchors, demo_counts
    )
    blocks = lax.axis_size("gx") * lax.axis_size("gy")
    fits = (
        anchors.shape[0] == blocks
        and blocks % 8 == 0
        and lax.axis_size("dst") == 2
        and lax.axis_size("gx") in (2, 4, 8)
        and lax.axis_size("gy") in (2, 4, 8)
        and successors.shape[1] == 8 * LANES
        and border_lists.shape[1] == LANES
    )
    return per_destination(*args) if fits else per_block(*args)


def solution(mesh):
    in_specs = (
        P(None, None, ("gx", "gy")),
        P(),
        P(None, ("gx", "gy")),
        P(None, ("gx", "gy")),
        P(None, ("gx", "gy")),
        P("dst"),
        P("dst", ("gx", "gy")),
        P(None, ("gx", "gy")),
    )
    out_specs = (P(None, ("gx", "gy")), P())
    return jax.shard_map(local, mesh=mesh, in_specs=in_specs, out_specs=out_specs, check_vma=False)
```

```python
import functools

import jax
import jax.numpy as jnp
from jax import lax
from jax.experimental import pallas as pl
from jax.experimental.pallas import tpu as pltpu
from jax.sharding import PartitionSpec as P

HORIZON = 8
NEG = -1e30
START_COST = 100.0
LANES = 128
ROWS = 60
RANKS = -(-ROWS // 16) * 16
STEP = 14
USUAL = 56
DEPTH = -(-ROWS // STEP) * STEP
BLOCK_AXES = ("gy", "gx")

LANE_PICK = lax.GatherDimensionNumbers(
    offset_dims=(),
    collapsed_slice_dims=(1,),
    start_index_map=(1,),
    operand_batching_dims=(0,),
    start_indices_batching_dims=(0,),
)


def lane_gather(table, index):
    return lax.gather(
        table,
        index[..., None],
        LANE_PICK,
        (1, 1),
        mode=lax.GatherScatterMode.PROMISE_IN_BOUNDS,
    )


def tree_select(picked, bits):
    level = list(picked)
    for bit in bits:
        if len(level) == 1:
            break
        nxt = []
        for n in range(0, len(level), 2):
            if n + 1 < len(level):
                nxt.append(jnp.where(bit, level[n + 1], level[n]))
            else:
                nxt.append(level[n])
        level = nxt
    return level[0]


def row_bits(index, count):
    return [(index & (LANES << i)) != 0 for i in range(count)]


def table_gather(table_rows, index):
    lane = index & (LANES - 1)
    bits = row_bits(index, max(len(table_rows) - 1, 1).bit_length())
    return tree_select([lane_gather(row, lane) for row in table_rows], bits)


def run_copies(copies):
    for copy in copies:
        copy.start()
    for copy in copies:
        copy.wait()


def of_blocks(ref, half, row, per_block):
    return ref[pl.ds(half * 8 * per_block + row, 8, stride=per_block), :]


def whole_copies(pairs, sem):
    return [pltpu.make_async_copy(src, dst, sem.at[n]) for n, (src, dst) in enumerate(pairs)]


def by_core(what, mine, other):
    first = lax.axis_index("dst") == 0
    pl.when(first)(lambda: what(mine, other))
    pl.when(jnp.logical_not(first))(lambda: what(other, mine))


def own_block(grid_x):
    return lax.axis_index("gy") * grid_x + lax.axis_index("gx")


def renumbered(segment, per_block, blocks, grid_x):
    grid_y = blocks // grid_x
    block, place = lax.div(segment, per_block), lax.rem(segment, per_block)
    return (lax.rem(block, grid_y) * grid_x + lax.div(block, grid_y)) * per_block + place


def padded_rows(rows):
    tiles = -(-rows // 8)
    return (tiles + 1 - tiles % 2) * 8


def target_mask(dest, half, chunk, per_block):
    sub = lax.broadcasted_iota(jnp.int32, (8, LANES), 0)
    lane = lax.broadcasted_iota(jnp.int32, (8, LANES), 1)
    return (half * 8 + sub) * per_block + chunk * LANES + lane == dest


def arrange_kernel(
    succ_any, valid_any, border_any, anchor_any, reward_ref, out_any,
    succ_ref, valid_ref, border_ref, anchor_ref, split_ref, out_ref, count_ref, first_ref, order_ref, inverse_ref, placed_ref,
    pair_ref, lane_ref, code_ref, column_ref, acc_ref, sem
):
    run_copies(
        whole_copies(
            [
                (succ_any, succ_ref),
                (valid_any, valid_ref),
                (border_any, border_ref),
                (anchor_any, anchor_ref),
            ],
            sem,
        )
    )
    turns, width = succ_ref.shape
    chunks = width // LANES
    slots = chunks + 4
    step = 2 * LANES
    tops = 16
    square = (LANES, LANES)
    down = lax.broadcasted_iota(jnp.int32, square, 0)
    along = lax.broadcasted_iota(jnp.int32, square, 1)
    down_f, along_f = down.astype(jnp.float32), along.astype(jnp.float32)
    before = down < along
    unit = jnp.where(down == along, 1.0, 0.0)
    lane_row = lax.broadcasted_iota(jnp.int32, (LANES, step), 0)
    top_row = lax.broadcasted_iota(jnp.int32, (tops, step), 0)
    rank_row = lax.broadcasted_iota(jnp.int32, (RANKS, step), 0).astype(jnp.float32)
    last_dims = (((1,), (1,)), ((), ()))

    def product(left, right):
        return lax.dot_general(left, right, last_dims, preferred_element_type=jnp.float32)

    def columns(rows):
        return lax.dot_general(
            unit, rows, last_dims, precision=lax.Precision.HIGHEST, preferred_element_type=jnp.float32
        )

    def summed_down(array):
        return jnp.sum(array, axis=0, keepdims=True)

    def place_of(row, col):
        return summed_down(jnp.where((col > row) | ((col == row) & before), 1.0, 0.0))

    def count(a, total):
        for c in range(width // step):
            cols = slice(c * step, (c + 1) * step)
            u = succ_ref[pl.ds(a, 1), cols]
            low = jnp.where(valid_ref[pl.ds(a, 1), cols] == 1, u & (LANES - 1), -1)
            hot_low = jnp.where(low == lane_row, 1.0, 0.0).astype(jnp.bfloat16)
            hot_top = jnp.where((u >> 7) == top_row, 1.0, 0.0).astype(jnp.bfloat16)
            total = total + product(hot_top, hot_low)
        return total

    counts = lax.fori_loop(0, turns, count, jnp.zeros((tops, LANES), jnp.float32), unroll=2)
    count_columns = columns(counts)
    out_ref[...] = jnp.zeros_like(out_ref)
    for ref in (count_ref, first_ref, order_ref, inverse_ref, placed_ref, pair_ref):
        ref[...] = jnp.zeros_like(ref)
    for n in range(slots):
        i = n if n < chunks else n - chunks
        place = place_of(counts[n : n + 1, :], count_columns[:, n : n + 1])
        place = place if i % 2 == 0 else (LANES - 1.0) - place
        if (i // 2) % 2:
            place = jnp.where(place >= LANES // 2, place - LANES // 2, place + LANES // 2)
        first_ref[n : n + 1, :] = place
    first_columns = columns(first_ref[...])
    for n in range(slots):
        hit = first_columns[:, n : n + 1] == along_f
        inverse_ref[n : n + 1, :] = summed_down(jnp.where(hit, down_f, 0.0))
        placed_ref[n : n + 1, :] = summed_down(jnp.where(hit, count_columns[:, n : n + 1], 0.0))
    local = summed_down(placed_ref[0:chunks, :])
    room = -summed_down(placed_ref[chunks:tops, :])
    pair_ref[0:1, :] = local
    pair_ref[1:2, :] = room
    pair = columns(pair_ref[...])
    local_place, room_place = place_of(local, pair[:, 0:1]), place_of(room, pair[:, 1:2])
    pair_ref[0:1, :] = local_place
    pair_ref[1:2, :] = room_place
    pair = columns(pair_ref[...])
    goes = summed_down(jnp.where(pair[:, 1:2] == local_place, down_f, 0.0))
    comes = summed_down(jnp.where(pair[:, 0:1] == room_place, down_f, 0.0))
    full = (chunks, LANES)
    comes = jnp.broadcast_to(comes, full).astype(jnp.int32)
    goes = jnp.broadcast_to(goes, full)
    order_ref[0:chunks, :] = lane_gather(goes, first_ref[0:chunks, :].astype(jnp.int32))
    order_ref[chunks:tops, :] = first_ref[chunks:tops, :]
    inverse_ref[0:chunks, :] = lane_gather(inverse_ref[0:chunks, :], comes)
    placed_ref[0:chunks, :] = lane_gather(placed_ref[0:chunks, :], comes)
    running = jnp.zeros((1, LANES), jnp.float32)
    for n in range(slots):
        count_ref[n : n + 1, :] = running
        running = running + placed_ref[n : n + 1, :]
        out_ref[ROWS + n : ROWS + n + 1, :] = running
        out_ref[ROWS + slots + n : ROWS + slots + n + 1, :] = order_ref[n : n + 1, :]
        out_ref[ROWS + 2 * slots + n : ROWS + 2 * slots + n + 1, :] = inverse_ref[n : n + 1, :]
    for k in range(chunks):
        cols = slice(k * LANES, (k + 1) * LANES)
        u = succ_ref[:, cols]
        rows = [jnp.broadcast_to(order_ref[n : n + 1, :], (turns, LANES)) for n in range(slots)]
        lane = jnp.where(valid_ref[:, cols] == 1, table_gather(rows, u), -1.0)
        code = jnp.where(lane >= 0.0, lane + ((u >> 7) * LANES).astype(jnp.float32), -1.0)
        lane_ref[:, cols] = lane
        code_ref[:, cols] = code
        column_ref[cols, :] = columns(code)
    acc_ref[...] = jnp.zeros_like(acc_ref)
    earlier = jnp.where(
        lax.broadcasted_iota(jnp.int32, (step, step), 0) < lax.broadcasted_iota(jnp.int32, (step, step), 1),
        1.0,
        0.0,
    )
    lane_row_f = lane_row.astype(jnp.float32)

    def one_chunk(c, base):
        start = pl.multiple_of(c * step, step)
        cols = pl.ds(start, step)
        s = start + lax.broadcasted_iota(jnp.int32, (1, step), 1)
        source = [
            (s & ~7).astype(jnp.float32).astype(jnp.bfloat16),
            (s & 7).astype(jnp.float32).astype(jnp.bfloat16),
        ]
        for a in range(turns):
            row = slice(a, a + 1)
            hot = jnp.where(lane_ref[row, cols] == lane_row_f, 1.0, 0.0).astype(jnp.bfloat16)
            hot_top = jnp.where((succ_ref[row, cols] >> 7) == top_row, 1.0, 0.0)
            same = column_ref[cols, row] == code_ref[row, cols]
            within = summed_down(jnp.where(same, earlier, 0.0))
            coarse = (base.astype(jnp.int32) & ~127).astype(jnp.float32)
            both = jnp.concatenate([coarse, base - coarse], axis=0).astype(jnp.bfloat16)
            starts = jnp.dot(both, hot, preferred_element_type=jnp.float32)
            begin = summed_down((starts[:tops] + starts[tops:]) * hot_top)
            base = base + product(hot_top.astype(jnp.bfloat16), hot)
            match = jnp.where(begin + within == rank_row, 1.0, 0.0).astype(jnp.bfloat16)
            r = reward_ref[row, cols]
            r1 = r.astype(jnp.bfloat16)
            rest = r - r1.astype(jnp.float32)
            r2 = rest.astype(jnp.bfloat16)
            r3 = (rest - r2.astype(jnp.float32)).astype(jnp.bfloat16)
            left = jnp.concatenate([match * piece for piece in (*source, r1, r2, r3)], axis=0)
            acc_ref[...] += product(left, hot)
        return base

    lax.fori_loop(0, width // step, one_chunk, count_ref[...])
    part = [acc_ref[i * RANKS : i * RANKS + ROWS, :] for i in range(5)]
    share = out_ref.shape[0] // 2
    out_ref[0:ROWS, :] = part[0] + part[1]
    out_ref[share : share + ROWS, :] = (part[2] + part[3]) + part[4]
    listed = columns(border_ref[...].astype(jnp.float32)).astype(jnp.int32)
    for side in range(4):
        for q in range(chunks):
            found = jnp.where(listed[:, side : side + 1] == along + q * LANES, down_f + 1.0, 0.0)
            row = share + ROWS + side * chunks + q
            out_ref[row : row + 1, :] = summed_down(found)
    blocks = anchor_ref.shape[0]
    for q in range(chunks):
        split_ref[pl.ds(q, blocks, chunks), :] = anchor_ref[:, q * LANES : (q + 1) * LANES]
    half = out_ref.at[pl.ds(pl.multiple_of(lax.axis_index("dst") * share, 8), share)]
    size = share + chunks
    pairs = []
    for b in range(blocks):
        pairs.append((half, out_any.at[pl.ds(b * size, share)]))
        pairs.append((split_ref.at[pl.ds(b * chunks, chunks)], out_any.at[pl.ds(b * size + share, chunks)]))
    run_copies(whole_copies(pairs, sem))


def graph_kernel(
    weight_ref, feature_any, succ_any, valid_any, border_any, out_ref, reward_ref,
    feature_ref, succ_ref, valid_ref, border_ref, part_ref, sem
):
    run_copies(
        whole_copies(
            [
                (feature_any, feature_ref),
                (succ_any, succ_ref),
                (valid_any, valid_ref),
                (border_any, border_ref),
            ],
            sem,
        )
    )
    turns, width = succ_ref.shape
    chunks = width // LANES
    edges = turns * chunks
    part_ref[edges : edges + 8, :] = jnp.zeros((8, LANES), jnp.float32)
    part_ref[edges : edges + 4, :] = border_ref[...].astype(jnp.float32)
    first_core = lax.axis_index("dst") == 0
    for q in range(chunks):
        cols = slice(q * LANES, (q + 1) * LANES)
        cost = weight_ref[0] * feature_ref[0, :, cols].astype(jnp.float32)
        for f in range(1, feature_ref.shape[0]):
            cost = cost + weight_ref[f] * feature_ref[f, :, cols].astype(jnp.float32)
        reward_ref[:, cols] = -cost
        masked = jnp.where(valid_ref[:, cols] == 1, -cost, NEG)
        turn_to = succ_ref[:, cols].astype(jnp.float32)
        part_ref[pl.ds(q, turns, chunks), :] = jnp.where(first_core, masked, turn_to)
    common = part_ref.shape[0]
    for b in range(out_ref.shape[0] // common):
        out_ref[b * common : (b + 1) * common, :] = part_ref[...]


def regroup_kernel(pieces_ref, out_ref):
    halves, rows = out_ref.shape[:2]
    size = pieces_ref.shape[0] // (8 * halves)
    for h in range(halves):

        def one_row(i, carry, h=h):
            out_ref[h, i] = of_blocks(pieces_ref, h, i, size)
            return carry

        lax.fori_loop(0, rows, one_row, 0, unroll=8)


def value_kernel(
    grid_x, dest_ref, mine_ref, other_ref, ext_ref, raised_ref, max_ref, inv_ref,
    reward, index, border, side_pad, spare_ref
):
    halves = ext_ref.shape[0]
    blocks = 8 * halves
    chunks = ext_ref.shape[1] - 4
    turns = raised_ref.shape[1] // chunks
    edges = turns * chunks
    per_block = chunks * LANES
    dest = renumbered(dest_ref[own_block(grid_x)], per_block, blocks, grid_x)
    side_pad[...] = jnp.zeros_like(side_pad)
    sub = lax.broadcasted_iota(jnp.int32, (8, LANES), 0)
    lane = lax.broadcasted_iota(jnp.int32, (8, LANES), 1)
    dest_block, dest_place = lax.div(dest, per_block), lax.rem(dest, per_block)

    def unpack(first, second):
        for h in range(halves):

            def rows(i, carry, h=h):
                reward[h, i] = first[h, i]
                index[h, i] = second[h, i].astype(jnp.int32)
                return carry

            lax.fori_loop(0, edges, rows, 0, unroll=8)
            for side in range(4):
                border[h, side] = first[h, edges + side].astype(jnp.int32)

    by_core(unpack, mine_ref, other_ref)
    for h in range(halves):
        for side in range(4):
            found = (border[h, side] == dest_place) & (h * 8 + sub == dest_block)
            entry = jnp.max(jnp.where(found, lane + 1, 0).astype(jnp.float32), axis=1, keepdims=True)
            side_pad[side, 8 + 8 * h : 16 + 8 * h, :] = jnp.broadcast_to(entry, (8, LANES))
    shifts = ((1, -1), (0, 1), (3, -grid_x), (2, grid_x))

    def shown(h, side):
        facing, by = shifts[side]
        start = 8 + 8 * h + by
        return side_pad[facing, start : start + 8, :]

    def dest_index(h):
        where = jnp.where(h * 8 + sub == dest_block, dest_place, -1)
        for side in range(4):
            entry = shown(h, side).astype(jnp.int32)
            where = jnp.where(entry > 0, per_block + side * LANES + entry - 1, where)
        return where

    def bring_halo(values):
        for h in range(halves):
            table = [values[h, q] for q in range(chunks)]
            for side in range(4):
                side_pad[side, 8 + 8 * h : 16 + 8 * h, :] = table_gather(table, border[h, side])
        for h in range(halves):
            for side in range(4):
                values[h, chunks + side] = shown(h, side)

    def summed(out):
        top = functools.reduce(jnp.maximum, out)
        raised = [jnp.exp(score - top) for score in out]
        return top, raised, functools.reduce(jnp.add, raised)

    def scores_of(values, h, q):
        tables = [values[h, r] for r in range(chunks + 4)]
        out = []
        for a in range(turns):
            rows = tables if a else tables[:chunks]
            out.append(reward[h, a * chunks + q] + table_gather(rows, index[h, a * chunks + q]))
        return summed(out)

    def store_value(h, q, top, total, into):
        value = top + jnp.log(total)
        into[h, q] = jnp.where(target_mask(dest, h, q, per_block), 0.0, value)

    wanted = [dest_index(h) for h in range(halves)]

    def first_chunk(q, inner):
        for h in range(halves):
            out = []
            for a in range(turns):
                before = jnp.where(index[h, a * chunks + q] == wanted[h], 0.0, -START_COST)
                out.append(reward[h, a * chunks + q] + before)
            top, _, total = summed(out)
            store_value(h, q, top, total, spare_ref)
        return inner

    lax.fori_loop(0, chunks, first_chunk, 0, unroll=2)

    def backup(values, into):
        bring_halo(values)

        def one_chunk(q, inner):
            for h in range(halves):
                top, _, total = scores_of(values, h, q)
                store_value(h, q, top, total, into)
            return inner

        lax.fori_loop(0, chunks, one_chunk, 0, unroll=chunks)

    def two_backups(step, carry):
        backup(spare_ref, ext_ref)
        backup(ext_ref, spare_ref)
        return carry

    lax.fori_loop(0, (HORIZON - 2) // 2, two_backups, 0)
    backup(spare_ref, ext_ref)
    bring_halo(ext_ref)

    def last_chunk(q, inner):
        for h in range(halves):
            top, raised, total = scores_of(ext_ref, h, q)
            max_ref[h, q] = top
            inv_ref[h, q] = 1.0 / total
            for a in range(turns):
                raised_ref[h, a * chunks + q] = raised[a]
        return inner

    lax.fori_loop(0, chunks, last_chunk, 0, unroll=chunks)


def push_kernel(
    grid_x, scale, dest_ref, mine_ref, other_ref, graph_mine, graph_other, ext_ref, raised_ref, max_ref,
    inv_ref, keep_ref, send_ref, counts, ends, order, values, source, slot, going, policy, flows, back, scaled, total, arrived, side_pad, raw
):
    halves = ext_ref.shape[0]
    blocks = 8 * halves
    share = mine_ref.shape[1]
    chunks = max_ref.shape[1]
    edges = raised_ref.shape[1]
    turns = edges // chunks
    per_block = chunks * LANES
    slots = chunks + 4
    dest = renumbered(dest_ref[own_block(grid_x)], per_block, blocks, grid_x)
    core = lax.axis_index("dst")
    side_pad[...] = jnp.zeros_like(side_pad)

    def unpack(first, second):
        for h in range(halves):
            for n in range(slots):
                ends[h, n] = first[h, ROWS + n]
                order[h, n] = first[h, ROWS + slots + n].astype(jnp.int32)
                inverse = first[h, ROWS + 2 * slots + n].astype(jnp.int32)
                values[h, n] = lane_gather(ext_ref[h, n], inverse)

            def rows(r, carry, h=h):
                source[h, r] = first[h, r].astype(jnp.int32)
                policy[h, r] = second[h, r]
                return carry

            lax.fori_loop(0, ROWS, rows, 0, unroll=6)
            for r in range(ROWS, DEPTH):
                source[h, r] = jnp.zeros((8, LANES), jnp.int32)
                policy[h, r] = jnp.zeros((8, LANES), jnp.float32)
            for n in range(4 * chunks):
                back[h, n] = second[h, ROWS + n].astype(jnp.int32) - 1

    by_core(unpack, mine_ref, other_ref)
    deepest = jnp.max(functools.reduce(jnp.maximum, [ends[h, slots - 1] for h in range(halves)]))
    deepest = deepest.astype(jnp.int32)
    fits = deepest <= ROWS
    steps = jnp.where(deepest <= USUAL, USUAL // STEP, DEPTH // STEP)
    shifts = ((1, -1), (0, 1), (3, -grid_x), (2, grid_x))

    def shown(h, side):
        facing, by = shifts[side]
        start = 8 + 8 * h + by
        return side_pad[facing, start : start + 8, :]

    @pl.when(jnp.logical_not(fits))
    def _():
        for h in range(halves):
            for n in range(slots):
                order[h, n] = lax.broadcasted_iota(jnp.int32, (8, LANES), 1)

    for h in range(halves):
        for side in range(4):
            side_pad[side, 8 + 8 * h : 16 + 8 * h, :] = order[h, chunks + side].astype(jnp.float32)
    for h in range(halves):
        for side in range(4):
            lanes = shown(h, side).astype(jnp.int32)
            for q in range(chunks):
                entry = back[h, side * chunks + q]
                back[h, side * chunks + q] = jnp.where(
                    entry >= 0, lane_gather(lanes, jnp.maximum(entry, 0)), -1
                )

    def prepare(t, carry):
        row_before = [None] * halves
        for i in range(STEP):
            for h in range(halves):
                r = t * STEP + i
                src = source[h, r]
                place = r.astype(jnp.float32)
                row = functools.reduce(
                    jnp.add, [jnp.where(ends[h, n] <= place, 1, 0) for n in range(slots)]
                )
                slot[h, r] = row
                if i:
                    going[h, r] = jnp.where(row == row_before[h], 1.0, 0.0)
                row_before[h] = row
                bits = [(row & (1 << n)) != 0 for n in range(4)]
                picked = tree_select([values[h, n] for n in range(slots)], bits)
                top = table_gather([max_ref[h, q] for q in range(chunks)], src)
                policy[h, r] = jnp.exp(policy[h, r] + picked - top)
        return carry

    lax.fori_loop(0, steps, prepare, 0)
    usual = deepest <= USUAL

    @pl.when(usual)
    def _():
        for h in range(halves):
            for r in range(STEP, USUAL, STEP):
                going[h, r] = jnp.where(slot[h, r] == slot[h, r - 1], 1.0, 0.0)

    for h in range(halves):
        for q in range(chunks):
            own = mine_ref[h, share - chunks + q]
            first = jnp.where(target_mask(dest, h, q, per_block), 0.0, own)
            total[h, q] = first
            scaled[h, q] = first * inv_ref[h, q]

    @pl.when(jnp.logical_not(fits))
    def _():
        def keep_turns(first, second):
            for h in range(halves):

                def rows(e, carry, h=h):
                    raw[h, e] = second[h, e].astype(jnp.int32)
                    return carry

                lax.fori_loop(0, edges, rows, 0)

        by_core(keep_turns, graph_mine, graph_other)

    zero = jnp.zeros((8, LANES), jnp.float32)

    def keep(h):
        for side in range(4):
            side_pad[side, 8 + 8 * h : 16 + 8 * h, :] = arrived[h, chunks + side]

    def add_flow(acc, row, flow):
        return [acc[n] + jnp.where(row == n, flow, 0.0) for n in range(slots)]

    def sum_arranged():
        for h in range(halves):
            for n in range(slots):
                arrived[h, n] = zero

        def one_step(t, carry):
            tables = [[scaled[h, q] for q in range(chunks)] for h in range(halves)]
            step_sums = [[zero] * slots for h in range(halves)]
            so_far = [None] * halves
            for i in range(STEP):
                r = t * STEP + i
                for h in range(halves):
                    flow = table_gather(tables[h], source[h, r]) * policy[h, r]
                    so_far[h] = flow + going[h, r] * so_far[h] if i else flow
                    row = slot[h, r]
                    step_sums[h] = [jnp.where(row == n, so_far[h], step_sums[h][n]) for n in range(slots)]
            for h in range(halves):
                for n in range(slots):
                    arrived[h, n] = arrived[h, n] + step_sums[h][n]
            return carry

        def usual_rows():
            for h in range(halves):
                table = [scaled[h, q] for q in range(chunks)]
                for r in range(USUAL):
                    flow = table_gather(table, source[h, r]) * policy[h, r]
                    so_far = flow + going[h, r] * so_far if r else flow
                    flows[h, r] = so_far
            for h in range(halves):
                sums = [zero] * slots
                for r in range(USUAL):
                    row, so_far = slot[h, r], flows[h, r]
                    sums = [jnp.where(row == n, so_far, sums[n]) for n in range(slots)]
                for n in range(slots):
                    arrived[h, n] = sums[n]

        pl.when(usual)(usual_rows)
        lax.fori_loop(0, jnp.where(usual, 0, steps), one_step, 0)
        for h in range(halves):
            keep(h)

    def sum_turned():
        lane = lax.broadcasted_iota(jnp.int32, (8, LANES), 1)
        for h in range(halves):

            def one_edge_row(e, acc, h=h):
                flow = scaled[h, lax.rem(e, chunks)] * raised_ref[h, e]
                where = raw[h, e]

                def one_turn(k, state):
                    flow, where, acc = state[0], state[1], list(state[2:])
                    here = jnp.where((where & (LANES - 1)) == lane, where >> 7, -1)
                    acc = add_flow(acc, here, flow)
                    return (pltpu.roll(flow, 1, 1), pltpu.roll(where, 1, 1), *acc)

                return tuple(lax.fori_loop(0, LANES, one_turn, (flow, where, *acc))[2:])

            for n, value in enumerate(lax.fori_loop(0, edges, one_edge_row, (zero,) * slots)):
                arrived[h, n] = value
            keep(h)

    def push(round_index, carry):
        pl.when(fits)(sum_arranged)
        pl.when(jnp.logical_not(fits))(sum_turned)
        for h in range(halves):
            landed = [shown(h, side) for side in range(4)]
            for q in range(chunks):
                value = lane_gather(arrived[h, q], order[h, q])
                for side in range(4):
                    entry = back[h, side * chunks + q]
                    got = lane_gather(landed[side], jnp.maximum(entry, 0))
                    value = value + jnp.where(entry >= 0, got, 0.0)
                value = jnp.where(target_mask(dest, h, q, per_block), 0.0, value)
                total[h, q] = total[h, q] + value
                scaled[h, q] = value * inv_ref[h, q]
        return carry

    lax.fori_loop(0, HORIZON - 1, push, 0)
    rows_out = edges // 2
    apart = counts.shape[1] // blocks
    for h in range(halves):
        for q in range(chunks):
            weight = total[h, q] * inv_ref[h, q] * scale
            for part, piece in ((core, 0), (1 - core, 1)):
                for a in range(turns // 2):
                    value = weight * raised_ref[h, (part * (turns // 2) + a) * chunks + q]
                    start = h * 8 * apart + a * chunks + q
                    counts[piece, pl.ds(start, 8, stride=apart), :] = value
    for piece, out_ref in ((0, keep_ref), (1, send_ref)):
        for b in range(blocks):
            out_ref[b * rows_out : (b + 1) * rows_out, :] = counts[
                piece, b * apart : b * apart + rows_out, :
            ]


VMEM_SPEC = pl.BlockSpec(memory_space=pltpu.VMEM)
SMEM_SPEC = pl.BlockSpec(memory_space=pltpu.SMEM)
HBM_SPEC = pl.BlockSpec(memory_space=pltpu.HBM)
PARAMS = pltpu.CompilerParams(vmem_limit_bytes=48 * 1024 * 1024)


def f32(*shape):
    return jax.ShapeDtypeStruct(shape, jnp.float32)


def call_graph(cost_weights, features, successors, turn_valid, border_lists, blocks):
    turns, width = successors.shape
    chunks = width // LANES
    rows = turns * chunks + 8
    return pl.pallas_call(
        graph_kernel,
        out_shape=(f32(blocks * rows, LANES), f32(turns, width)),
        in_specs=[SMEM_SPEC] + [HBM_SPEC] * 4,
        out_specs=(VMEM_SPEC, VMEM_SPEC),
        scratch_shapes=[
            pltpu.VMEM(features.shape, features.dtype),
            pltpu.VMEM(successors.shape, jnp.int32),
            pltpu.VMEM(turn_valid.shape, jnp.int32),
            pltpu.VMEM(border_lists.shape, jnp.int32),
            pltpu.VMEM((rows, LANES), jnp.float32),
            pltpu.SemaphoreType.DMA((4,)),
        ],
        compiler_params=pltpu.CompilerParams(vmem_limit_bytes=63 * 1024 * 1024),
        name="own_graph",
    )(cost_weights, features, successors, turn_valid, border_lists)


def arranged_rows(chunks):
    most = ROWS + max(3 * (chunks + 4), 4 * chunks)
    return -(-most // 8) * 8


def call_arrange(successors, turn_valid, border_lists, anchors, reward):
    chunks = successors.shape[1] // LANES
    share = arranged_rows(chunks)
    blocks = anchors.shape[0]
    return pl.pallas_call(
        arrange_kernel,
        out_shape=f32(blocks * (share + chunks), LANES),
        in_specs=[HBM_SPEC] * 4 + [VMEM_SPEC],
        out_specs=HBM_SPEC,
        scratch_shapes=[
            pltpu.VMEM(successors.shape, jnp.int32),
            pltpu.VMEM(turn_valid.shape, jnp.int32),
            pltpu.VMEM(border_lists.shape, jnp.int32),
            pltpu.VMEM(anchors.shape, jnp.float32),
            pltpu.VMEM((blocks * chunks, LANES), jnp.float32),
            pltpu.VMEM((2 * share, LANES), jnp.float32),
            *[pltpu.VMEM((16, LANES), jnp.float32)] * 5,
            pltpu.VMEM((8, LANES), jnp.float32),
            pltpu.VMEM(successors.shape, jnp.float32),
            pltpu.VMEM(successors.shape, jnp.float32),
            pltpu.VMEM(successors.shape[::-1], jnp.float32),
            pltpu.VMEM((5 * RANKS, LANES), jnp.float32),
            pltpu.SemaphoreType.DMA((2 * blocks,)),
        ],
        compiler_params=PARAMS,
        cost_estimate=pl.CostEstimate(flops=4_000_000_000, bytes_accessed=400_000, transcendentals=0),
        name="arrange_turns",
    )(successors, turn_valid, border_lists, anchors, reward)


def call_regroup(pieces, blocks):
    return pl.pallas_call(
        regroup_kernel,
        out_shape=f32(blocks // 8, pieces.shape[0] // blocks, 8, LANES),
        in_specs=[VMEM_SPEC],
        out_specs=VMEM_SPEC,
        compiler_params=PARAMS,
        name="regroup",
    )(pieces)


def call_values(destinations, mine, other, blocks, grid_x, turns, chunks):
    halves = blocks // 8
    edges = turns * chunks
    return pl.pallas_call(
        functools.partial(value_kernel, grid_x),
        out_shape=(
            f32(halves, chunks + 4, 8, LANES),
            f32(halves, edges, 8, LANES),
            f32(halves, chunks, 8, LANES),
            f32(halves, chunks, 8, LANES),
        ),
        in_specs=[SMEM_SPEC, VMEM_SPEC, VMEM_SPEC],
        out_specs=(VMEM_SPEC,) * 4,
        scratch_shapes=[
            pltpu.VMEM((halves, edges, 8, LANES), jnp.float32),
            pltpu.VMEM((halves, edges, 8, LANES), jnp.int32),
            pltpu.VMEM((halves, 4, 8, LANES), jnp.int32),
            pltpu.VMEM((4, blocks + 16, LANES), jnp.float32),
            pltpu.VMEM((halves, chunks + 4, 8, LANES), jnp.float32),
        ],
        compiler_params=PARAMS,
        cost_estimate=pl.CostEstimate(flops=40_000_000, bytes_accessed=40_000_000, transcendentals=2_000_000),
        name="soft_values",
    )(destinations, mine, other)


def call_push(destinations, mine, other, graph_mine, graph_other, ext, raised, top, inv, grid_x, scale):
    halves, edges = raised.shape[:2]
    blocks = 8 * halves
    chunks = top.shape[1]

    def vmem(rows, dtype=jnp.float32):
        return pltpu.VMEM((halves, rows, 8, LANES), dtype)

    return pl.pallas_call(
        functools.partial(push_kernel, grid_x, scale),
        out_shape=(f32(blocks * edges // 2, LANES),) * 2,
        in_specs=[SMEM_SPEC] + [VMEM_SPEC] * 8,
        out_specs=(VMEM_SPEC,) * 2,
        scratch_shapes=[
            pltpu.VMEM((2, blocks * padded_rows(edges // 2), LANES), jnp.float32),
            vmem(chunks + 4),
            vmem(chunks + 4, jnp.int32),
            vmem(chunks + 4),
            vmem(DEPTH, jnp.int32),
            vmem(DEPTH, jnp.int32),
            vmem(DEPTH),
            vmem(DEPTH),
            vmem(USUAL),
            vmem(4 * chunks, jnp.int32),
            vmem(chunks),
            vmem(chunks),
            vmem(chunks + 4),
            pltpu.VMEM((4, blocks + 16, LANES), jnp.float32),
            vmem(edges, jnp.int32),
        ],
        compiler_params=PARAMS,
        name="push_mass",
    )(destinations, mine, other, graph_mine, graph_other, ext, raised, top, inv)


def to_blocks(array):
    return lax.all_to_all(array, BLOCK_AXES, 0, 0, tiled=True)


def other_core(array):
    return lax.ppermute(array, "dst", [(0, 1), (1, 0)])


def per_destination(
    features, cost_weights, successors, turn_valid, border_lists, destinations, anchors, demo_counts
):
    turns, own_count = successors.shape
    chunks = own_count // LANES
    edges = turns * chunks
    grid_x = lax.axis_size("gx")
    blocks = lax.axis_size("gy") * grid_x
    groups = lax.axis_size("dst")
    pieces, reward = call_graph(cost_weights, features, successors, turn_valid, border_lists, blocks)
    graph = to_blocks(pieces)
    arranged = call_arrange(successors, turn_valid, border_lists, anchors, reward)
    core = lax.axis_index("dst")
    demo_term = jnp.where(turn_valid == 1, demo_counts, 0).astype(jnp.float32) / 3.0
    own_feats = lax.dynamic_slice_in_dim(features, core * (turns // 2), turns // 2, axis=1)
    first_core, own_feats, demo_term, arranged = lax.optimization_barrier(
        (core == 0, own_feats, demo_term, arranged)
    )
    graph = lax.optimization_barrier((graph, arranged))[0]
    arranged = to_blocks(arranged)
    graph = call_regroup(graph, blocks)
    graph = (graph, other_core(graph))
    values = call_values(destinations, *graph, blocks, grid_x, turns, chunks)
    arranged, *values = lax.optimization_barrier((arranged, *values))
    arranged = call_regroup(arranged, blocks)
    arranged = (arranged, other_core(arranged))
    scale = 1.0 / (anchors.shape[0] * groups * HORIZON)
    kept, sent = call_push(destinations, *arranged, *graph, *values, grid_x, scale)
    halved = (kept + other_core(sent)).reshape(blocks, edges // 2, LANES)
    half = jnp.sum(to_blocks(halved), axis=0)
    other = other_core(half)
    part = (turns // 2, own_count)
    own_gap = lax.dynamic_slice_in_dim(demo_term, core * part[0], part[0]) - half.reshape(part)
    own_feats = own_feats.astype(jnp.float32)
    block_term = jnp.sum(own_gap[None] * own_feats, axis=(1, 2)) / (own_count * blocks)
    visits = jnp.concatenate([jnp.where(first_core, half, other), jnp.where(first_core, other, half)])
    count_gap = demo_term - visits.reshape(turns, own_count)
    terms = jnp.broadcast_to(block_term, (groups * blocks, 1, block_term.shape[0]))
    terms = lax.all_to_all(terms, (*BLOCK_AXES, "dst"), 0, 0, tiled=True)
    terms, count_gap = lax.optimization_barrier((terms, count_gap))
    return count_gap, jnp.sum(terms, axis=(0, 1))


def passed_along(array, axis, by):
    length = lax.axis_size(axis)
    pairs = [(i, i + by) for i in range(length) if 0 <= i + by < length]
    return lax.ppermute(array, axis, pairs)


def bring_values(values, border_lists):
    outgoing = values[:, border_lists]
    north_part = passed_along(outgoing[:, 1], "gx", 1)
    south_part = passed_along(outgoing[:, 0], "gx", -1)
    west_part = passed_along(outgoing[:, 3], "gy", 1)
    east_part = passed_along(outgoing[:, 2], "gy", -1)
    return jnp.concatenate([north_part, south_part, west_part, east_part], axis=1)


def return_flow(arrived, border_lists, own_count, border_width):
    local_part = arrived[:, :own_count]
    halo_part = arrived[:, own_count:].reshape(arrived.shape[0], 4, border_width)
    from_south = passed_along(halo_part[:, 0], "gx", -1)
    from_north = passed_along(halo_part[:, 1], "gx", 1)
    from_east = passed_along(halo_part[:, 2], "gy", -1)
    from_west = passed_along(halo_part[:, 3], "gy", 1)
    returned = jnp.stack([from_north, from_south, from_west, from_east], axis=1)
    return local_part.at[:, border_lists].add(returned)


def select_cells(cells, flat_index, turn_shape):
    picked = jnp.take(cells, flat_index, axis=1)
    return picked.reshape(cells.shape[0], turn_shape[0], turn_shape[1])


def turn_scores(values, halo_cells, reward, flat_turns, usable):
    extended = jnp.concatenate([values, halo_cells], axis=1)
    scores = reward[None] + select_cells(extended, flat_turns, usable.shape)
    return jnp.where(usable[None], scores, NEG)


def per_block(
    features, cost_weights, successors, turn_valid, border_lists, destinations, anchors, demo_counts
):
    own_count = successors.shape[1]
    border_width = border_lists.shape[1]
    dest_count = anchors.shape[0]
    slot_total = own_count + 4 * border_width
    block_index = lax.axis_index("gx") * lax.axis_size("gy") + lax.axis_index("gy")
    positions = jnp.arange(own_count, dtype=jnp.int32)
    is_target = positions[None, :] == (destinations - block_index * own_count)[:, None]
    usable = turn_valid == 1
    feats = features.astype(jnp.float32)
    reward = -jnp.sum(feats * cost_weights[:, None, None], axis=0)
    flat_turns = successors.reshape(-1)
    values = jnp.where(is_target, 0.0, -START_COST).astype(jnp.float32)
    for round_index in range(HORIZON):
        halo_cells = bring_values(values, border_lists)
        scores = turn_scores(values, halo_cells, reward, flat_turns, usable)
        row_max = jnp.max(scores, axis=1)
        new_values = row_max + jnp.log(jnp.sum(jnp.exp(scores - row_max[:, None]), axis=1))
        values = jnp.where(is_target, 0.0, new_values)
    halo_cells = bring_values(values, border_lists)
    scores = turn_scores(values, halo_cells, reward, flat_turns, usable)
    row_max = jnp.max(scores, axis=1)
    raised = jnp.exp(scores - row_max[:, None])
    policy = raised / jnp.sum(raised, axis=1, keepdims=True)
    mass_now = jnp.where(is_target, 0.0, anchors)
    turn_counts = jnp.zeros(successors.shape, jnp.float32)
    for round_index in range(HORIZON):
        turn_flow = mass_now[:, None, :] * policy
        turn_counts = turn_counts + jnp.sum(turn_flow, axis=0)
        if round_index + 1 < HORIZON:
            arrived = (
                jnp.zeros((dest_count, slot_total), jnp.float32)
                .at[:, flat_turns]
                .add(turn_flow.reshape(dest_count, -1))
            )
            landed = return_flow(arrived, border_lists, own_count, border_width)
            mass_now = jnp.where(is_target, 0.0, landed)
    local_visits = turn_counts / (dest_count * lax.axis_size("dst") * HORIZON)
    visits = lax.psum(local_visits, "dst")
    demo_term = jnp.where(usable, demo_counts, 0).astype(jnp.float32) / 3.0
    count_gap = demo_term - visits
    total_segments = own_count * lax.axis_size("gx") * lax.axis_size("gy")
    own_gap = demo_term / lax.axis_size("dst") - local_visits
    block_term = jnp.sum(own_gap[None] * feats, axis=(1, 2)) / total_segments
    gradient = lax.psum(block_term, ("gx", "gy", "dst"))
    return (count_gap, gradient)


def local(features, cost_weights, successors, turn_valid, border_lists, destinations, anchors, demo_counts):
    args = (
        features, cost_weights, successors, turn_valid, border_lists, destinations, anchors, demo_counts
    )
    blocks = lax.axis_size("gx") * lax.axis_size("gy")
    fits = (
        anchors.shape[0] == blocks
        and blocks % 8 == 0
        and lax.axis_size("dst") == 2
        and lax.axis_size("gx") in (2, 4, 8)
        and lax.axis_size("gy") in (2, 4, 8)
        and successors.shape[1] == 8 * LANES
        and border_lists.shape[1] == LANES
    )
    return per_destination(*args) if fits else per_block(*args)


def solution(mesh):
    in_specs = (
        P(None, None, ("gx", "gy")),
        P(),
        P(None, ("gx", "gy")),
        P(None, ("gx", "gy")),
        P(None, ("gx", "gy")),
        P("dst"),
        P("dst", ("gx", "gy")),
        P(None, ("gx", "gy")),
    )
    out_specs = (P(None, ("gx", "gy")), P())
    return jax.shard_map(local, mesh=mesh, in_specs=in_specs, out_specs=out_specs, check_vma=False)
```

```python
import functools

import jax
import jax.numpy as jnp
from jax import lax
from jax.experimental import pallas as pl
from jax.experimental.pallas import tpu as pltpu
from jax.sharding import PartitionSpec as P

HORIZON = 8
NEG = -1e30
START_COST = 100.0
LANES = 128
ROWS = 60
RANKS = -(-ROWS // 16) * 16
STEP = 14
USUAL = 56
DEPTH = -(-ROWS // STEP) * STEP
BLOCK_AXES = ("gy", "gx")

LANE_PICK = lax.GatherDimensionNumbers(
    offset_dims=(),
    collapsed_slice_dims=(1,),
    start_index_map=(1,),
    operand_batching_dims=(0,),
    start_indices_batching_dims=(0,),
)


def lane_gather(table, index):
    return lax.gather(
        table,
        index[..., None],
        LANE_PICK,
        (1, 1),
        mode=lax.GatherScatterMode.PROMISE_IN_BOUNDS,
    )


def tree_select(picked, bits):
    level = list(picked)
    for bit in bits:
        if len(level) == 1:
            break
        nxt = []
        for n in range(0, len(level), 2):
            if n + 1 < len(level):
                nxt.append(jnp.where(bit, level[n + 1], level[n]))
            else:
                nxt.append(level[n])
        level = nxt
    return level[0]


def row_bits(index, count):
    return [(index & (LANES << i)) != 0 for i in range(count)]


def table_gather(table_rows, index):
    lane = index & (LANES - 1)
    bits = row_bits(index, max(len(table_rows) - 1, 1).bit_length())
    return tree_select([lane_gather(row, lane) for row in table_rows], bits)


def run_copies(copies):
    for copy in copies:
        copy.start()
    for copy in copies:
        copy.wait()


def of_blocks(ref, half, row, per_block):
    return ref[pl.ds(half * 8 * per_block + row, 8, stride=per_block), :]


def whole_copies(pairs, sem):
    return [pltpu.make_async_copy(src, dst, sem.at[n]) for n, (src, dst) in enumerate(pairs)]


def by_core(what, mine, other):
    first = lax.axis_index("dst") == 0
    pl.when(first)(lambda: what(mine, other))
    pl.when(jnp.logical_not(first))(lambda: what(other, mine))


def own_block(grid_x):
    return lax.axis_index("gy") * grid_x + lax.axis_index("gx")


def renumbered(segment, per_block, blocks, grid_x):
    grid_y = blocks // grid_x
    block, place = lax.div(segment, per_block), lax.rem(segment, per_block)
    return (lax.rem(block, grid_y) * grid_x + lax.div(block, grid_y)) * per_block + place


def padded_rows(rows):
    tiles = -(-rows // 8)
    return (tiles + 1 - tiles % 2) * 8


def target_mask(dest, half, chunk, per_block):
    sub = lax.broadcasted_iota(jnp.int32, (8, LANES), 0)
    lane = lax.broadcasted_iota(jnp.int32, (8, LANES), 1)
    return (half * 8 + sub) * per_block + chunk * LANES + lane == dest


def arrange_kernel(
    succ_any, valid_any, border_any, anchor_any, reward_ref, out_any,
    succ_ref, valid_ref, border_ref, anchor_ref, split_ref, out_ref, count_ref, first_ref, order_ref, inverse_ref, placed_ref,
    pair_ref, lane_ref, code_ref, column_ref, acc_ref, sem
):
    run_copies(
        whole_copies(
            [
                (succ_any, succ_ref),
                (valid_any, valid_ref),
                (border_any, border_ref),
                (anchor_any, anchor_ref),
            ],
            sem,
        )
    )
    turns, width = succ_ref.shape
    chunks = width // LANES
    slots = chunks + 4
    step = 2 * LANES
    tops = 16
    square = (LANES, LANES)
    down = lax.broadcasted_iota(jnp.int32, square, 0)
    along = lax.broadcasted_iota(jnp.int32, square, 1)
    down_f, along_f = down.astype(jnp.float32), along.astype(jnp.float32)
    before = down < along
    unit = jnp.where(down == along, 1.0, 0.0)
    lane_row = lax.broadcasted_iota(jnp.int32, (LANES, step), 0)
    top_row = lax.broadcasted_iota(jnp.int32, (tops, step), 0)
    rank_row = lax.broadcasted_iota(jnp.int32, (RANKS, step), 0).astype(jnp.float32)
    last_dims = (((1,), (1,)), ((), ()))

    def product(left, right):
        return lax.dot_general(left, right, last_dims, preferred_element_type=jnp.float32)

    def columns(rows):
        return lax.dot_general(
            unit, rows, last_dims, precision=lax.Precision.HIGHEST, preferred_element_type=jnp.float32
        )

    def summed_down(array):
        return jnp.sum(array, axis=0, keepdims=True)

    def place_of(row, col):
        return summed_down(jnp.where((col > row) | ((col == row) & before), 1.0, 0.0))

    def count(a, total):
        for c in range(width // step):
            cols = slice(c * step, (c + 1) * step)
            u = succ_ref[pl.ds(a, 1), cols]
            low = jnp.where(valid_ref[pl.ds(a, 1), cols] == 1, u & (LANES - 1), -1)
            hot_low = jnp.where(low == lane_row, 1.0, 0.0).astype(jnp.bfloat16)
            hot_top = jnp.where((u >> 7) == top_row, 1.0, 0.0).astype(jnp.bfloat16)
            total = total + product(hot_top, hot_low)
        return total

    counts = lax.fori_loop(0, turns, count, jnp.zeros((tops, LANES), jnp.float32), unroll=2)
    count_columns = columns(counts)
    out_ref[...] = jnp.zeros_like(out_ref)
    for ref in (count_ref, first_ref, order_ref, inverse_ref, placed_ref, pair_ref):
        ref[...] = jnp.zeros_like(ref)
    for n in range(slots):
        i = n if n < chunks else n - chunks
        place = place_of(counts[n : n + 1, :], count_columns[:, n : n + 1])
        place = place if i % 2 == 0 else (LANES - 1.0) - place
        if (i // 2) % 2:
            place = jnp.where(place >= LANES // 2, place - LANES // 2, place + LANES // 2)
        first_ref[n : n + 1, :] = place
    first_columns = columns(first_ref[...])
    for n in range(slots):
        hit = first_columns[:, n : n + 1] == along_f
        inverse_ref[n : n + 1, :] = summed_down(jnp.where(hit, down_f, 0.0))
        placed_ref[n : n + 1, :] = summed_down(jnp.where(hit, count_columns[:, n : n + 1], 0.0))
    local = summed_down(placed_ref[0:chunks, :])
    room = -summed_down(placed_ref[chunks:tops, :])
    pair_ref[0:1, :] = local
    pair_ref[1:2, :] = room
    pair = columns(pair_ref[...])
    local_place, room_place = place_of(local, pair[:, 0:1]), place_of(room, pair[:, 1:2])
    pair_ref[0:1, :] = local_place
    pair_ref[1:2, :] = room_place
    pair = columns(pair_ref[...])
    goes = summed_down(jnp.where(pair[:, 1:2] == local_place, down_f, 0.0))
    comes = summed_down(jnp.where(pair[:, 0:1] == room_place, down_f, 0.0))
    full = (chunks, LANES)
    comes = jnp.broadcast_to(comes, full).astype(jnp.int32)
    goes = jnp.broadcast_to(goes, full)
    order_ref[0:chunks, :] = lane_gather(goes, first_ref[0:chunks, :].astype(jnp.int32))
    order_ref[chunks:tops, :] = first_ref[chunks:tops, :]
    inverse_ref[0:chunks, :] = lane_gather(inverse_ref[0:chunks, :], comes)
    placed_ref[0:chunks, :] = lane_gather(placed_ref[0:chunks, :], comes)
    running = jnp.zeros((1, LANES), jnp.float32)
    for n in range(slots):
        count_ref[n : n + 1, :] = running
        running = running + placed_ref[n : n + 1, :]
        out_ref[ROWS + n : ROWS + n + 1, :] = running
        out_ref[ROWS + slots + n : ROWS + slots + n + 1, :] = order_ref[n : n + 1, :]
        out_ref[ROWS + 2 * slots + n : ROWS + 2 * slots + n + 1, :] = inverse_ref[n : n + 1, :]
    for k in range(chunks):
        cols = slice(k * LANES, (k + 1) * LANES)
        u = succ_ref[:, cols]
        rows = [jnp.broadcast_to(order_ref[n : n + 1, :], (turns, LANES)) for n in range(slots)]
        lane = jnp.where(valid_ref[:, cols] == 1, table_gather(rows, u), -1.0)
        code = jnp.where(lane >= 0.0, lane + ((u >> 7) * LANES).astype(jnp.float32), -1.0)
        lane_ref[:, cols] = lane
        code_ref[:, cols] = code
        column_ref[cols, :] = columns(code)
    acc_ref[...] = jnp.zeros_like(acc_ref)
    earlier = jnp.where(
        lax.broadcasted_iota(jnp.int32, (step, step), 0) < lax.broadcasted_iota(jnp.int32, (step, step), 1),
        1.0,
        0.0,
    )
    lane_row_f = lane_row.astype(jnp.float32)

    def one_chunk(c, base):
        start = pl.multiple_of(c * step, step)
        cols = pl.ds(start, step)
        s = start + lax.broadcasted_iota(jnp.int32, (1, step), 1)
        source = [
            (s & ~7).astype(jnp.float32).astype(jnp.bfloat16),
            (s & 7).astype(jnp.float32).astype(jnp.bfloat16),
        ]
        for a in range(turns):
            row = slice(a, a + 1)
            hot = jnp.where(lane_ref[row, cols] == lane_row_f, 1.0, 0.0).astype(jnp.bfloat16)
            hot_top = jnp.where((succ_ref[row, cols] >> 7) == top_row, 1.0, 0.0)
            same = column_ref[cols, row] == code_ref[row, cols]
            within = summed_down(jnp.where(same, earlier, 0.0))
            coarse = (base.astype(jnp.int32) & ~127).astype(jnp.float32)
            both = jnp.concatenate([coarse, base - coarse], axis=0).astype(jnp.bfloat16)
            starts = jnp.dot(both, hot, preferred_element_type=jnp.float32)
            begin = summed_down((starts[:tops] + starts[tops:]) * hot_top)
            base = base + product(hot_top.astype(jnp.bfloat16), hot)
            match = jnp.where(begin + within == rank_row, 1.0, 0.0).astype(jnp.bfloat16)
            r = reward_ref[row, cols]
            r1 = r.astype(jnp.bfloat16)
            rest = r - r1.astype(jnp.float32)
            r2 = rest.astype(jnp.bfloat16)
            r3 = (rest - r2.astype(jnp.float32)).astype(jnp.bfloat16)
            left = jnp.concatenate([match * piece for piece in (*source, r1, r2, r3)], axis=0)
            acc_ref[...] += product(left, hot)
        return base

    lax.fori_loop(0, width // step, one_chunk, count_ref[...])
    part = [acc_ref[i * RANKS : i * RANKS + ROWS, :] for i in range(5)]
    share = out_ref.shape[0] // 2
    out_ref[0:ROWS, :] = part[0] + part[1]
    out_ref[share : share + ROWS, :] = (part[2] + part[3]) + part[4]
    listed = columns(border_ref[...].astype(jnp.float32)).astype(jnp.int32)
    for side in range(4):
        for q in range(chunks):
            found = jnp.where(listed[:, side : side + 1] == along + q * LANES, down_f + 1.0, 0.0)
            row = share + ROWS + side * chunks + q
            out_ref[row : row + 1, :] = summed_down(found)
    blocks = anchor_ref.shape[0]
    for q in range(chunks):
        split_ref[pl.ds(q, blocks, chunks), :] = anchor_ref[:, q * LANES : (q + 1) * LANES]
    half = out_ref.at[pl.ds(pl.multiple_of(lax.axis_index("dst") * share, 8), share)]
    size = share + chunks
    pairs = []
    for b in range(blocks):
        pairs.append((half, out_any.at[pl.ds(b * size, share)]))
        pairs.append((split_ref.at[pl.ds(b * chunks, chunks)], out_any.at[pl.ds(b * size + share, chunks)]))
    run_copies(whole_copies(pairs, sem))


def graph_kernel(
    weight_ref, feature_any, succ_any, valid_any, border_any, out_ref, reward_ref,
    feature_ref, succ_ref, valid_ref, border_ref, part_ref, sem
):
    run_copies(
        whole_copies(
            [
                (feature_any, feature_ref),
                (succ_any, succ_ref),
                (valid_any, valid_ref),
                (border_any, border_ref),
            ],
            sem,
        )
    )
    turns, width = succ_ref.shape
    chunks = width // LANES
    edges = turns * chunks
    part_ref[edges : edges + 8, :] = jnp.zeros((8, LANES), jnp.float32)
    part_ref[edges : edges + 4, :] = border_ref[...].astype(jnp.float32)
    first_core = lax.axis_index("dst") == 0
    for q in range(chunks):
        cols = slice(q * LANES, (q + 1) * LANES)
        cost = weight_ref[0] * feature_ref[0, :, cols].astype(jnp.float32)
        for f in range(1, feature_ref.shape[0]):
            cost = cost + weight_ref[f] * feature_ref[f, :, cols].astype(jnp.float32)
        reward_ref[:, cols] = -cost
        masked = jnp.where(valid_ref[:, cols] == 1, -cost, NEG)
        turn_to = succ_ref[:, cols].astype(jnp.float32)
        part_ref[pl.ds(q, turns, chunks), :] = jnp.where(first_core, masked, turn_to)
    common = part_ref.shape[0]
    for b in range(out_ref.shape[0] // common):
        out_ref[b * common : (b + 1) * common, :] = part_ref[...]


def regroup_kernel(pieces_ref, out_ref):
    halves, rows = out_ref.shape[:2]
    size = pieces_ref.shape[0] // (8 * halves)
    for h in range(halves):

        def one_row(i, carry, h=h):
            out_ref[h, i] = of_blocks(pieces_ref, h, i, size)
            return carry

        lax.fori_loop(0, rows, one_row, 0, unroll=8)


def weigh(out):
    top = functools.reduce(jnp.maximum, out)
    raised = [jnp.exp(score - top) for score in out]
    return top, raised, functools.reduce(jnp.add, raised)


def weighed_turns(values, reward, index, h, q, turns, chunks):
    tables = [values[h, r] for r in range(chunks + 4)]
    out = []
    for a in range(turns):
        rows = tables if a else tables[:chunks]
        out.append(reward[h, a * chunks + q] + table_gather(rows, index[h, a * chunks + q]))
    return weigh(out)


def policy_kernel(values_ref, reward_ref, index_ref, raised_ref, max_ref, inv_ref):
    halves, chunks = max_ref.shape[:2]
    turns = reward_ref.shape[1] // chunks

    def one_chunk(q, inner):
        for h in range(halves):
            top, raised, total = weighed_turns(values_ref, reward_ref, index_ref, h, q, turns, chunks)
            max_ref[h, q] = top
            inv_ref[h, q] = 1.0 / total
            for a in range(turns):
                raised_ref[h, a * chunks + q] = raised[a]
        return inner

    lax.fori_loop(0, chunks, one_chunk, 0, unroll=chunks)


def value_kernel(
    grid_x, dest_ref, mine_ref, other_ref, ext_ref, reward, index, border, side_pad, spare_ref
):
    halves = ext_ref.shape[0]
    blocks = 8 * halves
    chunks = ext_ref.shape[1] - 4
    edges = reward.shape[1]
    turns = edges // chunks
    per_block = chunks * LANES
    dest = renumbered(dest_ref[own_block(grid_x)], per_block, blocks, grid_x)
    side_pad[...] = jnp.zeros_like(side_pad)
    sub = lax.broadcasted_iota(jnp.int32, (8, LANES), 0)
    lane = lax.broadcasted_iota(jnp.int32, (8, LANES), 1)
    dest_block, dest_place = lax.div(dest, per_block), lax.rem(dest, per_block)

    def unpack(first, second):
        for h in range(halves):

            def rows(i, carry, h=h):
                reward[h, i] = first[h, i]
                index[h, i] = second[h, i].astype(jnp.int32)
                return carry

            lax.fori_loop(0, edges, rows, 0, unroll=8)
            for side in range(4):
                border[h, side] = first[h, edges + side].astype(jnp.int32)

    by_core(unpack, mine_ref, other_ref)
    for h in range(halves):
        for side in range(4):
            found = (border[h, side] == dest_place) & (h * 8 + sub == dest_block)
            entry = jnp.max(jnp.where(found, lane + 1, 0).astype(jnp.float32), axis=1, keepdims=True)
            side_pad[side, 8 + 8 * h : 16 + 8 * h, :] = jnp.broadcast_to(entry, (8, LANES))
    shifts = ((1, -1), (0, 1), (3, -grid_x), (2, grid_x))

    def shown(h, side):
        facing, by = shifts[side]
        start = 8 + 8 * h + by
        return side_pad[facing, start : start + 8, :]

    def dest_index(h):
        where = jnp.where(h * 8 + sub == dest_block, dest_place, -1)
        for side in range(4):
            entry = shown(h, side).astype(jnp.int32)
            where = jnp.where(entry > 0, per_block + side * LANES + entry - 1, where)
        return where

    def bring_halo(values):
        for h in range(halves):
            table = [values[h, q] for q in range(chunks)]
            for side in range(4):
                side_pad[side, 8 + 8 * h : 16 + 8 * h, :] = table_gather(table, border[h, side])
        for h in range(halves):
            for side in range(4):
                values[h, chunks + side] = shown(h, side)

    def store_value(h, q, top, total, into):
        value = top + jnp.log(total)
        into[h, q] = jnp.where(target_mask(dest, h, q, per_block), 0.0, value)

    wanted = [dest_index(h) for h in range(halves)]

    def first_chunk(q, inner):
        for h in range(halves):
            out = []
            for a in range(turns):
                before = jnp.where(index[h, a * chunks + q] == wanted[h], 0.0, -START_COST)
                out.append(reward[h, a * chunks + q] + before)
            top, _, total = weigh(out)
            store_value(h, q, top, total, spare_ref)
        return inner

    lax.fori_loop(0, chunks, first_chunk, 0, unroll=2)

    def backup(values, into):
        bring_halo(values)

        def one_chunk(q, inner):
            for h in range(halves):
                top, _, total = weighed_turns(values, reward, index, h, q, turns, chunks)
                store_value(h, q, top, total, into)
            return inner

        lax.fori_loop(0, chunks, one_chunk, 0, unroll=chunks)

    def two_backups(step, carry):
        backup(spare_ref, ext_ref)
        backup(ext_ref, spare_ref)
        return carry

    lax.fori_loop(0, (HORIZON - 2) // 2, two_backups, 0)
    backup(spare_ref, ext_ref)
    bring_halo(ext_ref)


def push_kernel(
    grid_x, scale, dest_ref, mine_ref, other_ref, graph_mine, graph_other, ext_ref, raised_ref, max_ref,
    inv_ref, keep_ref, send_ref, counts, ends, order, values, source, slot, going, policy, flows, back, scaled, total, arrived, side_pad, raw
):
    halves = ext_ref.shape[0]
    blocks = 8 * halves
    share = mine_ref.shape[1]
    chunks = max_ref.shape[1]
    edges = raised_ref.shape[1]
    turns = edges // chunks
    per_block = chunks * LANES
    slots = chunks + 4
    dest = renumbered(dest_ref[own_block(grid_x)], per_block, blocks, grid_x)
    core = lax.axis_index("dst")
    side_pad[...] = jnp.zeros_like(side_pad)

    def unpack(first, second):
        for h in range(halves):
            for n in range(slots):
                ends[h, n] = first[h, ROWS + n]
                order[h, n] = first[h, ROWS + slots + n].astype(jnp.int32)
                inverse = first[h, ROWS + 2 * slots + n].astype(jnp.int32)
                values[h, n] = lane_gather(ext_ref[h, n], inverse)

            def rows(r, carry, h=h):
                source[h, r] = first[h, r].astype(jnp.int32)
                policy[h, r] = second[h, r]
                return carry

            lax.fori_loop(0, ROWS, rows, 0, unroll=6)
            for r in range(ROWS, DEPTH):
                source[h, r] = jnp.zeros((8, LANES), jnp.int32)
                policy[h, r] = jnp.zeros((8, LANES), jnp.float32)
            for n in range(4 * chunks):
                back[h, n] = second[h, ROWS + n].astype(jnp.int32) - 1

    by_core(unpack, mine_ref, other_ref)
    deepest = jnp.max(functools.reduce(jnp.maximum, [ends[h, slots - 1] for h in range(halves)]))
    deepest = deepest.astype(jnp.int32)
    fits = deepest <= ROWS
    steps = jnp.where(deepest <= USUAL, USUAL // STEP, DEPTH // STEP)
    shifts = ((1, -1), (0, 1), (3, -grid_x), (2, grid_x))

    def shown(h, side):
        facing, by = shifts[side]
        start = 8 + 8 * h + by
        return side_pad[facing, start : start + 8, :]

    @pl.when(jnp.logical_not(fits))
    def _():
        for h in range(halves):
            for n in range(slots):
                order[h, n] = lax.broadcasted_iota(jnp.int32, (8, LANES), 1)

    for h in range(halves):
        for side in range(4):
            side_pad[side, 8 + 8 * h : 16 + 8 * h, :] = order[h, chunks + side].astype(jnp.float32)
    for h in range(halves):
        for side in range(4):
            lanes = shown(h, side).astype(jnp.int32)
            for q in range(chunks):
                entry = back[h, side * chunks + q]
                back[h, side * chunks + q] = jnp.where(
                    entry >= 0, lane_gather(lanes, jnp.maximum(entry, 0)), -1
                )

    def prepare_rows(rows):
        row_before = [None] * halves
        for i, r in enumerate(rows):
            for h in range(halves):
                src = source[h, r]
                place = jnp.asarray(r).astype(jnp.float32)
                row = functools.reduce(
                    jnp.add, [jnp.where(ends[h, n] <= place, 1, 0) for n in range(slots)]
                )
                slot[h, r] = row
                if i:
                    going[h, r] = jnp.where(row == row_before[h], 1.0, 0.0)
                row_before[h] = row
                bits = [(row & (1 << n)) != 0 for n in range(4)]
                picked = tree_select([values[h, n] for n in range(slots)], bits)
                top = table_gather([max_ref[h, q] for q in range(chunks)], src)
                policy[h, r] = jnp.exp(policy[h, r] + picked - top)

    def prepare_step(t, carry):
        prepare_rows([t * STEP + i for i in range(STEP)])
        return carry

    usual = deepest <= USUAL
    pl.when(usual)(lambda: prepare_rows(range(USUAL)))
    lax.fori_loop(0, jnp.where(usual, 0, steps), prepare_step, 0)
    for h in range(halves):
        for q in range(chunks):
            own = mine_ref[h, share - chunks + q]
            first = jnp.where(target_mask(dest, h, q, per_block), 0.0, own)
            total[h, q] = first
            scaled[h, q] = first * inv_ref[h, q]

    @pl.when(jnp.logical_not(fits))
    def _():
        def keep_turns(first, second):
            for h in range(halves):

                def rows(e, carry, h=h):
                    raw[h, e] = second[h, e].astype(jnp.int32)
                    return carry

                lax.fori_loop(0, edges, rows, 0)

        by_core(keep_turns, graph_mine, graph_other)

    zero = jnp.zeros((8, LANES), jnp.float32)

    def keep(h):
        for side in range(4):
            side_pad[side, 8 + 8 * h : 16 + 8 * h, :] = arrived[h, chunks + side]

    def add_flow(acc, row, flow):
        return [acc[n] + jnp.where(row == n, flow, 0.0) for n in range(slots)]

    def sum_arranged():
        for h in range(halves):
            for n in range(slots):
                arrived[h, n] = zero

        def one_step(t, carry):
            tables = [[scaled[h, q] for q in range(chunks)] for h in range(halves)]
            step_sums = [[zero] * slots for h in range(halves)]
            so_far = [None] * halves
            for i in range(STEP):
                r = t * STEP + i
                for h in range(halves):
                    flow = table_gather(tables[h], source[h, r]) * policy[h, r]
                    so_far[h] = flow + going[h, r] * so_far[h] if i else flow
                    row = slot[h, r]
                    step_sums[h] = [jnp.where(row == n, so_far[h], step_sums[h][n]) for n in range(slots)]
            for h in range(halves):
                for n in range(slots):
                    arrived[h, n] = arrived[h, n] + step_sums[h][n]
            return carry

        def usual_rows():
            for h in range(halves):
                table = [scaled[h, q] for q in range(chunks)]
                for r in range(USUAL):
                    flow = table_gather(table, source[h, r]) * policy[h, r]
                    so_far = flow + going[h, r] * so_far if r else flow
                    flows[h, r] = so_far
            for h in range(halves):
                sums = [zero] * slots
                for r in range(USUAL):
                    row, so_far = slot[h, r], flows[h, r]
                    sums = [jnp.where(row == n, so_far, sums[n]) for n in range(slots)]
                for n in range(slots):
                    arrived[h, n] = sums[n]

        pl.when(usual)(usual_rows)
        lax.fori_loop(0, jnp.where(usual, 0, steps), one_step, 0)
        for h in range(halves):
            keep(h)

    def sum_turned():
        lane = lax.broadcasted_iota(jnp.int32, (8, LANES), 1)
        for h in range(halves):

            def one_edge_row(e, acc, h=h):
                flow = scaled[h, lax.rem(e, chunks)] * raised_ref[h, e]
                where = raw[h, e]

                def one_turn(k, state):
                    flow, where, acc = state[0], state[1], list(state[2:])
                    here = jnp.where((where & (LANES - 1)) == lane, where >> 7, -1)
                    acc = add_flow(acc, here, flow)
                    return (pltpu.roll(flow, 1, 1), pltpu.roll(where, 1, 1), *acc)

                return tuple(lax.fori_loop(0, LANES, one_turn, (flow, where, *acc))[2:])

            for n, value in enumerate(lax.fori_loop(0, edges, one_edge_row, (zero,) * slots)):
                arrived[h, n] = value
            keep(h)

    def push(round_index, carry):
        pl.when(fits)(sum_arranged)
        pl.when(jnp.logical_not(fits))(sum_turned)
        for h in range(halves):
            landed = [shown(h, side) for side in range(4)]
            for q in range(chunks):
                value = lane_gather(arrived[h, q], order[h, q])
                for side in range(4):
                    entry = back[h, side * chunks + q]
                    got = lane_gather(landed[side], jnp.maximum(entry, 0))
                    value = value + jnp.where(entry >= 0, got, 0.0)
                value = jnp.where(target_mask(dest, h, q, per_block), 0.0, value)
                total[h, q] = total[h, q] + value
                scaled[h, q] = value * inv_ref[h, q]
        return carry

    lax.fori_loop(0, HORIZON - 1, push, 0)
    rows_out = edges // 2
    apart = counts.shape[1] // blocks
    for h in range(halves):
        for q in range(chunks):
            weight = total[h, q] * inv_ref[h, q] * scale
            for part, piece in ((core, 0), (1 - core, 1)):
                for a in range(turns // 2):
                    value = weight * raised_ref[h, (part * (turns // 2) + a) * chunks + q]
                    start = h * 8 * apart + a * chunks + q
                    counts[piece, pl.ds(start, 8, stride=apart), :] = value
    for piece, out_ref in ((0, keep_ref), (1, send_ref)):
        for b in range(blocks):
            out_ref[b * rows_out : (b + 1) * rows_out, :] = counts[
                piece, b * apart : b * apart + rows_out, :
            ]


VMEM_SPEC = pl.BlockSpec(memory_space=pltpu.VMEM)
SMEM_SPEC = pl.BlockSpec(memory_space=pltpu.SMEM)
HBM_SPEC = pl.BlockSpec(memory_space=pltpu.HBM)
PARAMS = pltpu.CompilerParams(vmem_limit_bytes=48 * 1024 * 1024)


def f32(*shape):
    return jax.ShapeDtypeStruct(shape, jnp.float32)


def call_graph(cost_weights, features, successors, turn_valid, border_lists, blocks):
    turns, width = successors.shape
    chunks = width // LANES
    rows = turns * chunks + 8
    return pl.pallas_call(
        graph_kernel,
        out_shape=(f32(blocks * rows, LANES), f32(turns, width)),
        in_specs=[SMEM_SPEC] + [HBM_SPEC] * 4,
        out_specs=(VMEM_SPEC, VMEM_SPEC),
        scratch_shapes=[
            pltpu.VMEM(features.shape, features.dtype),
            pltpu.VMEM(successors.shape, jnp.int32),
            pltpu.VMEM(turn_valid.shape, jnp.int32),
            pltpu.VMEM(border_lists.shape, jnp.int32),
            pltpu.VMEM((rows, LANES), jnp.float32),
            pltpu.SemaphoreType.DMA((4,)),
        ],
        compiler_params=pltpu.CompilerParams(vmem_limit_bytes=63 * 1024 * 1024),
        name="own_graph",
    )(cost_weights, features, successors, turn_valid, border_lists)


def arranged_rows(chunks):
    most = ROWS + max(3 * (chunks + 4), 4 * chunks)
    return -(-most // 8) * 8


def call_arrange(successors, turn_valid, border_lists, anchors, reward):
    chunks = successors.shape[1] // LANES
    share = arranged_rows(chunks)
    blocks = anchors.shape[0]
    return pl.pallas_call(
        arrange_kernel,
        out_shape=f32(blocks * (share + chunks), LANES),
        in_specs=[HBM_SPEC] * 4 + [VMEM_SPEC],
        out_specs=HBM_SPEC,
        scratch_shapes=[
            pltpu.VMEM(successors.shape, jnp.int32),
            pltpu.VMEM(turn_valid.shape, jnp.int32),
            pltpu.VMEM(border_lists.shape, jnp.int32),
            pltpu.VMEM(anchors.shape, jnp.float32),
            pltpu.VMEM((blocks * chunks, LANES), jnp.float32),
            pltpu.VMEM((2 * share, LANES), jnp.float32),
            *[pltpu.VMEM((16, LANES), jnp.float32)] * 5,
            pltpu.VMEM((8, LANES), jnp.float32),
            pltpu.VMEM(successors.shape, jnp.float32),
            pltpu.VMEM(successors.shape, jnp.float32),
            pltpu.VMEM(successors.shape[::-1], jnp.float32),
            pltpu.VMEM((5 * RANKS, LANES), jnp.float32),
            pltpu.SemaphoreType.DMA((2 * blocks,)),
        ],
        compiler_params=PARAMS,
        cost_estimate=pl.CostEstimate(flops=4_000_000_000, bytes_accessed=400_000, transcendentals=0),
        name="arrange_turns",
    )(successors, turn_valid, border_lists, anchors, reward)


def call_regroup(pieces, blocks):
    return pl.pallas_call(
        regroup_kernel,
        out_shape=f32(blocks // 8, pieces.shape[0] // blocks, 8, LANES),
        in_specs=[VMEM_SPEC],
        out_specs=VMEM_SPEC,
        compiler_params=PARAMS,
        name="regroup",
    )(pieces)


def call_values(destinations, mine, other, blocks, grid_x, turns, chunks):
    halves = blocks // 8
    edges = turns * chunks
    rows = (halves, edges, 8, LANES)
    return pl.pallas_call(
        functools.partial(value_kernel, grid_x),
        out_shape=(
            f32(halves, chunks + 4, 8, LANES),
            f32(*rows),
            jax.ShapeDtypeStruct(rows, jnp.int32),
        ),
        in_specs=[SMEM_SPEC, VMEM_SPEC, VMEM_SPEC],
        out_specs=(VMEM_SPEC,) * 3,
        scratch_shapes=[
            pltpu.VMEM((halves, 4, 8, LANES), jnp.int32),
            pltpu.VMEM((4, blocks + 16, LANES), jnp.float32),
            pltpu.VMEM((halves, chunks + 4, 8, LANES), jnp.float32),
        ],
        compiler_params=PARAMS,
        cost_estimate=pl.CostEstimate(flops=40_000_000, bytes_accessed=40_000_000, transcendentals=2_000_000),
        name="soft_values",
    )(destinations, mine, other)


def call_policy(ext, reward, index):
    halves, edges = reward.shape[:2]
    chunks = ext.shape[1] - 4
    return pl.pallas_call(
        policy_kernel,
        out_shape=(f32(*reward.shape), f32(halves, chunks, 8, LANES), f32(halves, chunks, 8, LANES)),
        in_specs=[VMEM_SPEC] * 3,
        out_specs=(VMEM_SPEC,) * 3,
        compiler_params=PARAMS,
        cost_estimate=pl.CostEstimate(flops=5_000_000, bytes_accessed=5_000_000, transcendentals=200_000),
        name="policy",
    )(ext, reward, index)


def call_push(destinations, mine, other, graph_mine, graph_other, ext, raised, top, inv, grid_x, scale):
    halves, edges = raised.shape[:2]
    blocks = 8 * halves
    chunks = top.shape[1]

    def vmem(rows, dtype=jnp.float32):
        return pltpu.VMEM((halves, rows, 8, LANES), dtype)

    return pl.pallas_call(
        functools.partial(push_kernel, grid_x, scale),
        out_shape=(f32(blocks * edges // 2, LANES),) * 2,
        in_specs=[SMEM_SPEC] + [VMEM_SPEC] * 8,
        out_specs=(VMEM_SPEC,) * 2,
        scratch_shapes=[
            pltpu.VMEM((2, blocks * padded_rows(edges // 2), LANES), jnp.float32),
            vmem(chunks + 4),
            vmem(chunks + 4, jnp.int32),
            vmem(chunks + 4),
            vmem(DEPTH, jnp.int32),
            vmem(DEPTH, jnp.int32),
            vmem(DEPTH),
            vmem(DEPTH),
            vmem(USUAL),
            vmem(4 * chunks, jnp.int32),
            vmem(chunks),
            vmem(chunks),
            vmem(chunks + 4),
            pltpu.VMEM((4, blocks + 16, LANES), jnp.float32),
            vmem(edges, jnp.int32),
        ],
        compiler_params=PARAMS,
        name="push_mass",
    )(destinations, mine, other, graph_mine, graph_other, ext, raised, top, inv)


def to_blocks(array):
    return lax.all_to_all(array, BLOCK_AXES, 0, 0, tiled=True)


def other_core(array):
    return lax.ppermute(array, "dst", [(0, 1), (1, 0)])


def per_destination(
    features, cost_weights, successors, turn_valid, border_lists, destinations, anchors, demo_counts
):
    turns, own_count = successors.shape
    chunks = own_count // LANES
    edges = turns * chunks
    grid_x = lax.axis_size("gx")
    blocks = lax.axis_size("gy") * grid_x
    groups = lax.axis_size("dst")
    pieces, reward = call_graph(cost_weights, features, successors, turn_valid, border_lists, blocks)
    graph = to_blocks(pieces)
    arranged = call_arrange(successors, turn_valid, border_lists, anchors, reward)
    core = lax.axis_index("dst")
    demo_term = jnp.where(turn_valid == 1, demo_counts, 0).astype(jnp.float32) / 3.0
    own_feats = lax.dynamic_slice_in_dim(features, core * (turns // 2), turns // 2, axis=1)
    first_core, own_feats, demo_term, arranged = lax.optimization_barrier(
        (core == 0, own_feats, demo_term, arranged)
    )
    graph = call_regroup(lax.optimization_barrier((graph, arranged))[0], blocks)
    graph, arranged = lax.optimization_barrier((graph, arranged))
    graph = (graph, other_core(graph))
    arranged = to_blocks(arranged)
    ext, reward, index = call_values(destinations, *graph, blocks, grid_x, turns, chunks)
    arranged, ext = lax.optimization_barrier((arranged, ext))
    arranged = call_regroup(arranged, blocks)
    arranged, ext = lax.optimization_barrier((arranged, ext))
    arranged = (arranged, other_core(arranged))
    values = (ext, *call_policy(ext, reward, index))
    scale = 1.0 / (anchors.shape[0] * groups * HORIZON)
    kept, sent = call_push(destinations, *arranged, *graph, *values, grid_x, scale)
    halved = (kept + other_core(sent)).reshape(blocks, edges // 2, LANES)
    half = jnp.sum(to_blocks(halved), axis=0)
    other = other_core(half)
    part = (turns // 2, own_count)
    own_gap = lax.dynamic_slice_in_dim(demo_term, core * part[0], part[0]) - half.reshape(part)
    own_feats = own_feats.astype(jnp.float32)
    block_term = jnp.sum(own_gap[None] * own_feats, axis=(1, 2)) / (own_count * blocks)
    visits = jnp.concatenate([jnp.where(first_core, half, other), jnp.where(first_core, other, half)])
    count_gap = demo_term - visits.reshape(turns, own_count)
    terms = jnp.broadcast_to(block_term, (groups * blocks, 1, block_term.shape[0]))
    terms = lax.all_to_all(terms, (*BLOCK_AXES, "dst"), 0, 0, tiled=True)
    terms, count_gap = lax.optimization_barrier((terms, count_gap))
    return count_gap, jnp.sum(terms, axis=(0, 1))


def passed_along(array, axis, by):
    length = lax.axis_size(axis)
    pairs = [(i, i + by) for i in range(length) if 0 <= i + by < length]
    return lax.ppermute(array, axis, pairs)


def bring_values(values, border_lists):
    outgoing = values[:, border_lists]
    north_part = passed_along(outgoing[:, 1], "gx", 1)
    south_part = passed_along(outgoing[:, 0], "gx", -1)
    west_part = passed_along(outgoing[:, 3], "gy", 1)
    east_part = passed_along(outgoing[:, 2], "gy", -1)
    return jnp.concatenate([north_part, south_part, west_part, east_part], axis=1)


def return_flow(arrived, border_lists, own_count, border_width):
    local_part = arrived[:, :own_count]
    halo_part = arrived[:, own_count:].reshape(arrived.shape[0], 4, border_width)
    from_south = passed_along(halo_part[:, 0], "gx", -1)
    from_north = passed_along(halo_part[:, 1], "gx", 1)
    from_east = passed_along(halo_part[:, 2], "gy", -1)
    from_west = passed_along(halo_part[:, 3], "gy", 1)
    returned = jnp.stack([from_north, from_south, from_west, from_east], axis=1)
    return local_part.at[:, border_lists].add(returned)


def select_cells(cells, flat_index, turn_shape):
    picked = jnp.take(cells, flat_index, axis=1)
    return picked.reshape(cells.shape[0], turn_shape[0], turn_shape[1])


def turn_scores(values, halo_cells, reward, flat_turns, usable):
    extended = jnp.concatenate([values, halo_cells], axis=1)
    scores = reward[None] + select_cells(extended, flat_turns, usable.shape)
    return jnp.where(usable[None], scores, NEG)


def per_block(
    features, cost_weights, successors, turn_valid, border_lists, destinations, anchors, demo_counts
):
    own_count = successors.shape[1]
    border_width = border_lists.shape[1]
    dest_count = anchors.shape[0]
    slot_total = own_count + 4 * border_width
    block_index = lax.axis_index("gx") * lax.axis_size("gy") + lax.axis_index("gy")
    positions = jnp.arange(own_count, dtype=jnp.int32)
    is_target = positions[None, :] == (destinations - block_index * own_count)[:, None]
    usable = turn_valid == 1
    feats = features.astype(jnp.float32)
    reward = -jnp.sum(feats * cost_weights[:, None, None], axis=0)
    flat_turns = successors.reshape(-1)
    values = jnp.where(is_target, 0.0, -START_COST).astype(jnp.float32)
    for round_index in range(HORIZON):
        halo_cells = bring_values(values, border_lists)
        scores = turn_scores(values, halo_cells, reward, flat_turns, usable)
        row_max = jnp.max(scores, axis=1)
        new_values = row_max + jnp.log(jnp.sum(jnp.exp(scores - row_max[:, None]), axis=1))
        values = jnp.where(is_target, 0.0, new_values)
    halo_cells = bring_values(values, border_lists)
    scores = turn_scores(values, halo_cells, reward, flat_turns, usable)
    row_max = jnp.max(scores, axis=1)
    raised = jnp.exp(scores - row_max[:, None])
    policy = raised / jnp.sum(raised, axis=1, keepdims=True)
    mass_now = jnp.where(is_target, 0.0, anchors)
    turn_counts = jnp.zeros(successors.shape, jnp.float32)
    for round_index in range(HORIZON):
        turn_flow = mass_now[:, None, :] * policy
        turn_counts = turn_counts + jnp.sum(turn_flow, axis=0)
        if round_index + 1 < HORIZON:
            arrived = (
                jnp.zeros((dest_count, slot_total), jnp.float32)
                .at[:, flat_turns]
                .add(turn_flow.reshape(dest_count, -1))
            )
            landed = return_flow(arrived, border_lists, own_count, border_width)
            mass_now = jnp.where(is_target, 0.0, landed)
    local_visits = turn_counts / (dest_count * lax.axis_size("dst") * HORIZON)
    visits = lax.psum(local_visits, "dst")
    demo_term = jnp.where(usable, demo_counts, 0).astype(jnp.float32) / 3.0
    count_gap = demo_term - visits
    total_segments = own_count * lax.axis_size("gx") * lax.axis_size("gy")
    own_gap = demo_term / lax.axis_size("dst") - local_visits
    block_term = jnp.sum(own_gap[None] * feats, axis=(1, 2)) / total_segments
    gradient = lax.psum(block_term, ("gx", "gy", "dst"))
    return (count_gap, gradient)


def local(features, cost_weights, successors, turn_valid, border_lists, destinations, anchors, demo_counts):
    args = (
        features, cost_weights, successors, turn_valid, border_lists, destinations, anchors, demo_counts
    )
    blocks = lax.axis_size("gx") * lax.axis_size("gy")
    fits = (
        anchors.shape[0] == blocks
        and blocks % 8 == 0
        and lax.axis_size("dst") == 2
        and lax.axis_size("gx") in (2, 4, 8)
        and lax.axis_size("gy") in (2, 4, 8)
        and successors.shape[1] == 8 * LANES
        and border_lists.shape[1] == LANES
    )
    return per_destination(*args) if fits else per_block(*args)


def solution(mesh):
    in_specs = (
        P(None, None, ("gx", "gy")),
        P(),
        P(None, ("gx", "gy")),
        P(None, ("gx", "gy")),
        P(None, ("gx", "gy")),
        P("dst"),
        P("dst", ("gx", "gy")),
        P(None, ("gx", "gy")),
    )
    out_specs = (P(None, ("gx", "gy")), P())
    return jax.shard_map(local, mesh=mesh, in_specs=in_specs, out_specs=out_specs, check_vma=False)
```

```python
import functools

import jax
import jax.numpy as jnp
from jax import lax
from jax.experimental import pallas as pl
from jax.experimental.pallas import tpu as pltpu
from jax.sharding import PartitionSpec as P

HORIZON = 8
NEG = -1e30
START_COST = 100.0
LANES = 128
ROWS = 60
RANKS = -(-ROWS // 16) * 16
STEP = 14
USUAL = 56
DEPTH = -(-ROWS // STEP) * STEP
BLOCK_AXES = ("gy", "gx")

LANE_PICK = lax.GatherDimensionNumbers(
    offset_dims=(),
    collapsed_slice_dims=(1,),
    start_index_map=(1,),
    operand_batching_dims=(0,),
    start_indices_batching_dims=(0,),
)


def lane_gather(table, index):
    return lax.gather(
        table,
        index[..., None],
        LANE_PICK,
        (1, 1),
        mode=lax.GatherScatterMode.PROMISE_IN_BOUNDS,
    )


def tree_select(picked, bits):
    level = list(picked)
    for bit in bits:
        if len(level) == 1:
            break
        nxt = []
        for n in range(0, len(level), 2):
            if n + 1 < len(level):
                nxt.append(jnp.where(bit, level[n + 1], level[n]))
            else:
                nxt.append(level[n])
        level = nxt
    return level[0]


def row_bits(index, count):
    return [(index & (LANES << i)) != 0 for i in range(count)]


def table_gather(table_rows, index):
    lane = index & (LANES - 1)
    bits = row_bits(index, max(len(table_rows) - 1, 1).bit_length())
    return tree_select([lane_gather(row, lane) for row in table_rows], bits)


def run_copies(copies):
    for copy in copies:
        copy.start()
    for copy in copies:
        copy.wait()


def of_blocks(ref, half, row, per_block):
    return ref[pl.ds(half * 8 * per_block + row, 8, stride=per_block), :]


def whole_copies(pairs, sem):
    return [pltpu.make_async_copy(src, dst, sem.at[n]) for n, (src, dst) in enumerate(pairs)]


def by_core(what, mine, other):
    first = lax.axis_index("dst") == 0
    pl.when(first)(lambda: what(mine, other))
    pl.when(jnp.logical_not(first))(lambda: what(other, mine))


def own_block(grid_x):
    return lax.axis_index("gy") * grid_x + lax.axis_index("gx")


def renumbered(segment, per_block, blocks, grid_x):
    grid_y = blocks // grid_x
    block, place = lax.div(segment, per_block), lax.rem(segment, per_block)
    return (lax.rem(block, grid_y) * grid_x + lax.div(block, grid_y)) * per_block + place


def padded_rows(rows):
    tiles = -(-rows // 8)
    return (tiles + 1 - tiles % 2) * 8


def target_mask(dest, half, chunk, per_block):
    sub = lax.broadcasted_iota(jnp.int32, (8, LANES), 0)
    lane = lax.broadcasted_iota(jnp.int32, (8, LANES), 1)
    return (half * 8 + sub) * per_block + chunk * LANES + lane == dest


def arrange_kernel(
    succ_any, valid_any, border_any, anchor_any, reward_ref, out_any,
    succ_ref, valid_ref, border_ref, anchor_ref, split_ref, out_ref, count_ref, first_ref, order_ref, inverse_ref, placed_ref,
    pair_ref, lane_ref, code_ref, column_ref, acc_ref, sem
):
    run_copies(
        whole_copies(
            [
                (succ_any, succ_ref),
                (valid_any, valid_ref),
                (border_any, border_ref),
                (anchor_any, anchor_ref),
            ],
            sem,
        )
    )
    turns, width = succ_ref.shape
    chunks = width // LANES
    slots = chunks + 4
    step = 2 * LANES
    tops = 16
    square = (LANES, LANES)
    down = lax.broadcasted_iota(jnp.int32, square, 0)
    along = lax.broadcasted_iota(jnp.int32, square, 1)
    down_f, along_f = down.astype(jnp.float32), along.astype(jnp.float32)
    before = down < along
    unit = jnp.where(down == along, 1.0, 0.0)
    lane_row = lax.broadcasted_iota(jnp.int32, (LANES, step), 0)
    top_row = lax.broadcasted_iota(jnp.int32, (tops, step), 0)
    rank_row = lax.broadcasted_iota(jnp.int32, (RANKS, step), 0).astype(jnp.float32)
    last_dims = (((1,), (1,)), ((), ()))

    def product(left, right):
        return lax.dot_general(left, right, last_dims, preferred_element_type=jnp.float32)

    def columns(rows):
        return lax.dot_general(
            unit, rows, last_dims, precision=lax.Precision.HIGHEST, preferred_element_type=jnp.float32
        )

    def summed_down(array):
        return jnp.sum(array, axis=0, keepdims=True)

    def place_of(row, col):
        return summed_down(jnp.where((col > row) | ((col == row) & before), 1.0, 0.0))

    def count(a, total):
        for c in range(width // step):
            cols = slice(c * step, (c + 1) * step)
            u = succ_ref[pl.ds(a, 1), cols]
            low = jnp.where(valid_ref[pl.ds(a, 1), cols] == 1, u & (LANES - 1), -1)
            hot_low = jnp.where(low == lane_row, 1.0, 0.0).astype(jnp.bfloat16)
            hot_top = jnp.where((u >> 7) == top_row, 1.0, 0.0).astype(jnp.bfloat16)
            total = total + product(hot_top, hot_low)
        return total

    counts = lax.fori_loop(0, turns, count, jnp.zeros((tops, LANES), jnp.float32), unroll=2)
    count_columns = columns(counts)
    out_ref[...] = jnp.zeros_like(out_ref)
    for ref in (count_ref, first_ref, order_ref, inverse_ref, placed_ref, pair_ref):
        ref[...] = jnp.zeros_like(ref)
    for n in range(slots):
        i = n if n < chunks else n - chunks
        place = place_of(counts[n : n + 1, :], count_columns[:, n : n + 1])
        place = place if i % 2 == 0 else (LANES - 1.0) - place
        if (i // 2) % 2:
            place = jnp.where(place >= LANES // 2, place - LANES // 2, place + LANES // 2)
        first_ref[n : n + 1, :] = place
    first_columns = columns(first_ref[...])
    for n in range(slots):
        hit = first_columns[:, n : n + 1] == along_f
        inverse_ref[n : n + 1, :] = summed_down(jnp.where(hit, down_f, 0.0))
        placed_ref[n : n + 1, :] = summed_down(jnp.where(hit, count_columns[:, n : n + 1], 0.0))
    local = summed_down(placed_ref[0:chunks, :])
    room = -summed_down(placed_ref[chunks:tops, :])
    pair_ref[0:1, :] = local
    pair_ref[1:2, :] = room
    pair = columns(pair_ref[...])
    local_place, room_place = place_of(local, pair[:, 0:1]), place_of(room, pair[:, 1:2])
    pair_ref[0:1, :] = local_place
    pair_ref[1:2, :] = room_place
    pair = columns(pair_ref[...])
    goes = summed_down(jnp.where(pair[:, 1:2] == local_place, down_f, 0.0))
    comes = summed_down(jnp.where(pair[:, 0:1] == room_place, down_f, 0.0))
    full = (chunks, LANES)
    comes = jnp.broadcast_to(comes, full).astype(jnp.int32)
    goes = jnp.broadcast_to(goes, full)
    order_ref[0:chunks, :] = lane_gather(goes, first_ref[0:chunks, :].astype(jnp.int32))
    order_ref[chunks:tops, :] = first_ref[chunks:tops, :]
    inverse_ref[0:chunks, :] = lane_gather(inverse_ref[0:chunks, :], comes)
    placed_ref[0:chunks, :] = lane_gather(placed_ref[0:chunks, :], comes)
    running = jnp.zeros((1, LANES), jnp.float32)
    for n in range(slots):
        count_ref[n : n + 1, :] = running
        running = running + placed_ref[n : n + 1, :]
        out_ref[ROWS + n : ROWS + n + 1, :] = running
        out_ref[ROWS + slots + n : ROWS + slots + n + 1, :] = order_ref[n : n + 1, :]
        row = inverse_row(n, slots)
        out_ref[row : row + 1, :] = inverse_ref[n : n + 1, :]
    for k in range(chunks):
        cols = slice(k * LANES, (k + 1) * LANES)
        u = succ_ref[:, cols]
        rows = [jnp.broadcast_to(order_ref[n : n + 1, :], (turns, LANES)) for n in range(slots)]
        lane = jnp.where(valid_ref[:, cols] == 1, table_gather(rows, u), -1.0)
        code = jnp.where(lane >= 0.0, lane + ((u >> 7) * LANES).astype(jnp.float32), -1.0)
        lane_ref[:, cols] = lane
        code_ref[:, cols] = code
        column_ref[cols, :] = columns(code)
    acc_ref[...] = jnp.zeros_like(acc_ref)
    earlier = jnp.where(
        lax.broadcasted_iota(jnp.int32, (step, step), 0) < lax.broadcasted_iota(jnp.int32, (step, step), 1),
        1.0,
        0.0,
    )
    lane_row_f = lane_row.astype(jnp.float32)

    def one_chunk(c, base):
        start = pl.multiple_of(c * step, step)
        cols = pl.ds(start, step)
        s = start + lax.broadcasted_iota(jnp.int32, (1, step), 1)
        source = [
            (s & ~7).astype(jnp.float32).astype(jnp.bfloat16),
            (s & 7).astype(jnp.float32).astype(jnp.bfloat16),
        ]
        for a in range(turns):
            row = slice(a, a + 1)
            hot = jnp.where(lane_ref[row, cols] == lane_row_f, 1.0, 0.0).astype(jnp.bfloat16)
            hot_top = jnp.where((succ_ref[row, cols] >> 7) == top_row, 1.0, 0.0)
            same = column_ref[cols, row] == code_ref[row, cols]
            within = summed_down(jnp.where(same, earlier, 0.0))
            coarse = (base.astype(jnp.int32) & ~127).astype(jnp.float32)
            both = jnp.concatenate([coarse, base - coarse], axis=0).astype(jnp.bfloat16)
            starts = jnp.dot(both, hot, preferred_element_type=jnp.float32)
            begin = summed_down((starts[:tops] + starts[tops:]) * hot_top)
            base = base + product(hot_top.astype(jnp.bfloat16), hot)
            match = jnp.where(begin + within == rank_row, 1.0, 0.0).astype(jnp.bfloat16)
            r = reward_ref[row, cols]
            r1 = r.astype(jnp.bfloat16)
            rest = r - r1.astype(jnp.float32)
            r2 = rest.astype(jnp.bfloat16)
            r3 = (rest - r2.astype(jnp.float32)).astype(jnp.bfloat16)
            left = jnp.concatenate([match * piece for piece in (*source, r1, r2, r3)], axis=0)
            acc_ref[...] += product(left, hot)
        return base

    lax.fori_loop(0, width // step, one_chunk, count_ref[...])
    part = [acc_ref[i * RANKS : i * RANKS + ROWS, :] for i in range(5)]
    share = out_ref.shape[0] // 2
    out_ref[0:ROWS, :] = part[0] + part[1]
    out_ref[share : share + ROWS, :] = (part[2] + part[3]) + part[4]
    listed = columns(border_ref[...].astype(jnp.float32)).astype(jnp.int32)
    for side in range(4):
        for q in range(chunks):
            found = jnp.where(listed[:, side : side + 1] == along + q * LANES, down_f + 1.0, 0.0)
            row = share + ROWS + side * chunks + q
            out_ref[row : row + 1, :] = summed_down(found)
    blocks = anchor_ref.shape[0]
    for q in range(chunks):
        split_ref[pl.ds(q, blocks, chunks), :] = anchor_ref[:, q * LANES : (q + 1) * LANES]
    start = pl.multiple_of(lax.axis_index("dst") * share, 8)
    common = share - chunks
    shared = out_ref[pl.ds(start + common, chunks), :]
    sub = lax.broadcasted_iota(jnp.int32, (chunks, LANES), 0)
    own_rows = (lax.axis_index("dst") == 0) & (sub >= 4)
    for b in range(blocks):
        rows = slice(b * chunks, (b + 1) * chunks)
        split_ref[rows, :] = jnp.where(own_rows, split_ref[rows, :], shared)
    half = out_ref.at[pl.ds(start, common)]
    pairs = []
    for b in range(blocks):
        pairs.append((half, out_any.at[pl.ds(b * share, common)]))
        pairs.append((split_ref.at[pl.ds(b * chunks, chunks)], out_any.at[pl.ds(b * share + common, chunks)]))
    run_copies(whole_copies(pairs, sem))


def inverse_row(n, slots):
    if n < slots - 4:
        return ROWS + 2 * slots + n
    return 2 * (ROWS + 3 * slots) - slots + n


def graph_kernel(
    weight_ref, feature_any, succ_any, valid_any, border_any, anchor_any, out_ref, reward_ref,
    feature_ref, succ_ref, valid_ref, border_ref, anchor_ref, part_ref, split_ref, sem
):
    run_copies(
        whole_copies(
            [
                (feature_any, feature_ref),
                (succ_any, succ_ref),
                (valid_any, valid_ref),
                (border_any, border_ref),
                (anchor_any, anchor_ref),
            ],
            sem,
        )
    )
    turns, width = succ_ref.shape
    chunks = width // LANES
    edges = turns * chunks
    part_ref[edges : edges + 8, :] = jnp.zeros((8, LANES), jnp.float32)
    part_ref[edges : edges + 4, :] = border_ref[...].astype(jnp.float32)
    blocks = anchor_ref.shape[0]
    split_ref[0:8, :] = jnp.zeros((8, LANES), jnp.float32)
    first_core = lax.axis_index("dst") == 0
    for q in range(chunks):
        cols = slice(q * LANES, (q + 1) * LANES)
        cost = weight_ref[0] * feature_ref[0, :, cols].astype(jnp.float32)
        for f in range(1, feature_ref.shape[0]):
            cost = cost + weight_ref[f] * feature_ref[f, :, cols].astype(jnp.float32)
        reward_ref[:, cols] = -cost
        masked = jnp.where(valid_ref[:, cols] == 1, -cost, NEG)
        turn_to = succ_ref[:, cols].astype(jnp.float32)
        part_ref[pl.ds(q, turns, chunks), :] = jnp.where(first_core, masked, turn_to)
        split_ref[pl.ds(8 + q, blocks, chunks), :] = anchor_ref[:, cols]
    size = part_ref.shape[0]
    lists = part_ref[edges:size, :]
    upper = lax.broadcasted_iota(jnp.int32, (8, LANES), 0) < 4
    for b in range(blocks):
        out_ref[b * size : b * size + edges, :] = part_ref[0:edges, :]
        own = split_ref[8 + b * chunks : 16 + b * chunks, :]
        lower = split_ref[4 + b * chunks : 12 + b * chunks, :]
        mixed = jnp.where(upper, lists, lower)
        out_ref[b * size + edges : (b + 1) * size, :] = jnp.where(first_core, mixed, own)


def regroup_kernel(pieces_ref, out_ref):
    halves, rows = out_ref.shape[:2]
    size = pieces_ref.shape[0] // (8 * halves)
    for h in range(halves):

        def one_row(i, carry, h=h):
            out_ref[h, i] = of_blocks(pieces_ref, h, i, size)
            return carry

        lax.fori_loop(0, rows, one_row, 0, unroll=8)


def weigh(out):
    top = functools.reduce(jnp.maximum, out)
    raised = [jnp.exp(score - top) for score in out]
    return top, raised, functools.reduce(jnp.add, raised)


def weighed_turns(values, reward, index, h, q, turns, chunks):
    tables = [values[h, r] for r in range(chunks + 4)]
    out = []
    for a in range(turns):
        rows = tables if a else tables[:chunks]
        out.append(reward[h, a * chunks + q] + table_gather(rows, index[h, a * chunks + q]))
    return weigh(out)


def policy_kernel(values_ref, reward_ref, index_ref, raised_ref, max_ref, inv_ref):
    halves, chunks = max_ref.shape[:2]
    turns = reward_ref.shape[1] // chunks

    def one_chunk(q, inner):
        for h in range(halves):
            top, raised, total = weighed_turns(values_ref, reward_ref, index_ref, h, q, turns, chunks)
            max_ref[h, q] = top
            inv_ref[h, q] = 1.0 / total
            for a in range(turns):
                raised_ref[h, a * chunks + q] = raised[a]
        return inner

    lax.fori_loop(0, chunks, one_chunk, 0, unroll=chunks)


def value_kernel(
    grid_x, dest_ref, mine_ref, other_ref, ext_ref, reward, index, border, side_pad, spare_ref
):
    halves = ext_ref.shape[0]
    blocks = 8 * halves
    chunks = ext_ref.shape[1] - 4
    edges = reward.shape[1]
    turns = edges // chunks
    per_block = chunks * LANES
    dest = renumbered(dest_ref[own_block(grid_x)], per_block, blocks, grid_x)
    side_pad[...] = jnp.zeros_like(side_pad)
    sub = lax.broadcasted_iota(jnp.int32, (8, LANES), 0)
    lane = lax.broadcasted_iota(jnp.int32, (8, LANES), 1)
    dest_block, dest_place = lax.div(dest, per_block), lax.rem(dest, per_block)

    def unpack(first, second):
        for h in range(halves):

            def rows(i, carry, h=h):
                reward[h, i] = first[h, i]
                index[h, i] = second[h, i].astype(jnp.int32)
                return carry

            lax.fori_loop(0, edges, rows, 0, unroll=8)
            for side in range(4):
                border[h, side] = first[h, edges + side].astype(jnp.int32)

    by_core(unpack, mine_ref, other_ref)
    for h in range(halves):
        for side in range(4):
            found = (border[h, side] == dest_place) & (h * 8 + sub == dest_block)
            entry = jnp.max(jnp.where(found, lane + 1, 0).astype(jnp.float32), axis=1, keepdims=True)
            side_pad[side, 8 + 8 * h : 16 + 8 * h, :] = jnp.broadcast_to(entry, (8, LANES))
    shifts = ((1, -1), (0, 1), (3, -grid_x), (2, grid_x))

    def shown(h, side):
        facing, by = shifts[side]
        start = 8 + 8 * h + by
        return side_pad[facing, start : start + 8, :]

    def dest_index(h):
        where = jnp.where(h * 8 + sub == dest_block, dest_place, -1)
        for side in range(4):
            entry = shown(h, side).astype(jnp.int32)
            where = jnp.where(entry > 0, per_block + side * LANES + entry - 1, where)
        return where

    def bring_halo(values):
        for h in range(halves):
            table = [values[h, q] for q in range(chunks)]
            for side in range(4):
                side_pad[side, 8 + 8 * h : 16 + 8 * h, :] = table_gather(table, border[h, side])
        for h in range(halves):
            for side in range(4):
                values[h, chunks + side] = shown(h, side)

    def store_value(h, q, top, total, into):
        value = top + jnp.log(total)
        into[h, q] = jnp.where(target_mask(dest, h, q, per_block), 0.0, value)

    wanted = [dest_index(h) for h in range(halves)]

    def first_chunk(q, inner):
        for h in range(halves):
            out = []
            for a in range(turns):
                before = jnp.where(index[h, a * chunks + q] == wanted[h], 0.0, -START_COST)
                out.append(reward[h, a * chunks + q] + before)
            top, _, total = weigh(out)
            store_value(h, q, top, total, spare_ref)
        return inner

    lax.fori_loop(0, chunks, first_chunk, 0, unroll=2)

    def backup(values, into):
        bring_halo(values)

        def one_chunk(q, inner):
            for h in range(halves):
                top, _, total = weighed_turns(values, reward, index, h, q, turns, chunks)
                store_value(h, q, top, total, into)
            return inner

        lax.fori_loop(0, chunks, one_chunk, 0, unroll=chunks)

    def two_backups(step, carry):
        backup(spare_ref, ext_ref)
        backup(ext_ref, spare_ref)
        return carry

    lax.fori_loop(0, (HORIZON - 2) // 2, two_backups, 0)
    backup(spare_ref, ext_ref)
    bring_halo(ext_ref)


def push_kernel(
    grid_x, scale, dest_ref, mine_ref, other_ref, graph_mine, graph_other, ext_ref, raised_ref, max_ref,
    inv_ref, keep_ref, send_ref, counts, ends, order, values, source, slot, going, policy, flows, back, scaled, total, arrived, side_pad, raw
):
    halves = ext_ref.shape[0]
    blocks = 8 * halves
    share = mine_ref.shape[1]
    chunks = max_ref.shape[1]
    edges = raised_ref.shape[1]
    turns = edges // chunks
    per_block = chunks * LANES
    slots = chunks + 4
    dest = renumbered(dest_ref[own_block(grid_x)], per_block, blocks, grid_x)
    core = lax.axis_index("dst")
    side_pad[...] = jnp.zeros_like(side_pad)

    def unpack(first, second):
        for h in range(halves):
            for n in range(slots):
                ends[h, n] = first[h, ROWS + n]
                order[h, n] = first[h, ROWS + slots + n].astype(jnp.int32)
                row = inverse_row(n, slots)
                inverse = (first[h, row] if row < share else second[h, row - share]).astype(jnp.int32)
                values[h, n] = lane_gather(ext_ref[h, n], inverse)

            def rows(r, carry, h=h):
                source[h, r] = first[h, r].astype(jnp.int32)
                policy[h, r] = second[h, r]
                return carry

            lax.fori_loop(0, ROWS, rows, 0, unroll=6)
            for r in range(ROWS, DEPTH):
                source[h, r] = jnp.zeros((8, LANES), jnp.int32)
                policy[h, r] = jnp.zeros((8, LANES), jnp.float32)
            for n in range(4 * chunks):
                back[h, n] = second[h, ROWS + n].astype(jnp.int32) - 1

    by_core(unpack, mine_ref, other_ref)

    def first_anchors():
        for h in range(halves):
            for q in range(4):
                total[h, q] = graph_mine[h, edges + 4 + q]
                total[h, 4 + q] = mine_ref[h, share - 4 + q]

    def second_anchors():
        for h in range(halves):
            for q in range(chunks):
                total[h, q] = graph_mine[h, edges + q]

    pl.when(core == 0)(first_anchors)
    pl.when(core != 0)(second_anchors)
    deepest = jnp.max(functools.reduce(jnp.maximum, [ends[h, slots - 1] for h in range(halves)]))
    deepest = deepest.astype(jnp.int32)
    fits = deepest <= ROWS
    steps = jnp.where(deepest <= USUAL, USUAL // STEP, DEPTH // STEP)
    shifts = ((1, -1), (0, 1), (3, -grid_x), (2, grid_x))

    def shown(h, side):
        facing, by = shifts[side]
        start = 8 + 8 * h + by
        return side_pad[facing, start : start + 8, :]

    @pl.when(jnp.logical_not(fits))
    def _():
        for h in range(halves):
            for n in range(slots):
                order[h, n] = lax.broadcasted_iota(jnp.int32, (8, LANES), 1)

    for h in range(halves):
        for side in range(4):
            side_pad[side, 8 + 8 * h : 16 + 8 * h, :] = order[h, chunks + side].astype(jnp.float32)
    for h in range(halves):
        for side in range(4):
            lanes = shown(h, side).astype(jnp.int32)
            for q in range(chunks):
                entry = back[h, side * chunks + q]
                back[h, side * chunks + q] = jnp.where(
                    entry >= 0, lane_gather(lanes, jnp.maximum(entry, 0)), -1
                )

    def prepare_rows(rows):
        row_before = [None] * halves
        for i, r in enumerate(rows):
            for h in range(halves):
                src = source[h, r]
                place = jnp.asarray(r).astype(jnp.float32)
                row = functools.reduce(
                    jnp.add, [jnp.where(ends[h, n] <= place, 1, 0) for n in range(slots)]
                )
                slot[h, r] = row
                if i:
                    going[h, r] = jnp.where(row == row_before[h], 1.0, 0.0)
                row_before[h] = row
                bits = [(row & (1 << n)) != 0 for n in range(4)]
                picked = tree_select([values[h, n] for n in range(slots)], bits)
                top = table_gather([max_ref[h, q] for q in range(chunks)], src)
                policy[h, r] = jnp.exp(policy[h, r] + picked - top)

    def prepare_step(t, carry):
        prepare_rows([t * STEP + i for i in range(STEP)])
        return carry

    usual = deepest <= USUAL
    pl.when(usual)(lambda: prepare_rows(range(USUAL)))
    lax.fori_loop(0, jnp.where(usual, 0, steps), prepare_step, 0)
    for h in range(halves):
        for q in range(chunks):
            first = jnp.where(target_mask(dest, h, q, per_block), 0.0, total[h, q])
            total[h, q] = first
            scaled[h, q] = first * inv_ref[h, q]

    @pl.when(jnp.logical_not(fits))
    def _():
        def keep_turns(first, second):
            for h in range(halves):

                def rows(e, carry, h=h):
                    raw[h, e] = second[h, e].astype(jnp.int32)
                    return carry

                lax.fori_loop(0, edges, rows, 0)

        by_core(keep_turns, graph_mine, graph_other)

    zero = jnp.zeros((8, LANES), jnp.float32)

    def keep(h):
        for side in range(4):
            side_pad[side, 8 + 8 * h : 16 + 8 * h, :] = arrived[h, chunks + side]

    def add_flow(acc, row, flow):
        return [acc[n] + jnp.where(row == n, flow, 0.0) for n in range(slots)]

    def sum_arranged():
        for h in range(halves):
            for n in range(slots):
                arrived[h, n] = zero

        def one_step(t, carry):
            tables = [[scaled[h, q] for q in range(chunks)] for h in range(halves)]
            step_sums = [[zero] * slots for h in range(halves)]
            so_far = [None] * halves
            for i in range(STEP):
                r = t * STEP + i
                for h in range(halves):
                    flow = table_gather(tables[h], source[h, r]) * policy[h, r]
                    so_far[h] = flow + going[h, r] * so_far[h] if i else flow
                    row = slot[h, r]
                    step_sums[h] = [jnp.where(row == n, so_far[h], step_sums[h][n]) for n in range(slots)]
            for h in range(halves):
                for n in range(slots):
                    arrived[h, n] = arrived[h, n] + step_sums[h][n]
            return carry

        def usual_rows():
            for h in range(halves + 1):
                sums = [zero] * slots
                table = [scaled[h, q] for q in range(chunks)] if h < halves else None
                for r in range(USUAL):
                    if h < halves:
                        flow = table_gather(table, source[h, r]) * policy[h, r]
                        so_far = flow + going[h, r] * so_far if r else flow
                        flows[h, r] = so_far
                    if h:
                        row, summed = slot[h - 1, r], flows[h - 1, r]
                        sums = [jnp.where(row == n, summed, sums[n]) for n in range(slots)]
                if h:
                    for n in range(slots):
                        arrived[h - 1, n] = sums[n]

        pl.when(usual)(usual_rows)
        lax.fori_loop(0, jnp.where(usual, 0, steps), one_step, 0)
        for h in range(halves):
            keep(h)

    def sum_turned():
        lane = lax.broadcasted_iota(jnp.int32, (8, LANES), 1)
        for h in range(halves):

            def one_edge_row(e, acc, h=h):
                flow = scaled[h, lax.rem(e, chunks)] * raised_ref[h, e]
                where = raw[h, e]

                def one_turn(k, state):
                    flow, where, acc = state[0], state[1], list(state[2:])
                    here = jnp.where((where & (LANES - 1)) == lane, where >> 7, -1)
                    acc = add_flow(acc, here, flow)
                    return (pltpu.roll(flow, 1, 1), pltpu.roll(where, 1, 1), *acc)

                return tuple(lax.fori_loop(0, LANES, one_turn, (flow, where, *acc))[2:])

            for n, value in enumerate(lax.fori_loop(0, edges, one_edge_row, (zero,) * slots)):
                arrived[h, n] = value
            keep(h)

    def push(round_index, carry):
        pl.when(fits)(sum_arranged)
        pl.when(jnp.logical_not(fits))(sum_turned)
        for h in range(halves):
            landed = [shown(h, side) for side in range(4)]
            for q in range(chunks):
                value = lane_gather(arrived[h, q], order[h, q])
                for side in range(4):
                    entry = back[h, side * chunks + q]
                    got = lane_gather(landed[side], jnp.maximum(entry, 0))
                    value = value + jnp.where(entry >= 0, got, 0.0)
                value = jnp.where(target_mask(dest, h, q, per_block), 0.0, value)
                total[h, q] = total[h, q] + value
                scaled[h, q] = value * inv_ref[h, q]
        return carry

    lax.fori_loop(0, HORIZON - 1, push, 0)
    rows_out = edges // 2
    apart = counts.shape[1] // blocks
    for h in range(halves):
        for q in range(chunks):
            weight = total[h, q] * inv_ref[h, q] * scale
            for part, piece in ((core, 0), (1 - core, 1)):
                for a in range(turns // 2):
                    value = weight * raised_ref[h, (part * (turns // 2) + a) * chunks + q]
                    start = h * 8 * apart + a * chunks + q
                    counts[piece, pl.ds(start, 8, stride=apart), :] = value
    for piece, out_ref in ((0, keep_ref), (1, send_ref)):
        for b in range(blocks):
            out_ref[b * rows_out : (b + 1) * rows_out, :] = counts[
                piece, b * apart : b * apart + rows_out, :
            ]


VMEM_SPEC = pl.BlockSpec(memory_space=pltpu.VMEM)
SMEM_SPEC = pl.BlockSpec(memory_space=pltpu.SMEM)
HBM_SPEC = pl.BlockSpec(memory_space=pltpu.HBM)
PARAMS = pltpu.CompilerParams(vmem_limit_bytes=48 * 1024 * 1024)


def f32(*shape):
    return jax.ShapeDtypeStruct(shape, jnp.float32)


def call_graph(cost_weights, features, successors, turn_valid, border_lists, anchors):
    turns, width = successors.shape
    blocks = anchors.shape[0]
    chunks = width // LANES
    rows = turns * chunks + 8
    return pl.pallas_call(
        graph_kernel,
        out_shape=(f32(blocks * rows, LANES), f32(turns, width)),
        in_specs=[SMEM_SPEC] + [HBM_SPEC] * 5,
        out_specs=(VMEM_SPEC, VMEM_SPEC),
        scratch_shapes=[
            pltpu.VMEM(features.shape, features.dtype),
            pltpu.VMEM(successors.shape, jnp.int32),
            pltpu.VMEM(turn_valid.shape, jnp.int32),
            pltpu.VMEM(border_lists.shape, jnp.int32),
            pltpu.VMEM(anchors.shape, jnp.float32),
            pltpu.VMEM((rows, LANES), jnp.float32),
            pltpu.VMEM((blocks * chunks + 8, LANES), jnp.float32),
            pltpu.SemaphoreType.DMA((5,)),
        ],
        compiler_params=pltpu.CompilerParams(vmem_limit_bytes=63 * 1024 * 1024),
        name="own_graph",
    )(cost_weights, features, successors, turn_valid, border_lists, anchors)


def call_arrange(successors, turn_valid, border_lists, anchors, reward):
    chunks = successors.shape[1] // LANES
    share = ROWS + 3 * (chunks + 4)
    blocks = anchors.shape[0]
    return pl.pallas_call(
        arrange_kernel,
        out_shape=f32(blocks * share, LANES),
        in_specs=[HBM_SPEC] * 4 + [VMEM_SPEC],
        out_specs=HBM_SPEC,
        scratch_shapes=[
            pltpu.VMEM(successors.shape, jnp.int32),
            pltpu.VMEM(turn_valid.shape, jnp.int32),
            pltpu.VMEM(border_lists.shape, jnp.int32),
            pltpu.VMEM(anchors.shape, jnp.float32),
            pltpu.VMEM((blocks * chunks, LANES), jnp.float32),
            pltpu.VMEM((2 * share, LANES), jnp.float32),
            *[pltpu.VMEM((16, LANES), jnp.float32)] * 5,
            pltpu.VMEM((8, LANES), jnp.float32),
            pltpu.VMEM(successors.shape, jnp.float32),
            pltpu.VMEM(successors.shape, jnp.float32),
            pltpu.VMEM(successors.shape[::-1], jnp.float32),
            pltpu.VMEM((5 * RANKS, LANES), jnp.float32),
            pltpu.SemaphoreType.DMA((2 * blocks,)),
        ],
        compiler_params=PARAMS,
        cost_estimate=pl.CostEstimate(flops=4_000_000_000, bytes_accessed=400_000, transcendentals=0),
        name="arrange_turns",
    )(successors, turn_valid, border_lists, anchors, reward)


def call_regroup(pieces, blocks):
    return pl.pallas_call(
        regroup_kernel,
        out_shape=f32(blocks // 8, pieces.shape[0] // blocks, 8, LANES),
        in_specs=[VMEM_SPEC],
        out_specs=VMEM_SPEC,
        compiler_params=PARAMS,
        name="regroup",
    )(pieces)


def call_values(destinations, mine, other, blocks, grid_x, turns, chunks):
    halves = blocks // 8
    edges = turns * chunks
    rows = (halves, edges, 8, LANES)
    return pl.pallas_call(
        functools.partial(value_kernel, grid_x),
        out_shape=(
            f32(halves, chunks + 4, 8, LANES),
            f32(*rows),
            jax.ShapeDtypeStruct(rows, jnp.int32),
        ),
        in_specs=[SMEM_SPEC, VMEM_SPEC, VMEM_SPEC],
        out_specs=(VMEM_SPEC,) * 3,
        scratch_shapes=[
            pltpu.VMEM((halves, 4, 8, LANES), jnp.int32),
            pltpu.VMEM((4, blocks + 16, LANES), jnp.float32),
            pltpu.VMEM((halves, chunks + 4, 8, LANES), jnp.float32),
        ],
        compiler_params=PARAMS,
        cost_estimate=pl.CostEstimate(flops=40_000_000, bytes_accessed=40_000_000, transcendentals=2_000_000),
        name="soft_values",
    )(destinations, mine, other)


def call_policy(ext, reward, index):
    halves, edges = reward.shape[:2]
    chunks = ext.shape[1] - 4
    return pl.pallas_call(
        policy_kernel,
        out_shape=(f32(*reward.shape), f32(halves, chunks, 8, LANES), f32(halves, chunks, 8, LANES)),
        in_specs=[VMEM_SPEC] * 3,
        out_specs=(VMEM_SPEC,) * 3,
        compiler_params=PARAMS,
        cost_estimate=pl.CostEstimate(flops=5_000_000, bytes_accessed=5_000_000, transcendentals=200_000),
        name="policy",
    )(ext, reward, index)


def call_push(destinations, mine, other, graph_mine, graph_other, ext, raised, top, inv, grid_x, scale):
    halves, edges = raised.shape[:2]
    blocks = 8 * halves
    chunks = top.shape[1]

    def vmem(rows, dtype=jnp.float32):
        return pltpu.VMEM((halves, rows, 8, LANES), dtype)

    return pl.pallas_call(
        functools.partial(push_kernel, grid_x, scale),
        out_shape=(f32(blocks * edges // 2, LANES),) * 2,
        in_specs=[SMEM_SPEC] + [VMEM_SPEC] * 8,
        out_specs=(VMEM_SPEC,) * 2,
        scratch_shapes=[
            pltpu.VMEM((2, blocks * padded_rows(edges // 2), LANES), jnp.float32),
            vmem(chunks + 4),
            vmem(chunks + 4, jnp.int32),
            vmem(chunks + 4),
            vmem(DEPTH, jnp.int32),
            vmem(DEPTH, jnp.int32),
            vmem(DEPTH),
            vmem(DEPTH),
            vmem(USUAL),
            vmem(4 * chunks, jnp.int32),
            vmem(chunks),
            vmem(chunks),
            vmem(chunks + 4),
            pltpu.VMEM((4, blocks + 16, LANES), jnp.float32),
            vmem(edges, jnp.int32),
        ],
        compiler_params=PARAMS,
        name="push_mass",
    )(destinations, mine, other, graph_mine, graph_other, ext, raised, top, inv)


def to_blocks(array):
    return lax.all_to_all(array, BLOCK_AXES, 0, 0, tiled=True)


def other_core(array):
    return lax.ppermute(array, "dst", [(0, 1), (1, 0)])


def per_destination(
    features, cost_weights, successors, turn_valid, border_lists, destinations, anchors, demo_counts
):
    turns, own_count = successors.shape
    chunks = own_count // LANES
    edges = turns * chunks
    grid_x = lax.axis_size("gx")
    blocks = lax.axis_size("gy") * grid_x
    groups = lax.axis_size("dst")
    pieces, reward = call_graph(cost_weights, features, successors, turn_valid, border_lists, anchors)
    graph = to_blocks(pieces)
    arranged = call_arrange(successors, turn_valid, border_lists, anchors, reward)
    core = lax.axis_index("dst")
    demo_term = jnp.where(turn_valid == 1, demo_counts, 0).astype(jnp.float32) / 3.0
    own_feats = lax.dynamic_slice_in_dim(features, core * (turns // 2), turns // 2, axis=1)
    first_core, own_feats, demo_term, arranged = lax.optimization_barrier(
        (core == 0, own_feats, demo_term, arranged)
    )
    graph = lax.optimization_barrier((graph, arranged))[0]
    arranged = to_blocks(arranged)
    graph = call_regroup(graph, blocks)
    graph = (graph, other_core(graph))
    ext, reward, index = call_values(destinations, *graph, blocks, grid_x, turns, chunks)
    arranged, ext = lax.optimization_barrier((arranged, ext))
    arranged = call_regroup(arranged, blocks)
    arranged, ext = lax.optimization_barrier((arranged, ext))
    arranged = (arranged, other_core(arranged))
    values = (ext, *call_policy(ext, reward, index))
    scale = 1.0 / (anchors.shape[0] * groups * HORIZON)
    kept, sent = call_push(destinations, *arranged, *graph, *values, grid_x, scale)
    halved = (kept + other_core(sent)).reshape(blocks, edges // 2, LANES)
    half = jnp.sum(to_blocks(halved), axis=0)
    other = other_core(half)
    part = (turns // 2, own_count)
    own_gap = lax.dynamic_slice_in_dim(demo_term, core * part[0], part[0]) - half.reshape(part)
    own_feats = own_feats.astype(jnp.float32)
    block_term = jnp.sum(own_gap[None] * own_feats, axis=(1, 2)) / (own_count * blocks)
    visits = jnp.concatenate([jnp.where(first_core, half, other), jnp.where(first_core, other, half)])
    count_gap = demo_term - visits.reshape(turns, own_count)
    terms = jnp.broadcast_to(block_term, (groups * blocks, 1, block_term.shape[0]))
    terms = lax.all_to_all(terms, (*BLOCK_AXES, "dst"), 0, 0, tiled=True)
    terms, count_gap = lax.optimization_barrier((terms, count_gap))
    return count_gap, jnp.sum(terms, axis=(0, 1))


def passed_along(array, axis, by):
    length = lax.axis_size(axis)
    pairs = [(i, i + by) for i in range(length) if 0 <= i + by < length]
    return lax.ppermute(array, axis, pairs)


def bring_values(values, border_lists):
    outgoing = values[:, border_lists]
    north_part = passed_along(outgoing[:, 1], "gx", 1)
    south_part = passed_along(outgoing[:, 0], "gx", -1)
    west_part = passed_along(outgoing[:, 3], "gy", 1)
    east_part = passed_along(outgoing[:, 2], "gy", -1)
    return jnp.concatenate([north_part, south_part, west_part, east_part], axis=1)


def return_flow(arrived, border_lists, own_count, border_width):
    local_part = arrived[:, :own_count]
    halo_part = arrived[:, own_count:].reshape(arrived.shape[0], 4, border_width)
    from_south = passed_along(halo_part[:, 0], "gx", -1)
    from_north = passed_along(halo_part[:, 1], "gx", 1)
    from_east = passed_along(halo_part[:, 2], "gy", -1)
    from_west = passed_along(halo_part[:, 3], "gy", 1)
    returned = jnp.stack([from_north, from_south, from_west, from_east], axis=1)
    return local_part.at[:, border_lists].add(returned)


def select_cells(cells, flat_index, turn_shape):
    picked = jnp.take(cells, flat_index, axis=1)
    return picked.reshape(cells.shape[0], turn_shape[0], turn_shape[1])


def turn_scores(values, halo_cells, reward, flat_turns, usable):
    extended = jnp.concatenate([values, halo_cells], axis=1)
    scores = reward[None] + select_cells(extended, flat_turns, usable.shape)
    return jnp.where(usable[None], scores, NEG)


def per_block(
    features, cost_weights, successors, turn_valid, border_lists, destinations, anchors, demo_counts
):
    own_count = successors.shape[1]
    border_width = border_lists.shape[1]
    dest_count = anchors.shape[0]
    slot_total = own_count + 4 * border_width
    block_index = lax.axis_index("gx") * lax.axis_size("gy") + lax.axis_index("gy")
    positions = jnp.arange(own_count, dtype=jnp.int32)
    is_target = positions[None, :] == (destinations - block_index * own_count)[:, None]
    usable = turn_valid == 1
    feats = features.astype(jnp.float32)
    reward = -jnp.sum(feats * cost_weights[:, None, None], axis=0)
    flat_turns = successors.reshape(-1)
    values = jnp.where(is_target, 0.0, -START_COST).astype(jnp.float32)
    for round_index in range(HORIZON):
        halo_cells = bring_values(values, border_lists)
        scores = turn_scores(values, halo_cells, reward, flat_turns, usable)
        row_max = jnp.max(scores, axis=1)
        new_values = row_max + jnp.log(jnp.sum(jnp.exp(scores - row_max[:, None]), axis=1))
        values = jnp.where(is_target, 0.0, new_values)
    halo_cells = bring_values(values, border_lists)
    scores = turn_scores(values, halo_cells, reward, flat_turns, usable)
    row_max = jnp.max(scores, axis=1)
    raised = jnp.exp(scores - row_max[:, None])
    policy = raised / jnp.sum(raised, axis=1, keepdims=True)
    mass_now = jnp.where(is_target, 0.0, anchors)
    turn_counts = jnp.zeros(successors.shape, jnp.float32)
    for round_index in range(HORIZON):
        turn_flow = mass_now[:, None, :] * policy
        turn_counts = turn_counts + jnp.sum(turn_flow, axis=0)
        if round_index + 1 < HORIZON:
            arrived = (
                jnp.zeros((dest_count, slot_total), jnp.float32)
                .at[:, flat_turns]
                .add(turn_flow.reshape(dest_count, -1))
            )
            landed = return_flow(arrived, border_lists, own_count, border_width)
            mass_now = jnp.where(is_target, 0.0, landed)
    local_visits = turn_counts / (dest_count * lax.axis_size("dst") * HORIZON)
    visits = lax.psum(local_visits, "dst")
    demo_term = jnp.where(usable, demo_counts, 0).astype(jnp.float32) / 3.0
    count_gap = demo_term - visits
    total_segments = own_count * lax.axis_size("gx") * lax.axis_size("gy")
    own_gap = demo_term / lax.axis_size("dst") - local_visits
    block_term = jnp.sum(own_gap[None] * feats, axis=(1, 2)) / total_segments
    gradient = lax.psum(block_term, ("gx", "gy", "dst"))
    return (count_gap, gradient)


def local(features, cost_weights, successors, turn_valid, border_lists, destinations, anchors, demo_counts):
    args = (
        features, cost_weights, successors, turn_valid, border_lists, destinations, anchors, demo_counts
    )
    blocks = lax.axis_size("gx") * lax.axis_size("gy")
    fits = (
        anchors.shape[0] == blocks
        and blocks % 8 == 0
        and lax.axis_size("dst") == 2
        and lax.axis_size("gx") in (2, 4, 8)
        and lax.axis_size("gy") in (2, 4, 8)
        and successors.shape[1] == 8 * LANES
        and border_lists.shape[1] == LANES
        and successors.shape[0] == 8
    )
    return per_destination(*args) if fits else per_block(*args)


def solution(mesh):
    in_specs = (
        P(None, None, ("gx", "gy")),
        P(),
        P(None, ("gx", "gy")),
        P(None, ("gx", "gy")),
        P(None, ("gx", "gy")),
        P("dst"),
        P("dst", ("gx", "gy")),
        P(None, ("gx", "gy")),
    )
    out_specs = (P(None, ("gx", "gy")), P())
    return jax.shard_map(local, mesh=mesh, in_specs=in_specs, out_specs=out_specs, check_vma=False)
```

```python
import functools

import jax
import jax.numpy as jnp
from jax import lax
from jax.experimental import pallas as pl
from jax.experimental.pallas import tpu as pltpu
from jax.sharding import PartitionSpec as P

HORIZON = 8
NEG = -1e30
START_COST = 100.0
LANES = 128
ROWS = 60
RANKS = -(-ROWS // 16) * 16
STEP = 14
USUAL = 56
DEPTH = -(-ROWS // STEP) * STEP
BLOCK_AXES = ("gy", "gx")

LANE_PICK = lax.GatherDimensionNumbers(
    offset_dims=(),
    collapsed_slice_dims=(1,),
    start_index_map=(1,),
    operand_batching_dims=(0,),
    start_indices_batching_dims=(0,),
)


def lane_gather(table, index):
    return lax.gather(
        table,
        index[..., None],
        LANE_PICK,
        (1, 1),
        mode=lax.GatherScatterMode.PROMISE_IN_BOUNDS,
    )


def tree_select(picked, bits):
    level = list(picked)
    for bit in bits:
        if len(level) == 1:
            break
        nxt = []
        for n in range(0, len(level), 2):
            if n + 1 < len(level):
                nxt.append(jnp.where(bit, level[n + 1], level[n]))
            else:
                nxt.append(level[n])
        level = nxt
    return level[0]


def row_bits(index, count):
    return [(index & (LANES << i)) != 0 for i in range(count)]


def table_gather(table_rows, index):
    lane = index & (LANES - 1)
    bits = row_bits(index, max(len(table_rows) - 1, 1).bit_length())
    return tree_select([lane_gather(row, lane) for row in table_rows], bits)


def run_copies(copies):
    for copy in copies:
        copy.start()
    for copy in copies:
        copy.wait()


def of_blocks(ref, half, row, per_block):
    return ref[pl.ds(half * 8 * per_block + row, 8, stride=per_block), :]


def whole_copies(pairs, sem):
    return [pltpu.make_async_copy(src, dst, sem.at[n]) for n, (src, dst) in enumerate(pairs)]


def by_core(what, mine, other):
    first = lax.axis_index("dst") == 0
    pl.when(first)(lambda: what(mine, other))
    pl.when(jnp.logical_not(first))(lambda: what(other, mine))


def own_block(grid_x):
    return lax.axis_index("gy") * grid_x + lax.axis_index("gx")


def renumbered(segment, per_block, blocks, grid_x):
    grid_y = blocks // grid_x
    block, place = lax.div(segment, per_block), lax.rem(segment, per_block)
    return (lax.rem(block, grid_y) * grid_x + lax.div(block, grid_y)) * per_block + place


def padded_rows(rows):
    tiles = -(-rows // 8)
    return (tiles + 1 - tiles % 2) * 8


def target_mask(dest, half, chunk, per_block):
    sub = lax.broadcasted_iota(jnp.int32, (8, LANES), 0)
    lane = lax.broadcasted_iota(jnp.int32, (8, LANES), 1)
    return (half * 8 + sub) * per_block + chunk * LANES + lane == dest


def arrange_kernel(
    succ_any, valid_any, border_any, anchor_any, reward_ref, out_any,
    succ_ref, valid_ref, border_ref, anchor_ref, split_ref, out_ref, count_ref, first_ref, order_ref, inverse_ref, placed_ref,
    pair_ref, lane_ref, code_ref, column_ref, acc_ref, sem
):
    run_copies(
        whole_copies(
            [
                (succ_any, succ_ref),
                (valid_any, valid_ref),
                (border_any, border_ref),
                (anchor_any, anchor_ref),
            ],
            sem,
        )
    )
    turns, width = succ_ref.shape
    chunks = width // LANES
    slots = chunks + 4
    step = 2 * LANES
    tops = 16
    square = (LANES, LANES)
    down = lax.broadcasted_iota(jnp.int32, square, 0)
    along = lax.broadcasted_iota(jnp.int32, square, 1)
    down_f, along_f = down.astype(jnp.float32), along.astype(jnp.float32)
    before = down < along
    unit = jnp.where(down == along, 1.0, 0.0)
    lane_row = lax.broadcasted_iota(jnp.int32, (LANES, step), 0)
    top_row = lax.broadcasted_iota(jnp.int32, (tops, step), 0)
    rank_row = lax.broadcasted_iota(jnp.int32, (RANKS, step), 0).astype(jnp.float32)
    last_dims = (((1,), (1,)), ((), ()))

    def product(left, right):
        return lax.dot_general(left, right, last_dims, preferred_element_type=jnp.float32)

    def columns(rows):
        return lax.dot_general(
            unit, rows, last_dims, precision=lax.Precision.HIGHEST, preferred_element_type=jnp.float32
        )

    def summed_down(array):
        return jnp.sum(array, axis=0, keepdims=True)

    def place_of(row, col):
        return summed_down(jnp.where((col > row) | ((col == row) & before), 1.0, 0.0))

    def count(a, total):
        for c in range(width // step):
            cols = slice(c * step, (c + 1) * step)
            u = succ_ref[pl.ds(a, 1), cols]
            low = jnp.where(valid_ref[pl.ds(a, 1), cols] == 1, u & (LANES - 1), -1)
            hot_low = jnp.where(low == lane_row, 1.0, 0.0).astype(jnp.bfloat16)
            hot_top = jnp.where((u >> 7) == top_row, 1.0, 0.0).astype(jnp.bfloat16)
            total = total + product(hot_top, hot_low)
        return total

    counts = lax.fori_loop(0, turns, count, jnp.zeros((tops, LANES), jnp.float32), unroll=2)
    count_columns = columns(counts)
    out_ref[...] = jnp.zeros_like(out_ref)
    for ref in (count_ref, first_ref, order_ref, inverse_ref, placed_ref, pair_ref):
        ref[...] = jnp.zeros_like(ref)
    for n in range(slots):
        i = n if n < chunks else n - chunks
        place = place_of(counts[n : n + 1, :], count_columns[:, n : n + 1])
        place = place if i % 2 == 0 else (LANES - 1.0) - place
        if (i // 2) % 2:
            place = jnp.where(place >= LANES // 2, place - LANES // 2, place + LANES // 2)
        first_ref[n : n + 1, :] = place
    first_columns = columns(first_ref[...])
    for n in range(slots):
        hit = first_columns[:, n : n + 1] == along_f
        inverse_ref[n : n + 1, :] = summed_down(jnp.where(hit, down_f, 0.0))
        placed_ref[n : n + 1, :] = summed_down(jnp.where(hit, count_columns[:, n : n + 1], 0.0))
    local = summed_down(placed_ref[0:chunks, :])
    room = -summed_down(placed_ref[chunks:tops, :])
    pair_ref[0:1, :] = local
    pair_ref[1:2, :] = room
    pair = columns(pair_ref[...])
    local_place, room_place = place_of(local, pair[:, 0:1]), place_of(room, pair[:, 1:2])
    pair_ref[0:1, :] = local_place
    pair_ref[1:2, :] = room_place
    pair = columns(pair_ref[...])
    goes = summed_down(jnp.where(pair[:, 1:2] == local_place, down_f, 0.0))
    comes = summed_down(jnp.where(pair[:, 0:1] == room_place, down_f, 0.0))
    full = (chunks, LANES)
    comes = jnp.broadcast_to(comes, full).astype(jnp.int32)
    goes = jnp.broadcast_to(goes, full)
    order_ref[0:chunks, :] = lane_gather(goes, first_ref[0:chunks, :].astype(jnp.int32))
    order_ref[chunks:tops, :] = first_ref[chunks:tops, :]
    inverse_ref[0:chunks, :] = lane_gather(inverse_ref[0:chunks, :], comes)
    placed_ref[0:chunks, :] = lane_gather(placed_ref[0:chunks, :], comes)
    running = jnp.zeros((1, LANES), jnp.float32)
    for n in range(slots):
        count_ref[n : n + 1, :] = running
        running = running + placed_ref[n : n + 1, :]
        out_ref[ROWS + n : ROWS + n + 1, :] = running
        out_ref[ROWS + slots + n : ROWS + slots + n + 1, :] = order_ref[n : n + 1, :]
        row = inverse_row(n, slots)
        out_ref[row : row + 1, :] = inverse_ref[n : n + 1, :]
    for k in range(chunks):
        cols = slice(k * LANES, (k + 1) * LANES)
        u = succ_ref[:, cols]
        rows = [jnp.broadcast_to(order_ref[n : n + 1, :], (turns, LANES)) for n in range(slots)]
        lane = jnp.where(valid_ref[:, cols] == 1, table_gather(rows, u), -1.0)
        code = jnp.where(lane >= 0.0, lane + ((u >> 7) * LANES).astype(jnp.float32), -1.0)
        lane_ref[:, cols] = lane
        code_ref[:, cols] = code
        column_ref[cols, :] = columns(code)
    acc_ref[...] = jnp.zeros_like(acc_ref)
    earlier = jnp.where(
        lax.broadcasted_iota(jnp.int32, (step, step), 0) < lax.broadcasted_iota(jnp.int32, (step, step), 1),
        1.0,
        0.0,
    )
    lane_row_f = lane_row.astype(jnp.float32)

    def one_chunk(c, base):
        start = pl.multiple_of(c * step, step)
        cols = pl.ds(start, step)
        s = start + lax.broadcasted_iota(jnp.int32, (1, step), 1)
        source = [
            (s & ~7).astype(jnp.float32).astype(jnp.bfloat16),
            (s & 7).astype(jnp.float32).astype(jnp.bfloat16),
        ]
        for a in range(turns):
            row = slice(a, a + 1)
            hot = jnp.where(lane_ref[row, cols] == lane_row_f, 1.0, 0.0).astype(jnp.bfloat16)
            hot_top = jnp.where((succ_ref[row, cols] >> 7) == top_row, 1.0, 0.0)
            same = column_ref[cols, row] == code_ref[row, cols]
            within = summed_down(jnp.where(same, earlier, 0.0))
            coarse = (base.astype(jnp.int32) & ~127).astype(jnp.float32)
            both = jnp.concatenate([coarse, base - coarse], axis=0).astype(jnp.bfloat16)
            starts = jnp.dot(both, hot, preferred_element_type=jnp.float32)
            begin = summed_down((starts[:tops] + starts[tops:]) * hot_top)
            base = base + product(hot_top.astype(jnp.bfloat16), hot)
            match = jnp.where(begin + within == rank_row, 1.0, 0.0).astype(jnp.bfloat16)
            r = reward_ref[row, cols]
            r1 = r.astype(jnp.bfloat16)
            rest = r - r1.astype(jnp.float32)
            r2 = rest.astype(jnp.bfloat16)
            r3 = (rest - r2.astype(jnp.float32)).astype(jnp.bfloat16)
            left = jnp.concatenate([match * piece for piece in (*source, r1, r2, r3)], axis=0)
            acc_ref[...] += product(left, hot)
        return base

    lax.fori_loop(0, width // step, one_chunk, count_ref[...])
    part = [acc_ref[i * RANKS : i * RANKS + ROWS, :] for i in range(5)]
    share = out_ref.shape[0] // 2
    out_ref[0:ROWS, :] = part[0] + part[1]
    out_ref[share : share + ROWS, :] = (part[2] + part[3]) + part[4]
    listed = columns(border_ref[...].astype(jnp.float32)).astype(jnp.int32)
    for side in range(4):
        for q in range(chunks):
            found = jnp.where(listed[:, side : side + 1] == along + q * LANES, down_f + 1.0, 0.0)
            row = share + ROWS + side * chunks + q
            out_ref[row : row + 1, :] = summed_down(found)
    blocks = anchor_ref.shape[0]
    for q in range(chunks):
        split_ref[pl.ds(q, blocks, chunks), :] = anchor_ref[:, q * LANES : (q + 1) * LANES]
    start = pl.multiple_of(lax.axis_index("dst") * share, 8)
    common = share - chunks
    shared = out_ref[pl.ds(start + common, chunks), :]
    sub = lax.broadcasted_iota(jnp.int32, (chunks, LANES), 0)
    own_rows = (lax.axis_index("dst") == 0) & (sub >= 4)
    for b in range(blocks):
        rows = slice(b * chunks, (b + 1) * chunks)
        split_ref[rows, :] = jnp.where(own_rows, split_ref[rows, :], shared)
    half = out_ref.at[pl.ds(start, common)]
    pairs = []
    for b in range(blocks):
        pairs.append((half, out_any.at[pl.ds(b * share, common)]))
        pairs.append((split_ref.at[pl.ds(b * chunks, chunks)], out_any.at[pl.ds(b * share + common, chunks)]))
    run_copies(whole_copies(pairs, sem))


def inverse_row(n, slots):
    if n < slots - 4:
        return ROWS + 2 * slots + n
    return 2 * (ROWS + 3 * slots) - slots + n


def graph_kernel(
    weight_ref, feature_any, succ_any, valid_any, border_any, anchor_any, out_ref, reward_ref,
    feature_ref, succ_ref, valid_ref, border_ref, anchor_ref, part_ref, split_ref, sem
):
    run_copies(
        whole_copies(
            [
                (feature_any, feature_ref),
                (succ_any, succ_ref),
                (valid_any, valid_ref),
                (border_any, border_ref),
                (anchor_any, anchor_ref),
            ],
            sem,
        )
    )
    turns, width = succ_ref.shape
    chunks = width // LANES
    edges = turns * chunks
    part_ref[edges : edges + 8, :] = jnp.zeros((8, LANES), jnp.float32)
    part_ref[edges : edges + 4, :] = border_ref[...].astype(jnp.float32)
    blocks = anchor_ref.shape[0]
    split_ref[0:8, :] = jnp.zeros((8, LANES), jnp.float32)
    first_core = lax.axis_index("dst") == 0
    for q in range(chunks):
        cols = slice(q * LANES, (q + 1) * LANES)
        cost = weight_ref[0] * feature_ref[0, :, cols].astype(jnp.float32)
        for f in range(1, feature_ref.shape[0]):
            cost = cost + weight_ref[f] * feature_ref[f, :, cols].astype(jnp.float32)
        reward_ref[:, cols] = -cost
        masked = jnp.where(valid_ref[:, cols] == 1, -cost, NEG)
        turn_to = succ_ref[:, cols].astype(jnp.float32)
        part_ref[pl.ds(q, turns, chunks), :] = jnp.where(first_core, masked, turn_to)
        split_ref[pl.ds(8 + q, blocks, chunks), :] = anchor_ref[:, cols]
    size = part_ref.shape[0]
    lists = part_ref[edges:size, :]
    upper = lax.broadcasted_iota(jnp.int32, (8, LANES), 0) < 4
    for b in range(blocks):
        out_ref[b * size : b * size + edges, :] = part_ref[0:edges, :]
        own = split_ref[8 + b * chunks : 16 + b * chunks, :]
        lower = split_ref[4 + b * chunks : 12 + b * chunks, :]
        mixed = jnp.where(upper, lists, lower)
        out_ref[b * size + edges : (b + 1) * size, :] = jnp.where(first_core, mixed, own)


def regroup_kernel(pieces_ref, out_ref, padded_ref):
    halves, rows = out_ref.shape[:2]
    size, apart = pieces_ref.shape[0] // (8 * halves), padded_ref.shape[0] // (8 * halves)
    for b in range(8 * halves):
        padded_ref[b * apart : b * apart + size, :] = pieces_ref[b * size : (b + 1) * size, :]
    for h in range(halves):

        def one_row(i, carry, h=h):
            out_ref[h, i] = of_blocks(padded_ref, h, i, apart)
            return carry

        lax.fori_loop(0, rows, one_row, 0, unroll=8)


def weigh(out):
    top = functools.reduce(jnp.maximum, out)
    raised = [jnp.exp(score - top) for score in out]
    return top, raised, functools.reduce(jnp.add, raised)


def weighed_turns(values, reward, index, h, q, turns, chunks):
    tables = [values[h, r] for r in range(chunks + 4)]
    out = []
    for a in range(turns):
        rows = tables if a else tables[:chunks]
        out.append(reward[h, a * chunks + q] + table_gather(rows, index[h, a * chunks + q]))
    return weigh(out)


def policy_kernel(values_ref, reward_ref, index_ref, raised_ref, max_ref, inv_ref):
    halves, chunks = max_ref.shape[:2]
    turns = reward_ref.shape[1] // chunks

    def one_chunk(q, inner):
        for h in range(halves):
            top, raised, total = weighed_turns(values_ref, reward_ref, index_ref, h, q, turns, chunks)
            max_ref[h, q] = top
            inv_ref[h, q] = 1.0 / total
            for a in range(turns):
                raised_ref[h, a * chunks + q] = raised[a]
        return inner

    lax.fori_loop(0, chunks, one_chunk, 0, unroll=chunks)


def value_kernel(
    grid_x, dest_ref, mine_ref, other_ref, ext_ref, reward, index, border, side_pad, spare_ref
):
    halves = ext_ref.shape[0]
    blocks = 8 * halves
    chunks = ext_ref.shape[1] - 4
    edges = reward.shape[1]
    turns = edges // chunks
    per_block = chunks * LANES
    dest = renumbered(dest_ref[own_block(grid_x)], per_block, blocks, grid_x)
    side_pad[...] = jnp.zeros_like(side_pad)
    sub = lax.broadcasted_iota(jnp.int32, (8, LANES), 0)
    lane = lax.broadcasted_iota(jnp.int32, (8, LANES), 1)
    dest_block, dest_place = lax.div(dest, per_block), lax.rem(dest, per_block)

    def unpack(first, second):
        for h in range(halves):

            def rows(i, carry, h=h):
                reward[h, i] = first[h, i]
                index[h, i] = second[h, i].astype(jnp.int32)
                return carry

            lax.fori_loop(0, edges, rows, 0, unroll=8)
            for side in range(4):
                border[h, side] = first[h, edges + side].astype(jnp.int32)

    by_core(unpack, mine_ref, other_ref)
    for h in range(halves):
        for side in range(4):
            found = (border[h, side] == dest_place) & (h * 8 + sub == dest_block)
            entry = jnp.max(jnp.where(found, lane + 1, 0).astype(jnp.float32), axis=1, keepdims=True)
            side_pad[side, 8 + 8 * h : 16 + 8 * h, :] = jnp.broadcast_to(entry, (8, LANES))
    shifts = ((1, -1), (0, 1), (3, -grid_x), (2, grid_x))

    def shown(h, side):
        facing, by = shifts[side]
        start = 8 + 8 * h + by
        return side_pad[facing, start : start + 8, :]

    def dest_index(h):
        where = jnp.where(h * 8 + sub == dest_block, dest_place, -1)
        for side in range(4):
            entry = shown(h, side).astype(jnp.int32)
            where = jnp.where(entry > 0, per_block + side * LANES + entry - 1, where)
        return where

    def bring_halo(values):
        for h in range(halves):
            table = [values[h, q] for q in range(chunks)]
            for side in range(4):
                side_pad[side, 8 + 8 * h : 16 + 8 * h, :] = table_gather(table, border[h, side])
        for h in range(halves):
            for side in range(4):
                values[h, chunks + side] = shown(h, side)

    def store_value(h, q, top, total, into):
        value = top + jnp.log(total)
        into[h, q] = jnp.where(target_mask(dest, h, q, per_block), 0.0, value)

    wanted = [dest_index(h) for h in range(halves)]

    def first_chunk(q, inner):
        for h in range(halves):
            out = []
            for a in range(turns):
                before = jnp.where(index[h, a * chunks + q] == wanted[h], 0.0, -START_COST)
                out.append(reward[h, a * chunks + q] + before)
            top, _, total = weigh(out)
            store_value(h, q, top, total, spare_ref)
        return inner

    lax.fori_loop(0, chunks, first_chunk, 0, unroll=2)

    def backup(values, into):
        bring_halo(values)

        def one_chunk(q, inner):
            for h in range(halves):
                top, _, total = weighed_turns(values, reward, index, h, q, turns, chunks)
                store_value(h, q, top, total, into)
            return inner

        lax.fori_loop(0, chunks, one_chunk, 0, unroll=chunks)

    def two_backups(step, carry):
        backup(spare_ref, ext_ref)
        backup(ext_ref, spare_ref)
        return carry

    lax.fori_loop(0, (HORIZON - 2) // 2, two_backups, 0)
    backup(spare_ref, ext_ref)
    bring_halo(ext_ref)


def push_kernel(
    grid_x, scale, dest_ref, mine_ref, other_ref, graph_mine, graph_other, ext_ref, raised_ref, max_ref,
    inv_ref, keep_ref, send_ref, counts, ends, order, values, source, slot, going, policy, flows, back, scaled, total, arrived, side_pad, raw
):
    halves = ext_ref.shape[0]
    blocks = 8 * halves
    share = mine_ref.shape[1]
    chunks = max_ref.shape[1]
    edges = raised_ref.shape[1]
    turns = edges // chunks
    per_block = chunks * LANES
    slots = chunks + 4
    dest = renumbered(dest_ref[own_block(grid_x)], per_block, blocks, grid_x)
    core = lax.axis_index("dst")
    side_pad[...] = jnp.zeros_like(side_pad)

    def unpack(first, second):
        for h in range(halves):
            for n in range(slots):
                ends[h, n] = first[h, ROWS + n]
                order[h, n] = first[h, ROWS + slots + n].astype(jnp.int32)
                row = inverse_row(n, slots)
                inverse = (first[h, row] if row < share else second[h, row - share]).astype(jnp.int32)
                values[h, n] = lane_gather(ext_ref[h, n], inverse)

            def rows(r, carry, h=h):
                source[h, r] = first[h, r].astype(jnp.int32)
                policy[h, r] = second[h, r]
                return carry

            lax.fori_loop(0, ROWS, rows, 0, unroll=6)
            for r in range(ROWS, DEPTH):
                source[h, r] = jnp.zeros((8, LANES), jnp.int32)
                policy[h, r] = jnp.zeros((8, LANES), jnp.float32)
            for n in range(4 * chunks):
                back[h, n] = second[h, ROWS + n].astype(jnp.int32) - 1

    by_core(unpack, mine_ref, other_ref)

    def first_anchors():
        for h in range(halves):
            for q in range(4):
                total[h, q] = graph_mine[h, edges + 4 + q]
                total[h, 4 + q] = mine_ref[h, share - 4 + q]

    def second_anchors():
        for h in range(halves):
            for q in range(chunks):
                total[h, q] = graph_mine[h, edges + q]

    pl.when(core == 0)(first_anchors)
    pl.when(core != 0)(second_anchors)
    deepest = jnp.max(functools.reduce(jnp.maximum, [ends[h, slots - 1] for h in range(halves)]))
    deepest = deepest.astype(jnp.int32)
    fits = deepest <= ROWS
    steps = jnp.where(deepest <= USUAL, USUAL // STEP, DEPTH // STEP)
    shifts = ((1, -1), (0, 1), (3, -grid_x), (2, grid_x))

    def shown(h, side):
        facing, by = shifts[side]
        start = 8 + 8 * h + by
        return side_pad[facing, start : start + 8, :]

    @pl.when(jnp.logical_not(fits))
    def _():
        for h in range(halves):
            for n in range(slots):
                order[h, n] = lax.broadcasted_iota(jnp.int32, (8, LANES), 1)

    for h in range(halves):
        for side in range(4):
            side_pad[side, 8 + 8 * h : 16 + 8 * h, :] = order[h, chunks + side].astype(jnp.float32)
    for h in range(halves):
        for side in range(4):
            lanes = shown(h, side).astype(jnp.int32)
            for q in range(chunks):
                entry = back[h, side * chunks + q]
                back[h, side * chunks + q] = jnp.where(
                    entry >= 0, lane_gather(lanes, jnp.maximum(entry, 0)), -1
                )

    def prepare_rows(rows):
        row_before = [None] * halves
        for i, r in enumerate(rows):
            for h in range(halves):
                src = source[h, r]
                place = jnp.asarray(r).astype(jnp.float32)
                row = functools.reduce(
                    jnp.add, [jnp.where(ends[h, n] <= place, 1, 0) for n in range(slots)]
                )
                slot[h, r] = row
                if i:
                    going[h, r] = jnp.where(row == row_before[h], 1.0, 0.0)
                row_before[h] = row
                bits = [(row & (1 << n)) != 0 for n in range(4)]
                picked = tree_select([values[h, n] for n in range(slots)], bits)
                top = table_gather([max_ref[h, q] for q in range(chunks)], src)
                policy[h, r] = jnp.exp(policy[h, r] + picked - top)

    def prepare_step(t, carry):
        prepare_rows([t * STEP + i for i in range(STEP)])
        return carry

    usual = deepest <= USUAL
    pl.when(usual)(lambda: prepare_rows(range(USUAL)))
    lax.fori_loop(0, jnp.where(usual, 0, steps), prepare_step, 0)
    for h in range(halves):
        for q in range(chunks):
            first = jnp.where(target_mask(dest, h, q, per_block), 0.0, total[h, q])
            total[h, q] = first
            scaled[h, q] = first * inv_ref[h, q]

    @pl.when(jnp.logical_not(fits))
    def _():
        def keep_turns(first, second):
            for h in range(halves):

                def rows(e, carry, h=h):
                    raw[h, e] = second[h, e].astype(jnp.int32)
                    return carry

                lax.fori_loop(0, edges, rows, 0)

        by_core(keep_turns, graph_mine, graph_other)

    zero = jnp.zeros((8, LANES), jnp.float32)

    def keep(h):
        for side in range(4):
            side_pad[side, 8 + 8 * h : 16 + 8 * h, :] = arrived[h, chunks + side]

    def add_flow(acc, row, flow):
        return [acc[n] + jnp.where(row == n, flow, 0.0) for n in range(slots)]

    def sum_arranged():
        for h in range(halves):
            for n in range(slots):
                arrived[h, n] = zero

        def one_step(t, carry):
            tables = [[scaled[h, q] for q in range(chunks)] for h in range(halves)]
            step_sums = [[zero] * slots for h in range(halves)]
            so_far = [None] * halves
            for i in range(STEP):
                r = t * STEP + i
                for h in range(halves):
                    flow = table_gather(tables[h], source[h, r]) * policy[h, r]
                    so_far[h] = flow + going[h, r] * so_far[h] if i else flow
                    row = slot[h, r]
                    step_sums[h] = [jnp.where(row == n, so_far[h], step_sums[h][n]) for n in range(slots)]
            for h in range(halves):
                for n in range(slots):
                    arrived[h, n] = arrived[h, n] + step_sums[h][n]
            return carry

        def usual_rows():
            for h in range(halves + 1):
                sums = [zero] * slots
                table = [scaled[h, q] for q in range(chunks)] if h < halves else None
                for r in range(USUAL):
                    if h < halves:
                        flow = table_gather(table, source[h, r]) * policy[h, r]
                        so_far = flow + going[h, r] * so_far if r else flow
                        flows[h, r] = so_far
                    if h:
                        row, summed = slot[h - 1, r], flows[h - 1, r]
                        sums = [jnp.where(row == n, summed, sums[n]) for n in range(slots)]
                if h:
                    for n in range(slots):
                        arrived[h - 1, n] = sums[n]

        pl.when(usual)(usual_rows)
        lax.fori_loop(0, jnp.where(usual, 0, steps), one_step, 0)
        for h in range(halves):
            keep(h)

    def sum_turned():
        lane = lax.broadcasted_iota(jnp.int32, (8, LANES), 1)
        for h in range(halves):

            def one_edge_row(e, acc, h=h):
                flow = scaled[h, lax.rem(e, chunks)] * raised_ref[h, e]
                where = raw[h, e]

                def one_turn(k, state):
                    flow, where, acc = state[0], state[1], list(state[2:])
                    here = jnp.where((where & (LANES - 1)) == lane, where >> 7, -1)
                    acc = add_flow(acc, here, flow)
                    return (pltpu.roll(flow, 1, 1), pltpu.roll(where, 1, 1), *acc)

                return tuple(lax.fori_loop(0, LANES, one_turn, (flow, where, *acc))[2:])

            for n, value in enumerate(lax.fori_loop(0, edges, one_edge_row, (zero,) * slots)):
                arrived[h, n] = value
            keep(h)

    def push(round_index, carry):
        pl.when(fits)(sum_arranged)
        pl.when(jnp.logical_not(fits))(sum_turned)
        for h in range(halves):
            landed = [shown(h, side) for side in range(4)]
            for q in range(chunks):
                value = lane_gather(arrived[h, q], order[h, q])
                for side in range(4):
                    entry = back[h, side * chunks + q]
                    got = lane_gather(landed[side], jnp.maximum(entry, 0))
                    value = value + jnp.where(entry >= 0, got, 0.0)
                value = jnp.where(target_mask(dest, h, q, per_block), 0.0, value)
                total[h, q] = total[h, q] + value
                scaled[h, q] = value * inv_ref[h, q]
        return carry

    lax.fori_loop(0, HORIZON - 1, push, 0)
    rows_out = edges // 2
    apart = counts.shape[1] // blocks
    for h in range(halves):
        for q in range(chunks):
            weight = total[h, q] * inv_ref[h, q] * scale
            for part, piece in ((core, 0), (1 - core, 1)):
                for a in range(turns // 2):
                    value = weight * raised_ref[h, (part * (turns // 2) + a) * chunks + q]
                    start = h * 8 * apart + a * chunks + q
                    counts[piece, pl.ds(start, 8, stride=apart), :] = value
    for piece, out_ref in ((0, keep_ref), (1, send_ref)):
        for b in range(blocks):
            out_ref[b * rows_out : (b + 1) * rows_out, :] = counts[
                piece, b * apart : b * apart + rows_out, :
            ]


VMEM_SPEC = pl.BlockSpec(memory_space=pltpu.VMEM)
SMEM_SPEC = pl.BlockSpec(memory_space=pltpu.SMEM)
HBM_SPEC = pl.BlockSpec(memory_space=pltpu.HBM)
PARAMS = pltpu.CompilerParams(vmem_limit_bytes=48 * 1024 * 1024)


def f32(*shape):
    return jax.ShapeDtypeStruct(shape, jnp.float32)


def call_graph(cost_weights, features, successors, turn_valid, border_lists, anchors):
    turns, width = successors.shape
    blocks = anchors.shape[0]
    chunks = width // LANES
    rows = turns * chunks + 8
    return pl.pallas_call(
        graph_kernel,
        out_shape=(f32(blocks * rows, LANES), f32(turns, width)),
        in_specs=[SMEM_SPEC] + [HBM_SPEC] * 5,
        out_specs=(VMEM_SPEC, VMEM_SPEC),
        scratch_shapes=[
            pltpu.VMEM(features.shape, features.dtype),
            pltpu.VMEM(successors.shape, jnp.int32),
            pltpu.VMEM(turn_valid.shape, jnp.int32),
            pltpu.VMEM(border_lists.shape, jnp.int32),
            pltpu.VMEM(anchors.shape, jnp.float32),
            pltpu.VMEM((rows, LANES), jnp.float32),
            pltpu.VMEM((blocks * chunks + 8, LANES), jnp.float32),
            pltpu.SemaphoreType.DMA((5,)),
        ],
        compiler_params=pltpu.CompilerParams(vmem_limit_bytes=63 * 1024 * 1024),
        name="own_graph",
    )(cost_weights, features, successors, turn_valid, border_lists, anchors)


def call_arrange(successors, turn_valid, border_lists, anchors, reward):
    chunks = successors.shape[1] // LANES
    share = ROWS + 3 * (chunks + 4)
    blocks = anchors.shape[0]
    return pl.pallas_call(
        arrange_kernel,
        out_shape=f32(blocks * share, LANES),
        in_specs=[HBM_SPEC] * 4 + [VMEM_SPEC],
        out_specs=HBM_SPEC,
        scratch_shapes=[
            pltpu.VMEM(successors.shape, jnp.int32),
            pltpu.VMEM(turn_valid.shape, jnp.int32),
            pltpu.VMEM(border_lists.shape, jnp.int32),
            pltpu.VMEM(anchors.shape, jnp.float32),
            pltpu.VMEM((blocks * chunks, LANES), jnp.float32),
            pltpu.VMEM((2 * share, LANES), jnp.float32),
            *[pltpu.VMEM((16, LANES), jnp.float32)] * 5,
            pltpu.VMEM((8, LANES), jnp.float32),
            pltpu.VMEM(successors.shape, jnp.float32),
            pltpu.VMEM(successors.shape, jnp.float32),
            pltpu.VMEM(successors.shape[::-1], jnp.float32),
            pltpu.VMEM((5 * RANKS, LANES), jnp.float32),
            pltpu.SemaphoreType.DMA((2 * blocks,)),
        ],
        compiler_params=PARAMS,
        cost_estimate=pl.CostEstimate(flops=4_000_000_000, bytes_accessed=400_000, transcendentals=0),
        name="arrange_turns",
    )(successors, turn_valid, border_lists, anchors, reward)


def call_regroup(pieces, blocks):
    return pl.pallas_call(
        regroup_kernel,
        out_shape=f32(blocks // 8, pieces.shape[0] // blocks, 8, LANES),
        in_specs=[VMEM_SPEC],
        out_specs=VMEM_SPEC,
        scratch_shapes=[
            pltpu.VMEM((blocks * padded_rows(pieces.shape[0] // blocks), LANES), jnp.float32)
        ],
        compiler_params=PARAMS,
        name="regroup",
    )(pieces)


def call_values(destinations, mine, other, blocks, grid_x, turns, chunks):
    halves = blocks // 8
    edges = turns * chunks
    rows = (halves, edges, 8, LANES)
    return pl.pallas_call(
        functools.partial(value_kernel, grid_x),
        out_shape=(
            f32(halves, chunks + 4, 8, LANES),
            f32(*rows),
            jax.ShapeDtypeStruct(rows, jnp.int32),
        ),
        in_specs=[SMEM_SPEC, VMEM_SPEC, VMEM_SPEC],
        out_specs=(VMEM_SPEC,) * 3,
        scratch_shapes=[
            pltpu.VMEM((halves, 4, 8, LANES), jnp.int32),
            pltpu.VMEM((4, blocks + 16, LANES), jnp.float32),
            pltpu.VMEM((halves, chunks + 4, 8, LANES), jnp.float32),
        ],
        compiler_params=PARAMS,
        cost_estimate=pl.CostEstimate(flops=40_000_000, bytes_accessed=40_000_000, transcendentals=2_000_000),
        name="soft_values",
    )(destinations, mine, other)


def call_policy(ext, reward, index):
    halves, edges = reward.shape[:2]
    chunks = ext.shape[1] - 4
    return pl.pallas_call(
        policy_kernel,
        out_shape=(f32(*reward.shape), f32(halves, chunks, 8, LANES), f32(halves, chunks, 8, LANES)),
        in_specs=[VMEM_SPEC] * 3,
        out_specs=(VMEM_SPEC,) * 3,
        compiler_params=PARAMS,
        cost_estimate=pl.CostEstimate(flops=5_000_000, bytes_accessed=5_000_000, transcendentals=200_000),
        name="policy",
    )(ext, reward, index)


def call_push(destinations, mine, other, graph_mine, graph_other, ext, raised, top, inv, grid_x, scale):
    halves, edges = raised.shape[:2]
    blocks = 8 * halves
    chunks = top.shape[1]

    def vmem(rows, dtype=jnp.float32):
        return pltpu.VMEM((halves, rows, 8, LANES), dtype)

    return pl.pallas_call(
        functools.partial(push_kernel, grid_x, scale),
        out_shape=(f32(blocks * edges // 2, LANES),) * 2,
        in_specs=[SMEM_SPEC] + [VMEM_SPEC] * 8,
        out_specs=(VMEM_SPEC,) * 2,
        scratch_shapes=[
            pltpu.VMEM((2, blocks * padded_rows(edges // 2), LANES), jnp.float32),
            vmem(chunks + 4),
            vmem(chunks + 4, jnp.int32),
            vmem(chunks + 4),
            vmem(DEPTH, jnp.int32),
            vmem(DEPTH, jnp.int32),
            vmem(DEPTH),
            vmem(DEPTH),
            vmem(USUAL),
            vmem(4 * chunks, jnp.int32),
            vmem(chunks),
            vmem(chunks),
            vmem(chunks + 4),
            pltpu.VMEM((4, blocks + 16, LANES), jnp.float32),
            vmem(edges, jnp.int32),
        ],
        compiler_params=PARAMS,
        name="push_mass",
    )(destinations, mine, other, graph_mine, graph_other, ext, raised, top, inv)


def to_blocks(array):
    return lax.all_to_all(array, BLOCK_AXES, 0, 0, tiled=True)


def other_core(array):
    return lax.ppermute(array, "dst", [(0, 1), (1, 0)])


def per_destination(
    features, cost_weights, successors, turn_valid, border_lists, destinations, anchors, demo_counts
):
    turns, own_count = successors.shape
    chunks = own_count // LANES
    edges = turns * chunks
    grid_x = lax.axis_size("gx")
    blocks = lax.axis_size("gy") * grid_x
    groups = lax.axis_size("dst")
    pieces, reward = call_graph(cost_weights, features, successors, turn_valid, border_lists, anchors)
    graph = to_blocks(pieces)
    arranged = call_arrange(successors, turn_valid, border_lists, anchors, reward)
    core = lax.axis_index("dst")
    demo_term = jnp.where(turn_valid == 1, demo_counts, 0).astype(jnp.float32) / 3.0
    own_feats = lax.dynamic_slice_in_dim(features, core * (turns // 2), turns // 2, axis=1)
    first_core, own_feats, demo_term, arranged = lax.optimization_barrier(
        (core == 0, own_feats, demo_term, arranged)
    )
    graph = lax.optimization_barrier((graph, arranged))[0]
    arranged = to_blocks(arranged)
    graph = call_regroup(graph, blocks)
    graph = (graph, other_core(graph))
    ext, reward, index = call_values(destinations, *graph, blocks, grid_x, turns, chunks)
    arranged, ext = lax.optimization_barrier((arranged, ext))
    arranged = call_regroup(arranged, blocks)
    arranged, ext = lax.optimization_barrier((arranged, ext))
    arranged = (arranged, other_core(arranged))
    values = (ext, *call_policy(ext, reward, index))
    scale = 1.0 / (anchors.shape[0] * groups * HORIZON)
    kept, sent = call_push(destinations, *arranged, *graph, *values, grid_x, scale)
    halved = (kept + other_core(sent)).reshape(blocks, edges // 2, LANES)
    half = jnp.sum(to_blocks(halved), axis=0)
    other = other_core(half)
    part = (turns // 2, own_count)
    own_gap = lax.dynamic_slice_in_dim(demo_term, core * part[0], part[0]) - half.reshape(part)
    own_feats = own_feats.astype(jnp.float32)
    block_term = jnp.sum(own_gap[None] * own_feats, axis=(1, 2)) / (own_count * blocks)
    visits = jnp.concatenate([jnp.where(first_core, half, other), jnp.where(first_core, other, half)])
    count_gap = demo_term - visits.reshape(turns, own_count)
    terms = jnp.broadcast_to(block_term, (groups * blocks, 1, block_term.shape[0]))
    terms = lax.all_to_all(terms, (*BLOCK_AXES, "dst"), 0, 0, tiled=True)
    terms, count_gap = lax.optimization_barrier((terms, count_gap))
    return count_gap, jnp.sum(terms, axis=(0, 1))


def passed_along(array, axis, by):
    length = lax.axis_size(axis)
    pairs = [(i, i + by) for i in range(length) if 0 <= i + by < length]
    return lax.ppermute(array, axis, pairs)


def bring_values(values, border_lists):
    outgoing = values[:, border_lists]
    north_part = passed_along(outgoing[:, 1], "gx", 1)
    south_part = passed_along(outgoing[:, 0], "gx", -1)
    west_part = passed_along(outgoing[:, 3], "gy", 1)
    east_part = passed_along(outgoing[:, 2], "gy", -1)
    return jnp.concatenate([north_part, south_part, west_part, east_part], axis=1)


def return_flow(arrived, border_lists, own_count, border_width):
    local_part = arrived[:, :own_count]
    halo_part = arrived[:, own_count:].reshape(arrived.shape[0], 4, border_width)
    from_south = passed_along(halo_part[:, 0], "gx", -1)
    from_north = passed_along(halo_part[:, 1], "gx", 1)
    from_east = passed_along(halo_part[:, 2], "gy", -1)
    from_west = passed_along(halo_part[:, 3], "gy", 1)
    returned = jnp.stack([from_north, from_south, from_west, from_east], axis=1)
    return local_part.at[:, border_lists].add(returned)


def select_cells(cells, flat_index, turn_shape):
    picked = jnp.take(cells, flat_index, axis=1)
    return picked.reshape(cells.shape[0], turn_shape[0], turn_shape[1])


def turn_scores(values, halo_cells, reward, flat_turns, usable):
    extended = jnp.concatenate([values, halo_cells], axis=1)
    scores = reward[None] + select_cells(extended, flat_turns, usable.shape)
    return jnp.where(usable[None], scores, NEG)


def per_block(
    features, cost_weights, successors, turn_valid, border_lists, destinations, anchors, demo_counts
):
    own_count = successors.shape[1]
    border_width = border_lists.shape[1]
    dest_count = anchors.shape[0]
    slot_total = own_count + 4 * border_width
    block_index = lax.axis_index("gx") * lax.axis_size("gy") + lax.axis_index("gy")
    positions = jnp.arange(own_count, dtype=jnp.int32)
    is_target = positions[None, :] == (destinations - block_index * own_count)[:, None]
    usable = turn_valid == 1
    feats = features.astype(jnp.float32)
    reward = -jnp.sum(feats * cost_weights[:, None, None], axis=0)
    flat_turns = successors.reshape(-1)
    values = jnp.where(is_target, 0.0, -START_COST).astype(jnp.float32)
    for round_index in range(HORIZON):
        halo_cells = bring_values(values, border_lists)
        scores = turn_scores(values, halo_cells, reward, flat_turns, usable)
        row_max = jnp.max(scores, axis=1)
        new_values = row_max + jnp.log(jnp.sum(jnp.exp(scores - row_max[:, None]), axis=1))
        values = jnp.where(is_target, 0.0, new_values)
    halo_cells = bring_values(values, border_lists)
    scores = turn_scores(values, halo_cells, reward, flat_turns, usable)
    row_max = jnp.max(scores, axis=1)
    raised = jnp.exp(scores - row_max[:, None])
    policy = raised / jnp.sum(raised, axis=1, keepdims=True)
    mass_now = jnp.where(is_target, 0.0, anchors)
    turn_counts = jnp.zeros(successors.shape, jnp.float32)
    for round_index in range(HORIZON):
        turn_flow = mass_now[:, None, :] * policy
        turn_counts = turn_counts + jnp.sum(turn_flow, axis=0)
        if round_index + 1 < HORIZON:
            arrived = (
                jnp.zeros((dest_count, slot_total), jnp.float32)
                .at[:, flat_turns]
                .add(turn_flow.reshape(dest_count, -1))
            )
            landed = return_flow(arrived, border_lists, own_count, border_width)
            mass_now = jnp.where(is_target, 0.0, landed)
    local_visits = turn_counts / (dest_count * lax.axis_size("dst") * HORIZON)
    visits = lax.psum(local_visits, "dst")
    demo_term = jnp.where(usable, demo_counts, 0).astype(jnp.float32) / 3.0
    count_gap = demo_term - visits
    total_segments = own_count * lax.axis_size("gx") * lax.axis_size("gy")
    own_gap = demo_term / lax.axis_size("dst") - local_visits
    block_term = jnp.sum(own_gap[None] * feats, axis=(1, 2)) / total_segments
    gradient = lax.psum(block_term, ("gx", "gy", "dst"))
    return (count_gap, gradient)


def local(features, cost_weights, successors, turn_valid, border_lists, destinations, anchors, demo_counts):
    args = (
        features, cost_weights, successors, turn_valid, border_lists, destinations, anchors, demo_counts
    )
    blocks = lax.axis_size("gx") * lax.axis_size("gy")
    fits = (
        anchors.shape[0] == blocks
        and blocks % 8 == 0
        and lax.axis_size("dst") == 2
        and lax.axis_size("gx") in (2, 4, 8)
        and lax.axis_size("gy") in (2, 4, 8)
        and successors.shape[1] == 8 * LANES
        and border_lists.shape[1] == LANES
        and successors.shape[0] == 8
    )
    return per_destination(*args) if fits else per_block(*args)


def solution(mesh):
    in_specs = (
        P(None, None, ("gx", "gy")),
        P(),
        P(None, ("gx", "gy")),
        P(None, ("gx", "gy")),
        P(None, ("gx", "gy")),
        P("dst"),
        P("dst", ("gx", "gy")),
        P(None, ("gx", "gy")),
    )
    out_specs = (P(None, ("gx", "gy")), P())
    return jax.shard_map(local, mesh=mesh, in_specs=in_specs, out_specs=out_specs, check_vma=False)
```

```python
import functools

import jax
import jax.numpy as jnp
from jax import lax
from jax.experimental import pallas as pl
from jax.experimental.pallas import tpu as pltpu
from jax.sharding import PartitionSpec as P

HORIZON = 8
NEG = -1e30
START_COST = 100.0
LANES = 128
ROWS = 60
RANKS = -(-ROWS // 16) * 16
STEP = 14
USUAL = 56
DEPTH = -(-ROWS // STEP) * STEP
BLOCK_AXES = ("gy", "gx")

LANE_PICK = lax.GatherDimensionNumbers(
    offset_dims=(),
    collapsed_slice_dims=(1,),
    start_index_map=(1,),
    operand_batching_dims=(0,),
    start_indices_batching_dims=(0,),
)


def lane_gather(table, index):
    return lax.gather(
        table,
        index[..., None],
        LANE_PICK,
        (1, 1),
        mode=lax.GatherScatterMode.PROMISE_IN_BOUNDS,
    )


def tree_select(picked, bits):
    level = list(picked)
    for bit in bits:
        if len(level) == 1:
            break
        nxt = []
        for n in range(0, len(level), 2):
            if n + 1 < len(level):
                nxt.append(jnp.where(bit, level[n + 1], level[n]))
            else:
                nxt.append(level[n])
        level = nxt
    return level[0]


def row_bits(index, count):
    return [(index & (LANES << i)) != 0 for i in range(count)]


def table_gather(table_rows, index):
    lane = index & (LANES - 1)
    bits = row_bits(index, max(len(table_rows) - 1, 1).bit_length())
    return tree_select([lane_gather(row, lane) for row in table_rows], bits)


def run_copies(copies):
    for copy in copies:
        copy.start()
    for copy in copies:
        copy.wait()


def of_blocks(ref, half, row, per_block):
    return ref[pl.ds(half * 8 * per_block + row, 8, stride=per_block), :]


def whole_copies(pairs, sem):
    return [pltpu.make_async_copy(src, dst, sem.at[n]) for n, (src, dst) in enumerate(pairs)]


def by_core(what, mine, other):
    first = lax.axis_index("dst") == 0
    pl.when(first)(lambda: what(mine, other))
    pl.when(jnp.logical_not(first))(lambda: what(other, mine))


def own_block(grid_x):
    return lax.axis_index("gy") * grid_x + lax.axis_index("gx")


def renumbered(segment, per_block, blocks, grid_x):
    grid_y = blocks // grid_x
    block, place = lax.div(segment, per_block), lax.rem(segment, per_block)
    return (lax.rem(block, grid_y) * grid_x + lax.div(block, grid_y)) * per_block + place


def padded_rows(rows):
    tiles = -(-rows // 8)
    return (tiles + 1 - tiles % 2) * 8


def target_mask(dest, half, chunk, per_block):
    sub = lax.broadcasted_iota(jnp.int32, (8, LANES), 0)
    lane = lax.broadcasted_iota(jnp.int32, (8, LANES), 1)
    return (half * 8 + sub) * per_block + chunk * LANES + lane == dest


def arrange_kernel(
    succ_any, valid_any, border_any, anchor_any, reward_ref, out_any,
    succ_ref, valid_ref, border_ref, anchor_ref, split_ref, out_ref, count_ref, first_ref, order_ref, inverse_ref, placed_ref,
    pair_ref, lane_ref, code_ref, column_ref, acc_ref, sem
):
    run_copies(
        whole_copies(
            [
                (succ_any, succ_ref),
                (valid_any, valid_ref),
                (border_any, border_ref),
                (anchor_any, anchor_ref),
            ],
            sem,
        )
    )
    turns, width = succ_ref.shape
    chunks = width // LANES
    slots = chunks + 4
    step = 2 * LANES
    tops = 16
    square = (LANES, LANES)
    down = lax.broadcasted_iota(jnp.int32, square, 0)
    along = lax.broadcasted_iota(jnp.int32, square, 1)
    down_f, along_f = down.astype(jnp.float32), along.astype(jnp.float32)
    before = down < along
    unit = jnp.where(down == along, 1.0, 0.0)
    lane_row = lax.broadcasted_iota(jnp.int32, (LANES, step), 0)
    top_row = lax.broadcasted_iota(jnp.int32, (tops, step), 0)
    rank_row = lax.broadcasted_iota(jnp.int32, (RANKS, step), 0).astype(jnp.float32)
    last_dims = (((1,), (1,)), ((), ()))

    def product(left, right):
        return lax.dot_general(left, right, last_dims, preferred_element_type=jnp.float32)

    def columns(rows):
        return lax.dot_general(
            unit, rows, last_dims, precision=lax.Precision.HIGHEST, preferred_element_type=jnp.float32
        )

    def summed_down(array):
        return jnp.sum(array, axis=0, keepdims=True)

    def place_of(row, col):
        return summed_down(jnp.where((col > row) | ((col == row) & before), 1.0, 0.0))

    def count(a, total):
        for c in range(width // step):
            cols = slice(c * step, (c + 1) * step)
            u = succ_ref[pl.ds(a, 1), cols]
            low = jnp.where(valid_ref[pl.ds(a, 1), cols] == 1, u & (LANES - 1), -1)
            hot_low = jnp.where(low == lane_row, 1.0, 0.0).astype(jnp.bfloat16)
            hot_top = jnp.where((u >> 7) == top_row, 1.0, 0.0).astype(jnp.bfloat16)
            total = total + product(hot_top, hot_low)
        return total

    counts = lax.fori_loop(0, turns, count, jnp.zeros((tops, LANES), jnp.float32), unroll=2)
    count_columns = columns(counts)
    out_ref[...] = jnp.zeros_like(out_ref)
    for ref in (count_ref, first_ref, order_ref, inverse_ref, placed_ref, pair_ref):
        ref[...] = jnp.zeros_like(ref)
    for n in range(slots):
        i = n if n < chunks else n - chunks
        place = place_of(counts[n : n + 1, :], count_columns[:, n : n + 1])
        place = place if i % 2 == 0 else (LANES - 1.0) - place
        if (i // 2) % 2:
            place = jnp.where(place >= LANES // 2, place - LANES // 2, place + LANES // 2)
        first_ref[n : n + 1, :] = place
    first_columns = columns(first_ref[...])
    for n in range(slots):
        hit = first_columns[:, n : n + 1] == along_f
        inverse_ref[n : n + 1, :] = summed_down(jnp.where(hit, down_f, 0.0))
        placed_ref[n : n + 1, :] = summed_down(jnp.where(hit, count_columns[:, n : n + 1], 0.0))
    local = summed_down(placed_ref[0:chunks, :])
    room = -summed_down(placed_ref[chunks:tops, :])
    pair_ref[0:1, :] = local
    pair_ref[1:2, :] = room
    pair = columns(pair_ref[...])
    local_place, room_place = place_of(local, pair[:, 0:1]), place_of(room, pair[:, 1:2])
    pair_ref[0:1, :] = local_place
    pair_ref[1:2, :] = room_place
    pair = columns(pair_ref[...])
    goes = summed_down(jnp.where(pair[:, 1:2] == local_place, down_f, 0.0))
    comes = summed_down(jnp.where(pair[:, 0:1] == room_place, down_f, 0.0))
    full = (chunks, LANES)
    comes = jnp.broadcast_to(comes, full).astype(jnp.int32)
    goes = jnp.broadcast_to(goes, full)
    order_ref[0:chunks, :] = lane_gather(goes, first_ref[0:chunks, :].astype(jnp.int32))
    order_ref[chunks:tops, :] = first_ref[chunks:tops, :]
    inverse_ref[0:chunks, :] = lane_gather(inverse_ref[0:chunks, :], comes)
    placed_ref[0:chunks, :] = lane_gather(placed_ref[0:chunks, :], comes)
    running = jnp.zeros((1, LANES), jnp.float32)
    for n in range(slots):
        count_ref[n : n + 1, :] = running
        running = running + placed_ref[n : n + 1, :]
        out_ref[ROWS + n : ROWS + n + 1, :] = running
        out_ref[ROWS + slots + n : ROWS + slots + n + 1, :] = order_ref[n : n + 1, :]
        row = inverse_row(n, slots)
        out_ref[row : row + 1, :] = inverse_ref[n : n + 1, :]
    for k in range(chunks):
        cols = slice(k * LANES, (k + 1) * LANES)
        u = succ_ref[:, cols]
        rows = [jnp.broadcast_to(order_ref[n : n + 1, :], (turns, LANES)) for n in range(slots)]
        lane = jnp.where(valid_ref[:, cols] == 1, table_gather(rows, u), -1.0)
        code = jnp.where(lane >= 0.0, lane + ((u >> 7) * LANES).astype(jnp.float32), -1.0)
        lane_ref[:, cols] = lane
        code_ref[:, cols] = code
        column_ref[cols, :] = columns(code)
    acc_ref[...] = jnp.zeros_like(acc_ref)
    earlier = jnp.where(
        lax.broadcasted_iota(jnp.int32, (step, step), 0) < lax.broadcasted_iota(jnp.int32, (step, step), 1),
        1.0,
        0.0,
    )
    lane_row_f = lane_row.astype(jnp.float32)

    def one_chunk(c, base):
        start = pl.multiple_of(c * step, step)
        cols = pl.ds(start, step)
        s = start + lax.broadcasted_iota(jnp.int32, (1, step), 1)
        source = [
            (s & ~7).astype(jnp.float32).astype(jnp.bfloat16),
            (s & 7).astype(jnp.float32).astype(jnp.bfloat16),
        ]
        for a in range(turns):
            row = slice(a, a + 1)
            hot = jnp.where(lane_ref[row, cols] == lane_row_f, 1.0, 0.0).astype(jnp.bfloat16)
            hot_top = jnp.where((succ_ref[row, cols] >> 7) == top_row, 1.0, 0.0)
            same = column_ref[cols, row] == code_ref[row, cols]
            within = summed_down(jnp.where(same, earlier, 0.0))
            coarse = (base.astype(jnp.int32) & ~127).astype(jnp.float32)
            both = jnp.concatenate([coarse, base - coarse], axis=0).astype(jnp.bfloat16)
            starts = jnp.dot(both, hot, preferred_element_type=jnp.float32)
            begin = summed_down((starts[:tops] + starts[tops:]) * hot_top)
            base = base + product(hot_top.astype(jnp.bfloat16), hot)
            match = jnp.where(begin + within == rank_row, 1.0, 0.0).astype(jnp.bfloat16)
            r = reward_ref[row, cols]
            r1 = r.astype(jnp.bfloat16)
            rest = r - r1.astype(jnp.float32)
            r2 = rest.astype(jnp.bfloat16)
            r3 = (rest - r2.astype(jnp.float32)).astype(jnp.bfloat16)
            left = jnp.concatenate([match * piece for piece in (*source, r1, r2, r3)], axis=0)
            acc_ref[...] += product(left, hot)
        return base

    lax.fori_loop(0, width // step, one_chunk, count_ref[...])
    part = [acc_ref[i * RANKS : i * RANKS + ROWS, :] for i in range(5)]
    share = out_ref.shape[0] // 2
    out_ref[0:ROWS, :] = part[0] + part[1]
    out_ref[share : share + ROWS, :] = (part[2] + part[3]) + part[4]
    listed = columns(border_ref[...].astype(jnp.float32)).astype(jnp.int32)
    for side in range(4):
        for q in range(chunks):
            found = jnp.where(listed[:, side : side + 1] == along + q * LANES, down_f + 1.0, 0.0)
            row = share + ROWS + side * chunks + q
            out_ref[row : row + 1, :] = summed_down(found)
    blocks = anchor_ref.shape[0]
    for q in range(chunks):
        split_ref[pl.ds(q, blocks, chunks), :] = anchor_ref[:, q * LANES : (q + 1) * LANES]
    start = pl.multiple_of(lax.axis_index("dst") * share, 8)
    common = share - chunks
    shared = out_ref[pl.ds(start + common, chunks), :]
    sub = lax.broadcasted_iota(jnp.int32, (chunks, LANES), 0)
    own_rows = (lax.axis_index("dst") == 0) & (sub >= 4)
    for b in range(blocks):
        rows = slice(b * chunks, (b + 1) * chunks)
        split_ref[rows, :] = jnp.where(own_rows, split_ref[rows, :], shared)
    half = out_ref.at[pl.ds(start, common)]
    pairs = []
    for b in range(blocks):
        pairs.append((half, out_any.at[pl.ds(b * share, common)]))
        pairs.append((split_ref.at[pl.ds(b * chunks, chunks)], out_any.at[pl.ds(b * share + common, chunks)]))
    run_copies(whole_copies(pairs, sem))


def inverse_row(n, slots):
    if n < slots - 4:
        return ROWS + 2 * slots + n
    return 2 * (ROWS + 3 * slots) - slots + n


def graph_kernel(
    weight_ref, feature_any, succ_any, valid_any, border_any, anchor_any, out_ref, reward_ref,
    feature_ref, succ_ref, valid_ref, border_ref, anchor_ref, part_ref, split_ref, sem
):
    width = succ_ref.shape[1]
    parts = 4
    pairs = [
        (succ_any, succ_ref),
        (valid_any, valid_ref),
        (border_any, border_ref),
        (anchor_any, anchor_ref),
    ]
    for part in range(parts):
        cols = pl.ds(part * (width // parts), width // parts)
        pairs.append((feature_any.at[:, :, cols], feature_ref.at[:, :, cols]))
    copies = whole_copies(pairs, sem)
    for copy in copies:
        copy.start()
    for copy in copies[:-parts]:
        copy.wait()
    turns, width = succ_ref.shape
    chunks = width // LANES
    edges = turns * chunks
    part_ref[edges : edges + 8, :] = jnp.zeros((8, LANES), jnp.float32)
    part_ref[edges : edges + 4, :] = border_ref[...].astype(jnp.float32)
    blocks = anchor_ref.shape[0]
    split_ref[0:8, :] = jnp.zeros((8, LANES), jnp.float32)
    first_core = lax.axis_index("dst") == 0
    for q in range(chunks):
        if q * parts % chunks == 0:
            copies[q * parts // chunks - parts].wait()
        cols = slice(q * LANES, (q + 1) * LANES)
        cost = weight_ref[0] * feature_ref[0, :, cols].astype(jnp.float32)
        for f in range(1, feature_ref.shape[0]):
            cost = cost + weight_ref[f] * feature_ref[f, :, cols].astype(jnp.float32)
        reward_ref[:, cols] = -cost
        masked = jnp.where(valid_ref[:, cols] == 1, -cost, NEG)
        turn_to = succ_ref[:, cols].astype(jnp.float32)
        part_ref[pl.ds(q, turns, chunks), :] = jnp.where(first_core, masked, turn_to)
        split_ref[pl.ds(8 + q, blocks, chunks), :] = anchor_ref[:, cols]
    size = part_ref.shape[0]
    lists = part_ref[edges:size, :]
    upper = lax.broadcasted_iota(jnp.int32, (8, LANES), 0) < 4
    for b in range(blocks):
        out_ref[b * size : b * size + edges, :] = part_ref[0:edges, :]
        own = split_ref[8 + b * chunks : 16 + b * chunks, :]
        lower = split_ref[4 + b * chunks : 12 + b * chunks, :]
        mixed = jnp.where(upper, lists, lower)
        out_ref[b * size + edges : (b + 1) * size, :] = jnp.where(first_core, mixed, own)


def regroup_kernel(pieces_ref, *refs):
    out_refs, padded_ref = refs[:-1], refs[-1]
    halves, rows = len(out_refs), out_refs[0].shape[0]
    size, apart = pieces_ref.shape[0] // (8 * halves), padded_ref.shape[0] // (8 * halves)
    for b in range(8 * halves):
        padded_ref[b * apart : b * apart + size, :] = pieces_ref[b * size : (b + 1) * size, :]
    for h in range(halves):

        def one_row(i, carry, h=h):
            out_refs[h][i] = of_blocks(padded_ref, h, i, apart)
            return carry

        lax.fori_loop(0, rows, one_row, 0, unroll=8)


def weigh(out):
    top = functools.reduce(jnp.maximum, out)
    raised = [jnp.exp(score - top) for score in out]
    return top, raised, functools.reduce(jnp.add, raised)


def weighed_turns(values, reward, index, h, q, turns, chunks):
    tables = [values[h, r] for r in range(chunks + 4)]
    out = []
    for a in range(turns):
        rows = tables if a else tables[:chunks]
        out.append(reward[h, a * chunks + q] + table_gather(rows, index[h, a * chunks + q]))
    return weigh(out)


def policy_kernel(values_ref, reward_ref, index_ref, raised_ref, max_ref, inv_ref):
    halves, chunks = max_ref.shape[:2]
    turns = reward_ref.shape[1] // chunks

    def one_chunk(q, inner):
        for h in range(halves):
            top, raised, total = weighed_turns(values_ref, reward_ref, index_ref, h, q, turns, chunks)
            max_ref[h, q] = top
            inv_ref[h, q] = 1.0 / total
            for a in range(turns):
                raised_ref[h, a * chunks + q] = raised[a]
        return inner

    lax.fori_loop(0, chunks, one_chunk, 0, unroll=chunks)


def value_kernel(
    grid_x, halves, dest_ref, *refs
):
    mine, other = refs[:halves], refs[halves : 2 * halves]
    ext_ref, reward, index, border, side_pad, spare_ref = refs[2 * halves :]
    blocks = 8 * halves
    chunks = ext_ref.shape[1] - 4
    edges = reward.shape[1]
    turns = edges // chunks
    per_block = chunks * LANES
    dest = renumbered(dest_ref[own_block(grid_x)], per_block, blocks, grid_x)
    side_pad[...] = jnp.zeros_like(side_pad)
    sub = lax.broadcasted_iota(jnp.int32, (8, LANES), 0)
    lane = lax.broadcasted_iota(jnp.int32, (8, LANES), 1)
    dest_block, dest_place = lax.div(dest, per_block), lax.rem(dest, per_block)

    def unpack(first, second):
        for h in range(halves):

            def rows(i, carry, h=h):
                reward[h, i] = first[h][i]
                index[h, i] = second[h][i].astype(jnp.int32)
                return carry

            lax.fori_loop(0, edges, rows, 0, unroll=8)
            for side in range(4):
                border[h, side] = first[h][edges + side].astype(jnp.int32)

    by_core(unpack, mine, other)
    for h in range(halves):
        for side in range(4):
            found = (border[h, side] == dest_place) & (h * 8 + sub == dest_block)
            entry = jnp.max(jnp.where(found, lane + 1, 0).astype(jnp.float32), axis=1, keepdims=True)
            side_pad[side, 8 + 8 * h : 16 + 8 * h, :] = jnp.broadcast_to(entry, (8, LANES))
    shifts = ((1, -1), (0, 1), (3, -grid_x), (2, grid_x))

    def shown(h, side):
        facing, by = shifts[side]
        start = 8 + 8 * h + by
        return side_pad[facing, start : start + 8, :]

    def dest_index(h):
        where = jnp.where(h * 8 + sub == dest_block, dest_place, -1)
        for side in range(4):
            entry = shown(h, side).astype(jnp.int32)
            where = jnp.where(entry > 0, per_block + side * LANES + entry - 1, where)
        return where

    def bring_halo(values):
        for h in range(halves):
            table = [values[h, q] for q in range(chunks)]
            for side in range(4):
                side_pad[side, 8 + 8 * h : 16 + 8 * h, :] = table_gather(table, border[h, side])
        for h in range(halves):
            for side in range(4):
                values[h, chunks + side] = shown(h, side)

    def store_value(h, q, top, total, into):
        value = top + jnp.log(total)
        into[h, q] = jnp.where(target_mask(dest, h, q, per_block), 0.0, value)

    wanted = [dest_index(h) for h in range(halves)]

    def first_chunk(q, inner):
        for h in range(halves):
            out = []
            for a in range(turns):
                before = jnp.where(index[h, a * chunks + q] == wanted[h], 0.0, -START_COST)
                out.append(reward[h, a * chunks + q] + before)
            top, _, total = weigh(out)
            store_value(h, q, top, total, spare_ref)
        return inner

    lax.fori_loop(0, chunks, first_chunk, 0, unroll=2)

    def backup(values, into):
        bring_halo(values)

        def one_chunk(q, inner):
            for h in range(halves):
                top, _, total = weighed_turns(values, reward, index, h, q, turns, chunks)
                store_value(h, q, top, total, into)
            return inner

        lax.fori_loop(0, chunks, one_chunk, 0, unroll=chunks)

    def two_backups(step, carry):
        backup(spare_ref, ext_ref)
        backup(ext_ref, spare_ref)
        return carry

    lax.fori_loop(0, (HORIZON - 2) // 2, two_backups, 0)
    backup(spare_ref, ext_ref)
    bring_halo(ext_ref)


def push_kernel(
    grid_x, scale, halves, dest_ref, *refs
):
    mine, other, graph_mine, graph_other = (refs[i * halves : (i + 1) * halves] for i in range(4))
    (
        ext_ref, raised_ref, max_ref, inv_ref, keep_ref, send_ref, counts, ends, order, values, source,
        slot, going, policy, flows, back, scaled, total, arrived, side_pad, raw,
    ) = refs[4 * halves :]
    blocks = 8 * halves
    share = mine[0].shape[0]
    chunks = max_ref.shape[1]
    edges = raised_ref.shape[1]
    turns = edges // chunks
    per_block = chunks * LANES
    slots = chunks + 4
    dest = renumbered(dest_ref[own_block(grid_x)], per_block, blocks, grid_x)
    core = lax.axis_index("dst")
    side_pad[...] = jnp.zeros_like(side_pad)

    def unpack(first, second):
        for h in range(halves):
            for n in range(slots):
                ends[h, n] = first[h][ROWS + n]
                order[h, n] = first[h][ROWS + slots + n].astype(jnp.int32)
                row = inverse_row(n, slots)
                inverse = (first[h][row] if row < share else second[h][row - share]).astype(jnp.int32)
                values[h, n] = lane_gather(ext_ref[h, n], inverse)

            def rows(r, carry, h=h):
                source[h, r] = first[h][r].astype(jnp.int32)
                policy[h, r] = second[h][r]
                return carry

            lax.fori_loop(0, ROWS, rows, 0, unroll=6)
            for r in range(ROWS, DEPTH):
                source[h, r] = jnp.zeros((8, LANES), jnp.int32)
                policy[h, r] = jnp.zeros((8, LANES), jnp.float32)
            for n in range(4 * chunks):
                back[h, n] = second[h][ROWS + n].astype(jnp.int32) - 1

    by_core(unpack, mine, other)

    def first_anchors():
        for h in range(halves):
            for q in range(4):
                total[h, q] = graph_mine[h][edges + 4 + q]
                total[h, 4 + q] = mine[h][share - 4 + q]

    def second_anchors():
        for h in range(halves):
            for q in range(chunks):
                total[h, q] = graph_mine[h][edges + q]

    pl.when(core == 0)(first_anchors)
    pl.when(core != 0)(second_anchors)
    deepest = jnp.max(functools.reduce(jnp.maximum, [ends[h, slots - 1] for h in range(halves)]))
    deepest = deepest.astype(jnp.int32)
    fits = deepest <= ROWS
    steps = jnp.where(deepest <= USUAL, USUAL // STEP, DEPTH // STEP)
    shifts = ((1, -1), (0, 1), (3, -grid_x), (2, grid_x))

    def shown(h, side):
        facing, by = shifts[side]
        start = 8 + 8 * h + by
        return side_pad[facing, start : start + 8, :]

    @pl.when(jnp.logical_not(fits))
    def _():
        for h in range(halves):
            for n in range(slots):
                order[h, n] = lax.broadcasted_iota(jnp.int32, (8, LANES), 1)

    for h in range(halves):
        for side in range(4):
            side_pad[side, 8 + 8 * h : 16 + 8 * h, :] = order[h, chunks + side].astype(jnp.float32)
    for h in range(halves):
        for side in range(4):
            lanes = shown(h, side).astype(jnp.int32)
            for q in range(chunks):
                entry = back[h, side * chunks + q]
                back[h, side * chunks + q] = jnp.where(
                    entry >= 0, lane_gather(lanes, jnp.maximum(entry, 0)), -1
                )

    def prepare_rows(rows):
        row_before = [None] * halves
        for i, r in enumerate(rows):
            for h in range(halves):
                src = source[h, r]
                place = jnp.asarray(r).astype(jnp.float32)
                row = functools.reduce(
                    jnp.add, [jnp.where(ends[h, n] <= place, 1, 0) for n in range(slots)]
                )
                slot[h, r] = row
                if i:
                    going[h, r] = jnp.where(row == row_before[h], 1.0, 0.0)
                row_before[h] = row
                bits = [(row & (1 << n)) != 0 for n in range(4)]
                picked = tree_select([values[h, n] for n in range(slots)], bits)
                top = table_gather([max_ref[h, q] for q in range(chunks)], src)
                policy[h, r] = jnp.exp(policy[h, r] + picked - top)

    def prepare_step(t, carry):
        prepare_rows([t * STEP + i for i in range(STEP)])
        return carry

    usual = deepest <= USUAL
    pl.when(usual)(lambda: prepare_rows(range(USUAL)))
    lax.fori_loop(0, jnp.where(usual, 0, steps), prepare_step, 0)
    for h in range(halves):
        for q in range(chunks):
            first = jnp.where(target_mask(dest, h, q, per_block), 0.0, total[h, q])
            total[h, q] = first
            scaled[h, q] = first * inv_ref[h, q]

    @pl.when(jnp.logical_not(fits))
    def _():
        def keep_turns(first, second):
            for h in range(halves):

                def rows(e, carry, h=h):
                    raw[h, e] = second[h][e].astype(jnp.int32)
                    return carry

                lax.fori_loop(0, edges, rows, 0)

        by_core(keep_turns, graph_mine, graph_other)

    zero = jnp.zeros((8, LANES), jnp.float32)

    def keep(h):
        for side in range(4):
            side_pad[side, 8 + 8 * h : 16 + 8 * h, :] = arrived[h, chunks + side]

    def add_flow(acc, row, flow):
        return [acc[n] + jnp.where(row == n, flow, 0.0) for n in range(slots)]

    def sum_arranged():
        for h in range(halves):
            for n in range(slots):
                arrived[h, n] = zero

        def one_step(t, carry):
            tables = [[scaled[h, q] for q in range(chunks)] for h in range(halves)]
            step_sums = [[zero] * slots for h in range(halves)]
            so_far = [None] * halves
            for i in range(STEP):
                r = t * STEP + i
                for h in range(halves):
                    flow = table_gather(tables[h], source[h, r]) * policy[h, r]
                    so_far[h] = flow + going[h, r] * so_far[h] if i else flow
                    row = slot[h, r]
                    step_sums[h] = [jnp.where(row == n, so_far[h], step_sums[h][n]) for n in range(slots)]
            for h in range(halves):
                for n in range(slots):
                    arrived[h, n] = arrived[h, n] + step_sums[h][n]
            return carry

        def usual_rows():
            for h in range(halves + 1):
                sums = [zero] * slots
                table = [scaled[h, q] for q in range(chunks)] if h < halves else None
                for r in range(USUAL):
                    if h < halves:
                        flow = table_gather(table, source[h, r]) * policy[h, r]
                        so_far = flow + going[h, r] * so_far if r else flow
                        flows[h, r] = so_far
                    if h:
                        row, summed = slot[h - 1, r], flows[h - 1, r]
                        sums = [jnp.where(row == n, summed, sums[n]) for n in range(slots)]
                if h:
                    for n in range(slots):
                        arrived[h - 1, n] = sums[n]

        pl.when(usual)(usual_rows)
        lax.fori_loop(0, jnp.where(usual, 0, steps), one_step, 0)
        for h in range(halves):
            keep(h)

    def sum_turned():
        lane = lax.broadcasted_iota(jnp.int32, (8, LANES), 1)
        for h in range(halves):

            def one_edge_row(e, acc, h=h):
                flow = scaled[h, lax.rem(e, chunks)] * raised_ref[h, e]
                where = raw[h, e]

                def one_turn(k, state):
                    flow, where, acc = state[0], state[1], list(state[2:])
                    here = jnp.where((where & (LANES - 1)) == lane, where >> 7, -1)
                    acc = add_flow(acc, here, flow)
                    return (pltpu.roll(flow, 1, 1), pltpu.roll(where, 1, 1), *acc)

                return tuple(lax.fori_loop(0, LANES, one_turn, (flow, where, *acc))[2:])

            for n, value in enumerate(lax.fori_loop(0, edges, one_edge_row, (zero,) * slots)):
                arrived[h, n] = value
            keep(h)

    def push(round_index, carry):
        pl.when(fits)(sum_arranged)
        pl.when(jnp.logical_not(fits))(sum_turned)
        for h in range(halves):
            landed = [shown(h, side) for side in range(4)]
            for q in range(chunks):
                value = lane_gather(arrived[h, q], order[h, q])
                for side in range(4):
                    entry = back[h, side * chunks + q]
                    got = lane_gather(landed[side], jnp.maximum(entry, 0))
                    value = value + jnp.where(entry >= 0, got, 0.0)
                value = jnp.where(target_mask(dest, h, q, per_block), 0.0, value)
                total[h, q] = total[h, q] + value
                scaled[h, q] = value * inv_ref[h, q]
        return carry

    lax.fori_loop(0, HORIZON - 1, push, 0)
    rows_out = edges // 2
    apart = counts.shape[1] // blocks
    for h in range(halves):
        for q in range(chunks):
            weight = total[h, q] * inv_ref[h, q] * scale
            for part, piece in ((core, 0), (1 - core, 1)):
                for a in range(turns // 2):
                    value = weight * raised_ref[h, (part * (turns // 2) + a) * chunks + q]
                    start = h * 8 * apart + a * chunks + q
                    counts[piece, pl.ds(start, 8, stride=apart), :] = value
    for piece, out_ref in ((0, keep_ref), (1, send_ref)):
        for b in range(blocks):
            out_ref[b * rows_out : (b + 1) * rows_out, :] = counts[
                piece, b * apart : b * apart + rows_out, :
            ]


VMEM_SPEC = pl.BlockSpec(memory_space=pltpu.VMEM)
SMEM_SPEC = pl.BlockSpec(memory_space=pltpu.SMEM)
HBM_SPEC = pl.BlockSpec(memory_space=pltpu.HBM)
PARAMS = pltpu.CompilerParams(vmem_limit_bytes=48 * 1024 * 1024)


def f32(*shape):
    return jax.ShapeDtypeStruct(shape, jnp.float32)


def call_graph(cost_weights, features, successors, turn_valid, border_lists, anchors):
    turns, width = successors.shape
    blocks = anchors.shape[0]
    chunks = width // LANES
    rows = turns * chunks + 8
    return pl.pallas_call(
        graph_kernel,
        out_shape=(f32(blocks * rows, LANES), f32(turns, width)),
        in_specs=[SMEM_SPEC] + [HBM_SPEC] * 5,
        out_specs=(VMEM_SPEC, VMEM_SPEC),
        scratch_shapes=[
            pltpu.VMEM(features.shape, features.dtype),
            pltpu.VMEM(successors.shape, jnp.int32),
            pltpu.VMEM(turn_valid.shape, jnp.int32),
            pltpu.VMEM(border_lists.shape, jnp.int32),
            pltpu.VMEM(anchors.shape, jnp.float32),
            pltpu.VMEM((rows, LANES), jnp.float32),
            pltpu.VMEM((blocks * chunks + 8, LANES), jnp.float32),
            pltpu.SemaphoreType.DMA((8,)),
        ],
        compiler_params=pltpu.CompilerParams(vmem_limit_bytes=63 * 1024 * 1024),
        name="own_graph",
    )(cost_weights, features, successors, turn_valid, border_lists, anchors)


def call_arrange(successors, turn_valid, border_lists, anchors, reward):
    chunks = successors.shape[1] // LANES
    share = ROWS + 3 * (chunks + 4)
    blocks = anchors.shape[0]
    return pl.pallas_call(
        arrange_kernel,
        out_shape=f32(blocks * share, LANES),
        in_specs=[HBM_SPEC] * 4 + [VMEM_SPEC],
        out_specs=HBM_SPEC,
        scratch_shapes=[
            pltpu.VMEM(successors.shape, jnp.int32),
            pltpu.VMEM(turn_valid.shape, jnp.int32),
            pltpu.VMEM(border_lists.shape, jnp.int32),
            pltpu.VMEM(anchors.shape, jnp.float32),
            pltpu.VMEM((blocks * chunks, LANES), jnp.float32),
            pltpu.VMEM((2 * share, LANES), jnp.float32),
            *[pltpu.VMEM((16, LANES), jnp.float32)] * 5,
            pltpu.VMEM((8, LANES), jnp.float32),
            pltpu.VMEM(successors.shape, jnp.float32),
            pltpu.VMEM(successors.shape, jnp.float32),
            pltpu.VMEM(successors.shape[::-1], jnp.float32),
            pltpu.VMEM((5 * RANKS, LANES), jnp.float32),
            pltpu.SemaphoreType.DMA((2 * blocks,)),
        ],
        compiler_params=PARAMS,
        cost_estimate=pl.CostEstimate(flops=4_000_000_000, bytes_accessed=400_000, transcendentals=0),
        name="arrange_turns",
    )(successors, turn_valid, border_lists, anchors, reward)


def call_regroup(pieces, blocks):
    return pl.pallas_call(
        regroup_kernel,
        out_shape=(f32(pieces.shape[0] // blocks, 8, LANES),) * (blocks // 8),
        in_specs=[VMEM_SPEC],
        out_specs=(VMEM_SPEC,) * (blocks // 8),
        scratch_shapes=[
            pltpu.VMEM((blocks * padded_rows(pieces.shape[0] // blocks), LANES), jnp.float32)
        ],
        compiler_params=PARAMS,
        name="regroup",
    )(pieces)


def call_values(destinations, mine, other, blocks, grid_x, turns, chunks):
    halves = blocks // 8
    edges = turns * chunks
    rows = (halves, edges, 8, LANES)
    return pl.pallas_call(
        functools.partial(value_kernel, grid_x, halves),
        out_shape=(
            f32(halves, chunks + 4, 8, LANES),
            f32(*rows),
            jax.ShapeDtypeStruct(rows, jnp.int32),
        ),
        in_specs=[SMEM_SPEC] + [VMEM_SPEC] * (2 * halves),
        out_specs=(VMEM_SPEC,) * 3,
        scratch_shapes=[
            pltpu.VMEM((halves, 4, 8, LANES), jnp.int32),
            pltpu.VMEM((4, blocks + 16, LANES), jnp.float32),
            pltpu.VMEM((halves, chunks + 4, 8, LANES), jnp.float32),
        ],
        compiler_params=PARAMS,
        cost_estimate=pl.CostEstimate(flops=40_000_000, bytes_accessed=40_000_000, transcendentals=2_000_000),
        name="soft_values",
    )(destinations, *mine, *other)


def call_policy(ext, reward, index):
    halves, edges = reward.shape[:2]
    chunks = ext.shape[1] - 4
    return pl.pallas_call(
        policy_kernel,
        out_shape=(f32(*reward.shape), f32(halves, chunks, 8, LANES), f32(halves, chunks, 8, LANES)),
        in_specs=[VMEM_SPEC] * 3,
        out_specs=(VMEM_SPEC,) * 3,
        compiler_params=PARAMS,
        cost_estimate=pl.CostEstimate(flops=5_000_000, bytes_accessed=5_000_000, transcendentals=200_000),
        name="policy",
    )(ext, reward, index)


def call_push(destinations, mine, other, graph_mine, graph_other, ext, raised, top, inv, grid_x, scale):
    halves, edges = raised.shape[:2]
    blocks = 8 * halves
    chunks = top.shape[1]

    def vmem(rows, dtype=jnp.float32):
        return pltpu.VMEM((halves, rows, 8, LANES), dtype)

    return pl.pallas_call(
        functools.partial(push_kernel, grid_x, scale, halves),
        out_shape=(f32(blocks * edges // 2, LANES),) * 2,
        in_specs=[SMEM_SPEC] + [VMEM_SPEC] * (4 * halves + 4),
        out_specs=(VMEM_SPEC,) * 2,
        scratch_shapes=[
            pltpu.VMEM((2, blocks * padded_rows(edges // 2), LANES), jnp.float32),
            vmem(chunks + 4),
            vmem(chunks + 4, jnp.int32),
            vmem(chunks + 4),
            vmem(DEPTH, jnp.int32),
            vmem(DEPTH, jnp.int32),
            vmem(DEPTH),
            vmem(DEPTH),
            vmem(USUAL),
            vmem(4 * chunks, jnp.int32),
            vmem(chunks),
            vmem(chunks),
            vmem(chunks + 4),
            pltpu.VMEM((4, blocks + 16, LANES), jnp.float32),
            vmem(edges, jnp.int32),
        ],
        compiler_params=PARAMS,
        name="push_mass",
    )(destinations, *mine, *other, *graph_mine, *graph_other, ext, raised, top, inv)


def to_blocks(array):
    return lax.all_to_all(array, BLOCK_AXES, 0, 0, tiled=True)


def other_core(array):
    return lax.ppermute(array, "dst", [(0, 1), (1, 0)])


def per_destination(
    features, cost_weights, successors, turn_valid, border_lists, destinations, anchors, demo_counts
):
    turns, own_count = successors.shape
    chunks = own_count // LANES
    edges = turns * chunks
    grid_x = lax.axis_size("gx")
    blocks = lax.axis_size("gy") * grid_x
    groups = lax.axis_size("dst")
    pieces, reward = call_graph(cost_weights, features, successors, turn_valid, border_lists, anchors)
    graph = to_blocks(pieces)
    arranged = call_arrange(successors, turn_valid, border_lists, anchors, reward)
    core = lax.axis_index("dst")
    demo_term = jnp.where(turn_valid == 1, demo_counts, 0).astype(jnp.float32) / 3.0
    own_feats = lax.dynamic_slice_in_dim(features, core * (turns // 2), turns // 2, axis=1)
    first_core, own_feats, demo_term, arranged = lax.optimization_barrier(
        (core == 0, own_feats, demo_term, arranged)
    )
    graph = lax.optimization_barrier((graph, arranged))[0]
    arranged = to_blocks(arranged)
    graph = call_regroup(graph, blocks)
    graph = (graph, [other_core(half) for half in graph])
    ext, reward, index = call_values(destinations, *graph, blocks, grid_x, turns, chunks)
    arranged, ext = lax.optimization_barrier((arranged, ext))
    arranged = call_regroup(arranged, blocks)
    *arranged, ext = lax.optimization_barrier((*arranged, ext))
    arranged = (arranged, [other_core(half) for half in arranged])
    values = (ext, *call_policy(ext, reward, index))
    scale = 1.0 / (anchors.shape[0] * groups * HORIZON)
    kept, sent = call_push(destinations, *arranged, *graph, *values, grid_x, scale)
    halved = (kept + other_core(sent)).reshape(blocks, edges // 2, LANES)
    half = jnp.sum(to_blocks(halved), axis=0)
    other = other_core(half)
    part = (turns // 2, own_count)
    own_gap = lax.dynamic_slice_in_dim(demo_term, core * part[0], part[0]) - half.reshape(part)
    own_feats = own_feats.astype(jnp.float32)
    block_term = jnp.sum(own_gap[None] * own_feats, axis=(1, 2)) / (own_count * blocks)
    visits = jnp.concatenate([jnp.where(first_core, half, other), jnp.where(first_core, other, half)])
    count_gap = demo_term - visits.reshape(turns, own_count)
    terms = jnp.broadcast_to(block_term, (groups * blocks, 1, block_term.shape[0]))
    terms = lax.all_to_all(terms, (*BLOCK_AXES, "dst"), 0, 0, tiled=True)
    terms, count_gap = lax.optimization_barrier((terms, count_gap))
    return count_gap, jnp.sum(terms, axis=(0, 1))


def passed_along(array, axis, by):
    length = lax.axis_size(axis)
    pairs = [(i, i + by) for i in range(length) if 0 <= i + by < length]
    return lax.ppermute(array, axis, pairs)


def bring_values(values, border_lists):
    outgoing = values[:, border_lists]
    north_part = passed_along(outgoing[:, 1], "gx", 1)
    south_part = passed_along(outgoing[:, 0], "gx", -1)
    west_part = passed_along(outgoing[:, 3], "gy", 1)
    east_part = passed_along(outgoing[:, 2], "gy", -1)
    return jnp.concatenate([north_part, south_part, west_part, east_part], axis=1)


def return_flow(arrived, border_lists, own_count, border_width):
    local_part = arrived[:, :own_count]
    halo_part = arrived[:, own_count:].reshape(arrived.shape[0], 4, border_width)
    from_south = passed_along(halo_part[:, 0], "gx", -1)
    from_north = passed_along(halo_part[:, 1], "gx", 1)
    from_east = passed_along(halo_part[:, 2], "gy", -1)
    from_west = passed_along(halo_part[:, 3], "gy", 1)
    returned = jnp.stack([from_north, from_south, from_west, from_east], axis=1)
    return local_part.at[:, border_lists].add(returned)


def select_cells(cells, flat_index, turn_shape):
    picked = jnp.take(cells, flat_index, axis=1)
    return picked.reshape(cells.shape[0], turn_shape[0], turn_shape[1])


def turn_scores(values, halo_cells, reward, flat_turns, usable):
    extended = jnp.concatenate([values, halo_cells], axis=1)
    scores = reward[None] + select_cells(extended, flat_turns, usable.shape)
    return jnp.where(usable[None], scores, NEG)


def per_block(
    features, cost_weights, successors, turn_valid, border_lists, destinations, anchors, demo_counts
):
    own_count = successors.shape[1]
    border_width = border_lists.shape[1]
    dest_count = anchors.shape[0]
    slot_total = own_count + 4 * border_width
    block_index = lax.axis_index("gx") * lax.axis_size("gy") + lax.axis_index("gy")
    positions = jnp.arange(own_count, dtype=jnp.int32)
    is_target = positions[None, :] == (destinations - block_index * own_count)[:, None]
    usable = turn_valid == 1
    feats = features.astype(jnp.float32)
    reward = -jnp.sum(feats * cost_weights[:, None, None], axis=0)
    flat_turns = successors.reshape(-1)
    values = jnp.where(is_target, 0.0, -START_COST).astype(jnp.float32)
    for round_index in range(HORIZON):
        halo_cells = bring_values(values, border_lists)
        scores = turn_scores(values, halo_cells, reward, flat_turns, usable)
        row_max = jnp.max(scores, axis=1)
        new_values = row_max + jnp.log(jnp.sum(jnp.exp(scores - row_max[:, None]), axis=1))
        values = jnp.where(is_target, 0.0, new_values)
    halo_cells = bring_values(values, border_lists)
    scores = turn_scores(values, halo_cells, reward, flat_turns, usable)
    row_max = jnp.max(scores, axis=1)
    raised = jnp.exp(scores - row_max[:, None])
    policy = raised / jnp.sum(raised, axis=1, keepdims=True)
    mass_now = jnp.where(is_target, 0.0, anchors)
    turn_counts = jnp.zeros(successors.shape, jnp.float32)
    for round_index in range(HORIZON):
        turn_flow = mass_now[:, None, :] * policy
        turn_counts = turn_counts + jnp.sum(turn_flow, axis=0)
        if round_index + 1 < HORIZON:
            arrived = (
                jnp.zeros((dest_count, slot_total), jnp.float32)
                .at[:, flat_turns]
                .add(turn_flow.reshape(dest_count, -1))
            )
            landed = return_flow(arrived, border_lists, own_count, border_width)
            mass_now = jnp.where(is_target, 0.0, landed)
    local_visits = turn_counts / (dest_count * lax.axis_size("dst") * HORIZON)
    visits = lax.psum(local_visits, "dst")
    demo_term = jnp.where(usable, demo_counts, 0).astype(jnp.float32) / 3.0
    count_gap = demo_term - visits
    total_segments = own_count * lax.axis_size("gx") * lax.axis_size("gy")
    own_gap = demo_term / lax.axis_size("dst") - local_visits
    block_term = jnp.sum(own_gap[None] * feats, axis=(1, 2)) / total_segments
    gradient = lax.psum(block_term, ("gx", "gy", "dst"))
    return (count_gap, gradient)


def local(features, cost_weights, successors, turn_valid, border_lists, destinations, anchors, demo_counts):
    args = (
        features, cost_weights, successors, turn_valid, border_lists, destinations, anchors, demo_counts
    )
    blocks = lax.axis_size("gx") * lax.axis_size("gy")
    fits = (
        anchors.shape[0] == blocks
        and blocks % 8 == 0
        and lax.axis_size("dst") == 2
        and lax.axis_size("gx") in (2, 4, 8)
        and lax.axis_size("gy") in (2, 4, 8)
        and successors.shape[1] == 8 * LANES
        and border_lists.shape[1] == LANES
        and successors.shape[0] == 8
    )
    return per_destination(*args) if fits else per_block(*args)


def solution(mesh):
    in_specs = (
        P(None, None, ("gx", "gy")),
        P(),
        P(None, ("gx", "gy")),
        P(None, ("gx", "gy")),
        P(None, ("gx", "gy")),
        P("dst"),
        P("dst", ("gx", "gy")),
        P(None, ("gx", "gy")),
    )
    out_specs = (P(None, ("gx", "gy")), P())
    return jax.shard_map(local, mesh=mesh, in_specs=in_specs, out_specs=out_specs, check_vma=False)
```

```python
import functools

import jax
import jax.numpy as jnp
from jax import lax
from jax.experimental import pallas as pl
from jax.experimental.pallas import tpu as pltpu
from jax.sharding import PartitionSpec as P

HORIZON = 8
NEG = -1e30
START_COST = 100.0
LANES = 128
ROWS = 60
RANKS = -(-ROWS // 16) * 16
STEP = 14
USUAL = 56
DEPTH = -(-ROWS // STEP) * STEP
BLOCK_AXES = ("gy", "gx")

LANE_PICK = lax.GatherDimensionNumbers(
    offset_dims=(),
    collapsed_slice_dims=(1,),
    start_index_map=(1,),
    operand_batching_dims=(0,),
    start_indices_batching_dims=(0,),
)


def lane_gather(table, index):
    return lax.gather(
        table,
        index[..., None],
        LANE_PICK,
        (1, 1),
        mode=lax.GatherScatterMode.PROMISE_IN_BOUNDS,
    )


def tree_select(picked, bits):
    level = list(picked)
    for bit in bits:
        if len(level) == 1:
            break
        nxt = []
        for n in range(0, len(level), 2):
            if n + 1 < len(level):
                nxt.append(jnp.where(bit, level[n + 1], level[n]))
            else:
                nxt.append(level[n])
        level = nxt
    return level[0]


def row_bits(index, count):
    return [(index & (LANES << i)) != 0 for i in range(count)]


def table_gather(table_rows, index):
    lane = index & (LANES - 1)
    bits = row_bits(index, max(len(table_rows) - 1, 1).bit_length())
    return tree_select([lane_gather(row, lane) for row in table_rows], bits)


def run_copies(copies):
    for copy in copies:
        copy.start()
    for copy in copies:
        copy.wait()


def of_blocks(ref, half, row, per_block):
    return ref[pl.ds(half * 8 * per_block + row, 8, stride=per_block), :]


def whole_copies(pairs, sem):
    return [pltpu.make_async_copy(src, dst, sem.at[n]) for n, (src, dst) in enumerate(pairs)]


def by_core(what, mine, other):
    first = lax.axis_index("dst") == 0
    pl.when(first)(lambda: what(mine, other))
    pl.when(jnp.logical_not(first))(lambda: what(other, mine))


def own_block(grid_x):
    return lax.axis_index("gy") * grid_x + lax.axis_index("gx")


def renumbered(segment, per_block, blocks, grid_x):
    grid_y = blocks // grid_x
    block, place = lax.div(segment, per_block), lax.rem(segment, per_block)
    return (lax.rem(block, grid_y) * grid_x + lax.div(block, grid_y)) * per_block + place


def padded_rows(rows):
    tiles = -(-rows // 8)
    return (tiles + 1 - tiles % 2) * 8


def target_mask(dest, half, chunk, per_block):
    sub = lax.broadcasted_iota(jnp.int32, (8, LANES), 0)
    lane = lax.broadcasted_iota(jnp.int32, (8, LANES), 1)
    return (half * 8 + sub) * per_block + chunk * LANES + lane == dest


def arrange_kernel(
    succ_any, valid_any, border_any, anchor_any, reward_ref, out_any,
    succ_ref, valid_ref, border_ref, anchor_ref, split_ref, out_ref, count_ref, first_ref, order_ref, inverse_ref, placed_ref,
    pair_ref, lane_ref, code_ref, column_ref, acc_ref, sem
):
    run_copies(
        whole_copies(
            [
                (succ_any, succ_ref),
                (valid_any, valid_ref),
                (border_any, border_ref),
                (anchor_any, anchor_ref),
            ],
            sem,
        )
    )
    turns, width = succ_ref.shape
    chunks = width // LANES
    slots = chunks + 4
    step = 2 * LANES
    tops = 16
    square = (LANES, LANES)
    down = lax.broadcasted_iota(jnp.int32, square, 0)
    along = lax.broadcasted_iota(jnp.int32, square, 1)
    down_f, along_f = down.astype(jnp.float32), along.astype(jnp.float32)
    before = down < along
    unit = jnp.where(down == along, 1.0, 0.0)
    lane_row = lax.broadcasted_iota(jnp.int32, (LANES, step), 0)
    top_row = lax.broadcasted_iota(jnp.int32, (tops, step), 0)
    rank_row = lax.broadcasted_iota(jnp.int32, (RANKS, step), 0).astype(jnp.float32)
    last_dims = (((1,), (1,)), ((), ()))

    def product(left, right):
        return lax.dot_general(left, right, last_dims, preferred_element_type=jnp.float32)

    def columns(rows):
        return lax.dot_general(
            unit, rows, last_dims, precision=lax.Precision.HIGHEST, preferred_element_type=jnp.float32
        )

    def summed_down(array):
        return jnp.sum(array, axis=0, keepdims=True)

    def place_of(row, col):
        return summed_down(jnp.where((col > row) | ((col == row) & before), 1.0, 0.0))

    def count(a, total):
        for c in range(width // step):
            cols = slice(c * step, (c + 1) * step)
            u = succ_ref[pl.ds(a, 1), cols]
            low = jnp.where(valid_ref[pl.ds(a, 1), cols] == 1, u & (LANES - 1), -1)
            hot_low = jnp.where(low == lane_row, 1.0, 0.0).astype(jnp.bfloat16)
            hot_top = jnp.where((u >> 7) == top_row, 1.0, 0.0).astype(jnp.bfloat16)
            total = total + product(hot_top, hot_low)
        return total

    counts = lax.fori_loop(0, turns, count, jnp.zeros((tops, LANES), jnp.float32), unroll=2)
    count_columns = columns(counts)
    out_ref[...] = jnp.zeros_like(out_ref)
    for ref in (count_ref, first_ref, order_ref, inverse_ref, placed_ref, pair_ref):
        ref[...] = jnp.zeros_like(ref)
    for n in range(slots):
        i = n if n < chunks else n - chunks
        place = place_of(counts[n : n + 1, :], count_columns[:, n : n + 1])
        place = place if i % 2 == 0 else (LANES - 1.0) - place
        if (i // 2) % 2:
            place = jnp.where(place >= LANES // 2, place - LANES // 2, place + LANES // 2)
        first_ref[n : n + 1, :] = place
    first_columns = columns(first_ref[...])
    for n in range(slots):
        hit = first_columns[:, n : n + 1] == along_f
        inverse_ref[n : n + 1, :] = summed_down(jnp.where(hit, down_f, 0.0))
        placed_ref[n : n + 1, :] = summed_down(jnp.where(hit, count_columns[:, n : n + 1], 0.0))
    local = summed_down(placed_ref[0:chunks, :])
    room = -summed_down(placed_ref[chunks:tops, :])
    pair_ref[0:1, :] = local
    pair_ref[1:2, :] = room
    pair = columns(pair_ref[...])
    local_place, room_place = place_of(local, pair[:, 0:1]), place_of(room, pair[:, 1:2])
    pair_ref[0:1, :] = local_place
    pair_ref[1:2, :] = room_place
    pair = columns(pair_ref[...])
    goes = summed_down(jnp.where(pair[:, 1:2] == local_place, down_f, 0.0))
    comes = summed_down(jnp.where(pair[:, 0:1] == room_place, down_f, 0.0))
    full = (chunks, LANES)
    comes = jnp.broadcast_to(comes, full).astype(jnp.int32)
    goes = jnp.broadcast_to(goes, full)
    order_ref[0:chunks, :] = lane_gather(goes, first_ref[0:chunks, :].astype(jnp.int32))
    order_ref[chunks:tops, :] = first_ref[chunks:tops, :]
    inverse_ref[0:chunks, :] = lane_gather(inverse_ref[0:chunks, :], comes)
    placed_ref[0:chunks, :] = lane_gather(placed_ref[0:chunks, :], comes)
    running = jnp.zeros((1, LANES), jnp.float32)
    for n in range(slots):
        count_ref[n : n + 1, :] = running
        running = running + placed_ref[n : n + 1, :]
        out_ref[ROWS + n : ROWS + n + 1, :] = running
        out_ref[ROWS + slots + n : ROWS + slots + n + 1, :] = order_ref[n : n + 1, :]
        row = inverse_row(n, slots)
        out_ref[row : row + 1, :] = inverse_ref[n : n + 1, :]
    for k in range(chunks):
        cols = slice(k * LANES, (k + 1) * LANES)
        u = succ_ref[:, cols]
        rows = [jnp.broadcast_to(order_ref[n : n + 1, :], (turns, LANES)) for n in range(slots)]
        lane = jnp.where(valid_ref[:, cols] == 1, table_gather(rows, u), -1.0)
        code = jnp.where(lane >= 0.0, lane + ((u >> 7) * LANES).astype(jnp.float32), -1.0)
        lane_ref[:, cols] = lane
        code_ref[:, cols] = code
        column_ref[cols, :] = columns(code)
    acc_ref[...] = jnp.zeros_like(acc_ref)
    earlier = jnp.where(
        lax.broadcasted_iota(jnp.int32, (step, step), 0) < lax.broadcasted_iota(jnp.int32, (step, step), 1),
        1.0,
        0.0,
    )
    lane_row_f = lane_row.astype(jnp.float32)

    def one_chunk(c, base):
        start = pl.multiple_of(c * step, step)
        cols = pl.ds(start, step)
        s = start + lax.broadcasted_iota(jnp.int32, (1, step), 1)
        source = [
            (s & ~7).astype(jnp.float32).astype(jnp.bfloat16),
            (s & 7).astype(jnp.float32).astype(jnp.bfloat16),
        ]
        for a in range(turns):
            row = slice(a, a + 1)
            hot = jnp.where(lane_ref[row, cols] == lane_row_f, 1.0, 0.0).astype(jnp.bfloat16)
            hot_top = jnp.where((succ_ref[row, cols] >> 7) == top_row, 1.0, 0.0)
            same = column_ref[cols, row] == code_ref[row, cols]
            within = summed_down(jnp.where(same, earlier, 0.0))
            coarse = (base.astype(jnp.int32) & ~127).astype(jnp.float32)
            both = jnp.concatenate([coarse, base - coarse], axis=0).astype(jnp.bfloat16)
            starts = jnp.dot(both, hot, preferred_element_type=jnp.float32)
            begin = summed_down((starts[:tops] + starts[tops:]) * hot_top)
            base = base + product(hot_top.astype(jnp.bfloat16), hot)
            match = jnp.where(begin + within == rank_row, 1.0, 0.0).astype(jnp.bfloat16)
            r = reward_ref[row, cols]
            r1 = r.astype(jnp.bfloat16)
            rest = r - r1.astype(jnp.float32)
            r2 = rest.astype(jnp.bfloat16)
            r3 = (rest - r2.astype(jnp.float32)).astype(jnp.bfloat16)
            left = jnp.concatenate([match * piece for piece in (*source, r1, r2, r3)], axis=0)
            acc_ref[...] += product(left, hot)
        return base

    lax.fori_loop(0, width // step, one_chunk, count_ref[...])
    part = [acc_ref[i * RANKS : i * RANKS + ROWS, :] for i in range(5)]
    share = out_ref.shape[0] // 2
    out_ref[0:ROWS, :] = part[0] + part[1]
    out_ref[share : share + ROWS, :] = (part[2] + part[3]) + part[4]
    listed = columns(border_ref[...].astype(jnp.float32)).astype(jnp.int32)
    for side in range(4):
        for q in range(chunks):
            found = jnp.where(listed[:, side : side + 1] == along + q * LANES, down_f + 1.0, 0.0)
            row = share + ROWS + side * chunks + q
            out_ref[row : row + 1, :] = summed_down(found)
    blocks = anchor_ref.shape[0]
    for q in range(chunks):
        split_ref[pl.ds(q, blocks, chunks), :] = anchor_ref[:, q * LANES : (q + 1) * LANES]
    start = pl.multiple_of(lax.axis_index("dst") * share, 8)
    common = share - chunks
    shared = out_ref[pl.ds(start + common, chunks), :]
    sub = lax.broadcasted_iota(jnp.int32, (chunks, LANES), 0)
    own_rows = (lax.axis_index("dst") == 0) & (sub >= 4)
    for b in range(blocks):
        rows = slice(b * chunks, (b + 1) * chunks)
        split_ref[rows, :] = jnp.where(own_rows, split_ref[rows, :], shared)
    half = out_ref.at[pl.ds(start, common)]
    pairs = []
    for b in range(blocks):
        pairs.append((half, out_any.at[pl.ds(b * share, common)]))
        pairs.append((split_ref.at[pl.ds(b * chunks, chunks)], out_any.at[pl.ds(b * share + common, chunks)]))
    run_copies(whole_copies(pairs, sem))


def inverse_row(n, slots):
    if n < slots - 4:
        return ROWS + 2 * slots + n
    return 2 * (ROWS + 3 * slots) - slots + n


def graph_kernel(
    weight_ref, feature_any, succ_any, valid_any, border_any, anchor_any, out_ref, reward_ref,
    feature_ref, succ_ref, valid_ref, border_ref, anchor_ref, part_ref, split_ref, sem
):
    run_copies(
        whole_copies(
            [
                (feature_any, feature_ref),
                (succ_any, succ_ref),
                (valid_any, valid_ref),
                (border_any, border_ref),
                (anchor_any, anchor_ref),
            ],
            sem,
        )
    )
    turns, width = succ_ref.shape
    chunks = width // LANES
    edges = turns * chunks
    part_ref[edges : edges + 8, :] = jnp.zeros((8, LANES), jnp.float32)
    part_ref[edges : edges + 4, :] = border_ref[...].astype(jnp.float32)
    blocks = anchor_ref.shape[0]
    split_ref[0:8, :] = jnp.zeros((8, LANES), jnp.float32)
    first_core = lax.axis_index("dst") == 0
    for q in range(chunks):
        cols = slice(q * LANES, (q + 1) * LANES)
        cost = weight_ref[0] * feature_ref[0, :, cols].astype(jnp.float32)
        for f in range(1, feature_ref.shape[0]):
            cost = cost + weight_ref[f] * feature_ref[f, :, cols].astype(jnp.float32)
        reward_ref[:, cols] = -cost
        masked = jnp.where(valid_ref[:, cols] == 1, -cost, NEG)
        turn_to = succ_ref[:, cols].astype(jnp.float32)
        part_ref[pl.ds(q, turns, chunks), :] = jnp.where(first_core, masked, turn_to)
        split_ref[pl.ds(8 + q, blocks, chunks), :] = anchor_ref[:, cols]
    size = part_ref.shape[0]
    lists = part_ref[edges:size, :]
    upper = lax.broadcasted_iota(jnp.int32, (8, LANES), 0) < 4
    for b in range(blocks):
        out_ref[b * size : b * size + edges, :] = part_ref[0:edges, :]
        own = split_ref[8 + b * chunks : 16 + b * chunks, :]
        lower = split_ref[4 + b * chunks : 12 + b * chunks, :]
        mixed = jnp.where(upper, lists, lower)
        out_ref[b * size + edges : (b + 1) * size, :] = jnp.where(first_core, mixed, own)


def regroup_kernel(pieces_ref, out_ref, padded_ref):
    halves, rows = out_ref.shape[:2]
    size, apart = pieces_ref.shape[0] // (8 * halves), padded_ref.shape[0] // (8 * halves)
    for b in range(8 * halves):
        padded_ref[b * apart : b * apart + size, :] = pieces_ref[b * size : (b + 1) * size, :]
    for h in range(halves):

        def one_row(i, carry, h=h):
            out_ref[h, i] = of_blocks(padded_ref, h, i, apart)
            return carry

        lax.fori_loop(0, rows, one_row, 0, unroll=8)


def weigh(out):
    top = functools.reduce(jnp.maximum, out)
    raised = [jnp.exp(score - top) for score in out]
    return top, raised, functools.reduce(jnp.add, raised)


def weighed_turns(values, reward, index, h, q, turns, chunks):
    tables = [values[h, r] for r in range(chunks + 4)]
    out = []
    for a in range(turns):
        rows = tables if a else tables[:chunks]
        out.append(reward[h, a * chunks + q] + table_gather(rows, index[h, a * chunks + q]))
    return weigh(out)


def policy_kernel(values_ref, reward_ref, index_ref, raised_ref, max_ref, inv_ref):
    halves, chunks = max_ref.shape[:2]
    turns = reward_ref.shape[1] // chunks

    def one_chunk(q, inner):
        for h in range(halves):
            top, raised, total = weighed_turns(values_ref, reward_ref, index_ref, h, q, turns, chunks)
            max_ref[h, q] = top
            inv_ref[h, q] = 1.0 / total
            for a in range(turns):
                raised_ref[h, a * chunks + q] = raised[a]
        return inner

    lax.fori_loop(0, chunks, one_chunk, 0, unroll=chunks)


def value_kernel(
    grid_x, dest_ref, mine_ref, other_ref, ext_ref, reward, index, border, side_pad, spare_ref
):
    halves = ext_ref.shape[0]
    blocks = 8 * halves
    chunks = ext_ref.shape[1] - 4
    edges = reward.shape[1]
    turns = edges // chunks
    per_block = chunks * LANES
    dest = renumbered(dest_ref[own_block(grid_x)], per_block, blocks, grid_x)
    side_pad[...] = jnp.zeros_like(side_pad)
    sub = lax.broadcasted_iota(jnp.int32, (8, LANES), 0)
    lane = lax.broadcasted_iota(jnp.int32, (8, LANES), 1)
    dest_block, dest_place = lax.div(dest, per_block), lax.rem(dest, per_block)

    def unpack(first, second):
        for h in range(halves):

            def rows(i, carry, h=h):
                reward[h, i] = first[h, i]
                index[h, i] = second[h, i].astype(jnp.int32)
                return carry

            lax.fori_loop(0, edges, rows, 0, unroll=8)
            for side in range(4):
                border[h, side] = first[h, edges + side].astype(jnp.int32)

    by_core(unpack, mine_ref, other_ref)
    for h in range(halves):
        for side in range(4):
            found = (border[h, side] == dest_place) & (h * 8 + sub == dest_block)
            entry = jnp.max(jnp.where(found, lane + 1, 0).astype(jnp.float32), axis=1, keepdims=True)
            side_pad[side, 8 + 8 * h : 16 + 8 * h, :] = jnp.broadcast_to(entry, (8, LANES))
    shifts = ((1, -1), (0, 1), (3, -grid_x), (2, grid_x))

    def shown(h, side):
        facing, by = shifts[side]
        start = 8 + 8 * h + by
        return side_pad[facing, start : start + 8, :]

    def dest_index(h):
        where = jnp.where(h * 8 + sub == dest_block, dest_place, -1)
        for side in range(4):
            entry = shown(h, side).astype(jnp.int32)
            where = jnp.where(entry > 0, per_block + side * LANES + entry - 1, where)
        return where

    def bring_halo(values):
        for h in range(halves):
            table = [values[h, q] for q in range(chunks)]
            for side in range(4):
                side_pad[side, 8 + 8 * h : 16 + 8 * h, :] = table_gather(table, border[h, side])
        for h in range(halves):
            for side in range(4):
                values[h, chunks + side] = shown(h, side)

    def store_value(h, q, top, total, into):
        value = top + jnp.log(total)
        into[h, q] = jnp.where(target_mask(dest, h, q, per_block), 0.0, value)

    wanted = [dest_index(h) for h in range(halves)]

    def first_chunk(q, inner):
        for h in range(halves):
            out = []
            for a in range(turns):
                before = jnp.where(index[h, a * chunks + q] == wanted[h], 0.0, -START_COST)
                out.append(reward[h, a * chunks + q] + before)
            top, _, total = weigh(out)
            store_value(h, q, top, total, spare_ref)
        return inner

    lax.fori_loop(0, chunks, first_chunk, 0, unroll=2)

    def backup(values, into):
        bring_halo(values)

        def one_chunk(q, inner):
            for h in range(halves):
                top, _, total = weighed_turns(values, reward, index, h, q, turns, chunks)
                store_value(h, q, top, total, into)
            return inner

        lax.fori_loop(0, chunks, one_chunk, 0, unroll=chunks)

    def two_backups(step, carry):
        backup(spare_ref, ext_ref)
        backup(ext_ref, spare_ref)
        return carry

    for step in range((HORIZON - 2) // 2):
        two_backups(step, 0)
    backup(spare_ref, ext_ref)
    bring_halo(ext_ref)


def push_kernel(
    grid_x, scale, dest_ref, mine_ref, other_ref, graph_mine, graph_other, ext_ref, raised_ref, max_ref,
    inv_ref, keep_ref, send_ref, counts, ends, order, values, source, slot, going, policy, flows, back, scaled, total, arrived, side_pad, raw
):
    halves = ext_ref.shape[0]
    blocks = 8 * halves
    share = mine_ref.shape[1]
    chunks = max_ref.shape[1]
    edges = raised_ref.shape[1]
    turns = edges // chunks
    per_block = chunks * LANES
    slots = chunks + 4
    dest = renumbered(dest_ref[own_block(grid_x)], per_block, blocks, grid_x)
    core = lax.axis_index("dst")
    side_pad[...] = jnp.zeros_like(side_pad)

    def unpack(first, second):
        for h in range(halves):
            for n in range(slots):
                ends[h, n] = first[h, ROWS + n]
                order[h, n] = first[h, ROWS + slots + n].astype(jnp.int32)
                row = inverse_row(n, slots)
                inverse = (first[h, row] if row < share else second[h, row - share]).astype(jnp.int32)
                values[h, n] = lane_gather(ext_ref[h, n], inverse)

            def rows(r, carry, h=h):
                source[h, r] = first[h, r].astype(jnp.int32)
                policy[h, r] = second[h, r]
                return carry

            lax.fori_loop(0, ROWS, rows, 0, unroll=6)
            for r in range(ROWS, DEPTH):
                source[h, r] = jnp.zeros((8, LANES), jnp.int32)
                policy[h, r] = jnp.zeros((8, LANES), jnp.float32)
            for n in range(4 * chunks):
                back[h, n] = second[h, ROWS + n].astype(jnp.int32) - 1

    by_core(unpack, mine_ref, other_ref)

    def first_anchors():
        for h in range(halves):
            for q in range(4):
                total[h, q] = graph_mine[h, edges + 4 + q]
                total[h, 4 + q] = mine_ref[h, share - 4 + q]

    def second_anchors():
        for h in range(halves):
            for q in range(chunks):
                total[h, q] = graph_mine[h, edges + q]

    pl.when(core == 0)(first_anchors)
    pl.when(core != 0)(second_anchors)
    deepest = jnp.max(functools.reduce(jnp.maximum, [ends[h, slots - 1] for h in range(halves)]))
    deepest = deepest.astype(jnp.int32)
    fits = deepest <= ROWS
    steps = jnp.where(deepest <= USUAL, USUAL // STEP, DEPTH // STEP)
    shifts = ((1, -1), (0, 1), (3, -grid_x), (2, grid_x))

    def shown(h, side):
        facing, by = shifts[side]
        start = 8 + 8 * h + by
        return side_pad[facing, start : start + 8, :]

    @pl.when(jnp.logical_not(fits))
    def _():
        for h in range(halves):
            for n in range(slots):
                order[h, n] = lax.broadcasted_iota(jnp.int32, (8, LANES), 1)

    for h in range(halves):
        for side in range(4):
            side_pad[side, 8 + 8 * h : 16 + 8 * h, :] = order[h, chunks + side].astype(jnp.float32)
    for h in range(halves):
        for side in range(4):
            lanes = shown(h, side).astype(jnp.int32)
            for q in range(chunks):
                entry = back[h, side * chunks + q]
                back[h, side * chunks + q] = jnp.where(
                    entry >= 0, lane_gather(lanes, jnp.maximum(entry, 0)), -1
                )

    def prepare_rows(rows):
        row_before = [None] * halves
        for i, r in enumerate(rows):
            for h in range(halves):
                src = source[h, r]
                place = jnp.asarray(r).astype(jnp.float32)
                row = functools.reduce(
                    jnp.add, [jnp.where(ends[h, n] <= place, 1, 0) for n in range(slots)]
                )
                slot[h, r] = row
                if i:
                    going[h, r] = jnp.where(row == row_before[h], 1.0, 0.0)
                row_before[h] = row
                bits = [(row & (1 << n)) != 0 for n in range(4)]
                picked = tree_select([values[h, n] for n in range(slots)], bits)
                top = table_gather([max_ref[h, q] for q in range(chunks)], src)
                policy[h, r] = jnp.exp(policy[h, r] + picked - top)

    def prepare_step(t, carry):
        prepare_rows([t * STEP + i for i in range(STEP)])
        return carry

    usual = deepest <= USUAL
    pl.when(usual)(lambda: prepare_rows(range(USUAL)))
    lax.fori_loop(0, jnp.where(usual, 0, steps), prepare_step, 0)
    for h in range(halves):
        for q in range(chunks):
            first = jnp.where(target_mask(dest, h, q, per_block), 0.0, total[h, q])
            total[h, q] = first
            scaled[h, q] = first * inv_ref[h, q]

    @pl.when(jnp.logical_not(fits))
    def _():
        def keep_turns(first, second):
            for h in range(halves):

                def rows(e, carry, h=h):
                    raw[h, e] = second[h, e].astype(jnp.int32)
                    return carry

                lax.fori_loop(0, edges, rows, 0)

        by_core(keep_turns, graph_mine, graph_other)

    zero = jnp.zeros((8, LANES), jnp.float32)

    def keep(h):
        for side in range(4):
            side_pad[side, 8 + 8 * h : 16 + 8 * h, :] = arrived[h, chunks + side]

    def add_flow(acc, row, flow):
        return [acc[n] + jnp.where(row == n, flow, 0.0) for n in range(slots)]

    def sum_arranged():
        for h in range(halves):
            for n in range(slots):
                arrived[h, n] = zero

        def one_step(t, carry):
            tables = [[scaled[h, q] for q in range(chunks)] for h in range(halves)]
            step_sums = [[zero] * slots for h in range(halves)]
            so_far = [None] * halves
            for i in range(STEP):
                r = t * STEP + i
                for h in range(halves):
                    flow = table_gather(tables[h], source[h, r]) * policy[h, r]
                    so_far[h] = flow + going[h, r] * so_far[h] if i else flow
                    row = slot[h, r]
                    step_sums[h] = [jnp.where(row == n, so_far[h], step_sums[h][n]) for n in range(slots)]
            for h in range(halves):
                for n in range(slots):
                    arrived[h, n] = arrived[h, n] + step_sums[h][n]
            return carry

        def usual_rows():
            for h in range(halves + 1):
                sums = [zero] * slots
                table = [scaled[h, q] for q in range(chunks)] if h < halves else None
                for r in range(USUAL):
                    if h < halves:
                        flow = table_gather(table, source[h, r]) * policy[h, r]
                        so_far = flow + going[h, r] * so_far if r else flow
                        flows[h, r] = so_far
                    if h:
                        row, summed = slot[h - 1, r], flows[h - 1, r]
                        sums = [jnp.where(row == n, summed, sums[n]) for n in range(slots)]
                if h:
                    for n in range(slots):
                        arrived[h - 1, n] = sums[n]

        pl.when(usual)(usual_rows)
        lax.fori_loop(0, jnp.where(usual, 0, steps), one_step, 0)
        for h in range(halves):
            keep(h)

    def sum_turned():
        lane = lax.broadcasted_iota(jnp.int32, (8, LANES), 1)
        for h in range(halves):

            def one_edge_row(e, acc, h=h):
                flow = scaled[h, lax.rem(e, chunks)] * raised_ref[h, e]
                where = raw[h, e]

                def one_turn(k, state):
                    flow, where, acc = state[0], state[1], list(state[2:])
                    here = jnp.where((where & (LANES - 1)) == lane, where >> 7, -1)
                    acc = add_flow(acc, here, flow)
                    return (pltpu.roll(flow, 1, 1), pltpu.roll(where, 1, 1), *acc)

                return tuple(lax.fori_loop(0, LANES, one_turn, (flow, where, *acc))[2:])

            for n, value in enumerate(lax.fori_loop(0, edges, one_edge_row, (zero,) * slots)):
                arrived[h, n] = value
            keep(h)

    def push(round_index, carry):
        pl.when(fits)(sum_arranged)
        pl.when(jnp.logical_not(fits))(sum_turned)
        for h in range(halves):
            landed = [shown(h, side) for side in range(4)]
            for q in range(chunks):
                value = lane_gather(arrived[h, q], order[h, q])
                for side in range(4):
                    entry = back[h, side * chunks + q]
                    got = lane_gather(landed[side], jnp.maximum(entry, 0))
                    value = value + jnp.where(entry >= 0, got, 0.0)
                value = jnp.where(target_mask(dest, h, q, per_block), 0.0, value)
                total[h, q] = total[h, q] + value
                scaled[h, q] = value * inv_ref[h, q]
        return carry

    lax.fori_loop(0, HORIZON - 1, push, 0)
    rows_out = edges // 2
    apart = counts.shape[1] // blocks
    for h in range(halves):
        for q in range(chunks):
            weight = total[h, q] * inv_ref[h, q] * scale
            for part, piece in ((core, 0), (1 - core, 1)):
                for a in range(turns // 2):
                    value = weight * raised_ref[h, (part * (turns // 2) + a) * chunks + q]
                    start = h * 8 * apart + a * chunks + q
                    counts[piece, pl.ds(start, 8, stride=apart), :] = value
    for piece, out_ref in ((0, keep_ref), (1, send_ref)):
        for b in range(blocks):
            out_ref[b * rows_out : (b + 1) * rows_out, :] = counts[
                piece, b * apart : b * apart + rows_out, :
            ]


VMEM_SPEC = pl.BlockSpec(memory_space=pltpu.VMEM)
SMEM_SPEC = pl.BlockSpec(memory_space=pltpu.SMEM)
HBM_SPEC = pl.BlockSpec(memory_space=pltpu.HBM)
PARAMS = pltpu.CompilerParams(vmem_limit_bytes=48 * 1024 * 1024)


def f32(*shape):
    return jax.ShapeDtypeStruct(shape, jnp.float32)


def call_graph(cost_weights, features, successors, turn_valid, border_lists, anchors):
    turns, width = successors.shape
    blocks = anchors.shape[0]
    chunks = width // LANES
    rows = turns * chunks + 8
    return pl.pallas_call(
        graph_kernel,
        out_shape=(f32(blocks * rows, LANES), f32(turns, width)),
        in_specs=[SMEM_SPEC] + [HBM_SPEC] * 5,
        out_specs=(VMEM_SPEC, VMEM_SPEC),
        scratch_shapes=[
            pltpu.VMEM(features.shape, features.dtype),
            pltpu.VMEM(successors.shape, jnp.int32),
            pltpu.VMEM(turn_valid.shape, jnp.int32),
            pltpu.VMEM(border_lists.shape, jnp.int32),
            pltpu.VMEM(anchors.shape, jnp.float32),
            pltpu.VMEM((rows, LANES), jnp.float32),
            pltpu.VMEM((blocks * chunks + 8, LANES), jnp.float32),
            pltpu.SemaphoreType.DMA((5,)),
        ],
        compiler_params=pltpu.CompilerParams(vmem_limit_bytes=63 * 1024 * 1024),
        name="own_graph",
    )(cost_weights, features, successors, turn_valid, border_lists, anchors)


def call_arrange(successors, turn_valid, border_lists, anchors, reward):
    chunks = successors.shape[1] // LANES
    share = ROWS + 3 * (chunks + 4)
    blocks = anchors.shape[0]
    return pl.pallas_call(
        arrange_kernel,
        out_shape=f32(blocks * share, LANES),
        in_specs=[HBM_SPEC] * 4 + [VMEM_SPEC],
        out_specs=HBM_SPEC,
        scratch_shapes=[
            pltpu.VMEM(successors.shape, jnp.int32),
            pltpu.VMEM(turn_valid.shape, jnp.int32),
            pltpu.VMEM(border_lists.shape, jnp.int32),
            pltpu.VMEM(anchors.shape, jnp.float32),
            pltpu.VMEM((blocks * chunks, LANES), jnp.float32),
            pltpu.VMEM((2 * share, LANES), jnp.float32),
            *[pltpu.VMEM((16, LANES), jnp.float32)] * 5,
            pltpu.VMEM((8, LANES), jnp.float32),
            pltpu.VMEM(successors.shape, jnp.float32),
            pltpu.VMEM(successors.shape, jnp.float32),
            pltpu.VMEM(successors.shape[::-1], jnp.float32),
            pltpu.VMEM((5 * RANKS, LANES), jnp.float32),
            pltpu.SemaphoreType.DMA((2 * blocks,)),
        ],
        compiler_params=PARAMS,
        cost_estimate=pl.CostEstimate(flops=4_000_000_000, bytes_accessed=400_000, transcendentals=0),
        name="arrange_turns",
    )(successors, turn_valid, border_lists, anchors, reward)


def call_regroup(pieces, blocks):
    return pl.pallas_call(
        regroup_kernel,
        out_shape=f32(blocks // 8, pieces.shape[0] // blocks, 8, LANES),
        in_specs=[VMEM_SPEC],
        out_specs=VMEM_SPEC,
        scratch_shapes=[
            pltpu.VMEM((blocks * padded_rows(pieces.shape[0] // blocks), LANES), jnp.float32)
        ],
        compiler_params=PARAMS,
        name="regroup",
    )(pieces)


def call_values(destinations, mine, other, blocks, grid_x, turns, chunks):
    halves = blocks // 8
    edges = turns * chunks
    rows = (halves, edges, 8, LANES)
    return pl.pallas_call(
        functools.partial(value_kernel, grid_x),
        out_shape=(
            f32(halves, chunks + 4, 8, LANES),
            f32(*rows),
            jax.ShapeDtypeStruct(rows, jnp.int32),
        ),
        in_specs=[SMEM_SPEC, VMEM_SPEC, VMEM_SPEC],
        out_specs=(VMEM_SPEC,) * 3,
        scratch_shapes=[
            pltpu.VMEM((halves, 4, 8, LANES), jnp.int32),
            pltpu.VMEM((4, blocks + 16, LANES), jnp.float32),
            pltpu.VMEM((halves, chunks + 4, 8, LANES), jnp.float32),
        ],
        compiler_params=PARAMS,
        cost_estimate=pl.CostEstimate(flops=40_000_000, bytes_accessed=40_000_000, transcendentals=2_000_000),
        name="soft_values",
    )(destinations, mine, other)


def call_policy(ext, reward, index):
    halves, edges = reward.shape[:2]
    chunks = ext.shape[1] - 4
    return pl.pallas_call(
        policy_kernel,
        out_shape=(f32(*reward.shape), f32(halves, chunks, 8, LANES), f32(halves, chunks, 8, LANES)),
        in_specs=[VMEM_SPEC] * 3,
        out_specs=(VMEM_SPEC,) * 3,
        compiler_params=PARAMS,
        cost_estimate=pl.CostEstimate(flops=5_000_000, bytes_accessed=5_000_000, transcendentals=200_000),
        name="policy",
    )(ext, reward, index)


def call_push(destinations, mine, other, graph_mine, graph_other, ext, raised, top, inv, grid_x, scale):
    halves, edges = raised.shape[:2]
    blocks = 8 * halves
    chunks = top.shape[1]

    def vmem(rows, dtype=jnp.float32):
        return pltpu.VMEM((halves, rows, 8, LANES), dtype)

    return pl.pallas_call(
        functools.partial(push_kernel, grid_x, scale),
        out_shape=(f32(blocks * edges // 2, LANES),) * 2,
        in_specs=[SMEM_SPEC] + [VMEM_SPEC] * 8,
        out_specs=(VMEM_SPEC,) * 2,
        scratch_shapes=[
            pltpu.VMEM((2, blocks * padded_rows(edges // 2), LANES), jnp.float32),
            vmem(chunks + 4),
            vmem(chunks + 4, jnp.int32),
            vmem(chunks + 4),
            vmem(DEPTH, jnp.int32),
            vmem(DEPTH, jnp.int32),
            vmem(DEPTH),
            vmem(DEPTH),
            vmem(USUAL),
            vmem(4 * chunks, jnp.int32),
            vmem(chunks),
            vmem(chunks),
            vmem(chunks + 4),
            pltpu.VMEM((4, blocks + 16, LANES), jnp.float32),
            vmem(edges, jnp.int32),
        ],
        compiler_params=PARAMS,
        name="push_mass",
    )(destinations, mine, other, graph_mine, graph_other, ext, raised, top, inv)


def to_blocks(array):
    return lax.all_to_all(array, BLOCK_AXES, 0, 0, tiled=True)


def other_core(array):
    return lax.ppermute(array, "dst", [(0, 1), (1, 0)])


def per_destination(
    features, cost_weights, successors, turn_valid, border_lists, destinations, anchors, demo_counts
):
    turns, own_count = successors.shape
    chunks = own_count // LANES
    edges = turns * chunks
    grid_x = lax.axis_size("gx")
    blocks = lax.axis_size("gy") * grid_x
    groups = lax.axis_size("dst")
    pieces, reward = call_graph(cost_weights, features, successors, turn_valid, border_lists, anchors)
    graph = to_blocks(pieces)
    arranged = call_arrange(successors, turn_valid, border_lists, anchors, reward)
    core = lax.axis_index("dst")
    demo_term = jnp.where(turn_valid == 1, demo_counts, 0).astype(jnp.float32) / 3.0
    own_feats = lax.dynamic_slice_in_dim(features, core * (turns // 2), turns // 2, axis=1)
    first_core, own_feats, demo_term, arranged = lax.optimization_barrier(
        (core == 0, own_feats, demo_term, arranged)
    )
    graph = lax.optimization_barrier((graph, arranged))[0]
    arranged = to_blocks(arranged)
    graph = call_regroup(graph, blocks)
    graph = (graph, other_core(graph))
    ext, reward, index = call_values(destinations, *graph, blocks, grid_x, turns, chunks)
    arranged, ext = lax.optimization_barrier((arranged, ext))
    arranged = call_regroup(arranged, blocks)
    arranged, ext = lax.optimization_barrier((arranged, ext))
    arranged = (arranged, other_core(arranged))
    values = (ext, *call_policy(ext, reward, index))
    scale = 1.0 / (anchors.shape[0] * groups * HORIZON)
    kept, sent = call_push(destinations, *arranged, *graph, *values, grid_x, scale)
    halved = (kept + other_core(sent)).reshape(blocks, edges // 2, LANES)
    half = jnp.sum(to_blocks(halved), axis=0)
    other = other_core(half)
    part = (turns // 2, own_count)
    own_gap = lax.dynamic_slice_in_dim(demo_term, core * part[0], part[0]) - half.reshape(part)
    own_feats = own_feats.astype(jnp.float32)
    block_term = jnp.sum(own_gap[None] * own_feats, axis=(1, 2)) / (own_count * blocks)
    visits = jnp.concatenate([jnp.where(first_core, half, other), jnp.where(first_core, other, half)])
    count_gap = demo_term - visits.reshape(turns, own_count)
    terms = jnp.broadcast_to(block_term, (groups * blocks, 1, block_term.shape[0]))
    terms = lax.all_to_all(terms, (*BLOCK_AXES, "dst"), 0, 0, tiled=True)
    terms, count_gap = lax.optimization_barrier((terms, count_gap))
    return count_gap, jnp.sum(terms, axis=(0, 1))


def passed_along(array, axis, by):
    length = lax.axis_size(axis)
    pairs = [(i, i + by) for i in range(length) if 0 <= i + by < length]
    return lax.ppermute(array, axis, pairs)


def bring_values(values, border_lists):
    outgoing = values[:, border_lists]
    north_part = passed_along(outgoing[:, 1], "gx", 1)
    south_part = passed_along(outgoing[:, 0], "gx", -1)
    west_part = passed_along(outgoing[:, 3], "gy", 1)
    east_part = passed_along(outgoing[:, 2], "gy", -1)
    return jnp.concatenate([north_part, south_part, west_part, east_part], axis=1)


def return_flow(arrived, border_lists, own_count, border_width):
    local_part = arrived[:, :own_count]
    halo_part = arrived[:, own_count:].reshape(arrived.shape[0], 4, border_width)
    from_south = passed_along(halo_part[:, 0], "gx", -1)
    from_north = passed_along(halo_part[:, 1], "gx", 1)
    from_east = passed_along(halo_part[:, 2], "gy", -1)
    from_west = passed_along(halo_part[:, 3], "gy", 1)
    returned = jnp.stack([from_north, from_south, from_west, from_east], axis=1)
    return local_part.at[:, border_lists].add(returned)


def select_cells(cells, flat_index, turn_shape):
    picked = jnp.take(cells, flat_index, axis=1)
    return picked.reshape(cells.shape[0], turn_shape[0], turn_shape[1])


def turn_scores(values, halo_cells, reward, flat_turns, usable):
    extended = jnp.concatenate([values, halo_cells], axis=1)
    scores = reward[None] + select_cells(extended, flat_turns, usable.shape)
    return jnp.where(usable[None], scores, NEG)


def per_block(
    features, cost_weights, successors, turn_valid, border_lists, destinations, anchors, demo_counts
):
    own_count = successors.shape[1]
    border_width = border_lists.shape[1]
    dest_count = anchors.shape[0]
    slot_total = own_count + 4 * border_width
    block_index = lax.axis_index("gx") * lax.axis_size("gy") + lax.axis_index("gy")
    positions = jnp.arange(own_count, dtype=jnp.int32)
    is_target = positions[None, :] == (destinations - block_index * own_count)[:, None]
    usable = turn_valid == 1
    feats = features.astype(jnp.float32)
    reward = -jnp.sum(feats * cost_weights[:, None, None], axis=0)
    flat_turns = successors.reshape(-1)
    values = jnp.where(is_target, 0.0, -START_COST).astype(jnp.float32)
    for round_index in range(HORIZON):
        halo_cells = bring_values(values, border_lists)
        scores = turn_scores(values, halo_cells, reward, flat_turns, usable)
        row_max = jnp.max(scores, axis=1)
        new_values = row_max + jnp.log(jnp.sum(jnp.exp(scores - row_max[:, None]), axis=1))
        values = jnp.where(is_target, 0.0, new_values)
    halo_cells = bring_values(values, border_lists)
    scores = turn_scores(values, halo_cells, reward, flat_turns, usable)
    row_max = jnp.max(scores, axis=1)
    raised = jnp.exp(scores - row_max[:, None])
    policy = raised / jnp.sum(raised, axis=1, keepdims=True)
    mass_now = jnp.where(is_target, 0.0, anchors)
    turn_counts = jnp.zeros(successors.shape, jnp.float32)
    for round_index in range(HORIZON):
        turn_flow = mass_now[:, None, :] * policy
        turn_counts = turn_counts + jnp.sum(turn_flow, axis=0)
        if round_index + 1 < HORIZON:
            arrived = (
                jnp.zeros((dest_count, slot_total), jnp.float32)
                .at[:, flat_turns]
                .add(turn_flow.reshape(dest_count, -1))
            )
            landed = return_flow(arrived, border_lists, own_count, border_width)
            mass_now = jnp.where(is_target, 0.0, landed)
    local_visits = turn_counts / (dest_count * lax.axis_size("dst") * HORIZON)
    visits = lax.psum(local_visits, "dst")
    demo_term = jnp.where(usable, demo_counts, 0).astype(jnp.float32) / 3.0
    count_gap = demo_term - visits
    total_segments = own_count * lax.axis_size("gx") * lax.axis_size("gy")
    own_gap = demo_term / lax.axis_size("dst") - local_visits
    block_term = jnp.sum(own_gap[None] * feats, axis=(1, 2)) / total_segments
    gradient = lax.psum(block_term, ("gx", "gy", "dst"))
    return (count_gap, gradient)


def local(features, cost_weights, successors, turn_valid, border_lists, destinations, anchors, demo_counts):
    args = (
        features, cost_weights, successors, turn_valid, border_lists, destinations, anchors, demo_counts
    )
    blocks = lax.axis_size("gx") * lax.axis_size("gy")
    fits = (
        anchors.shape[0] == blocks
        and blocks % 8 == 0
        and lax.axis_size("dst") == 2
        and lax.axis_size("gx") in (2, 4, 8)
        and lax.axis_size("gy") in (2, 4, 8)
        and successors.shape[1] == 8 * LANES
        and border_lists.shape[1] == LANES
        and successors.shape[0] == 8
    )
    return per_destination(*args) if fits else per_block(*args)


def solution(mesh):
    in_specs = (
        P(None, None, ("gx", "gy")),
        P(),
        P(None, ("gx", "gy")),
        P(None, ("gx", "gy")),
        P(None, ("gx", "gy")),
        P("dst"),
        P("dst", ("gx", "gy")),
        P(None, ("gx", "gy")),
    )
    out_specs = (P(None, ("gx", "gy")), P())
    return jax.shard_map(local, mesh=mesh, in_specs=in_specs, out_specs=out_specs, check_vma=False)
```
